32 devices in a mesh: img: 16 (over z, x, core), band: 2 (over y).
Axes of the slice: x: 2, y: 2, z: 4, core: 2. Of those that a mesh axis runs over, the one named last changes fastest.
Arguments:
- tokens: bfloat16 [128, 32, 32, 384], P('img', 'band'), may hold values from -6 to 6
- cotangent: bfloat16 [128, 32, 32, 384], P('img', 'band'), may hold values from -6 to 6
- valid_mask: int32 [128, 32, 32], P('img'), may hold values from 0 to 1, as said below
- timesteps: int32 [128], P('img'), may hold values from 0 to 999
- index_table: int32 [567], replicated, may hold values from 0 to 566, each once
- first_gain: float32 [2, 384], replicated, may hold values from 0.5 to 1.5
- first_shift: float32 [2, 384], replicated, may hold values from -1.25 to 1.25
- attend_weight: bfloat16 [2, 384, 1152], replicated, may hold values from -0.3125 to 0.3125
- time_weight: bfloat16 [2, 384, 768], replicated, may hold values from -0.078125 to 0.078125
- offset_bias: float32 [2, 6, 567], replicated, may hold values from -6 to 6
- output_weight: bfloat16 [2, 384, 384], replicated, may hold values from -1.75 to 1.75
- output_bias: float32 [2, 384], replicated, may hold values from -1.75 to 1.75
- second_gain: float32 [2, 384], replicated, may hold values from 0.5 to 1.5
- second_shift: float32 [2, 384], replicated, may hold values from -1.25 to 1.25
- expand_weight: bfloat16 [2, 384, 1536], replicated, may hold values from -0.3125 to 0.3125
- expand_bias: float32 [2, 1536], replicated, may hold values from -3 to 3
- reduce_weight: bfloat16 [2, 1536, 384], replicated, may hold values from -0.15625 to 0.15625
- reduce_bias: float32 [2, 384], replicated, may hold values from -1.75 to 1.75
Outputs:
- output: bfloat16 [128, 32, 32, 384], P('img', 'band')
- input_grad: bfloat16 [128, 32, 32, 384], P('img', 'band')
- grad_first_gain: float32 [2, 384], replicated
- grad_first_shift: float32 [2, 384], replicated
- grad_attend_weight: float32 [2, 384, 1152], replicated
- grad_time_weight: float32 [2, 384, 768], replicated
- grad_offset_bias: float32 [2, 6, 567], replicated
- grad_output_weight: float32 [2, 384, 384], replicated
- grad_output_bias: float32 [2, 384], replicated
- grad_second_gain: float32 [2, 384], replicated
- grad_second_shift: float32 [2, 384], replicated
- grad_expand_weight: float32 [2, 384, 1536], replicated
- grad_expand_bias: float32 [2, 1536], replicated
- grad_reduce_weight: float32 [2, 1536, 384], replicated
- grad_reduce_bias: float32 [2, 384], replicated
The draws below stay inside these ranges and needn't reach their ends.
Inputs may be any that keep to these rules, and one draw needn't show every extreme that they name: `valid_mask`: an image's valid patches are its first h rows and first w columns, h and w at least a quarter of 32 and 32; among the 8 images of each index of img, one has all 32 rows valid.
All inputs are finite; a program needn't handle non-finite values.
Results may differ from the reference program's by a relative error of at most 0.015.
Values may be sent and summed in bfloat16 or wider, within the bound.
A program may use at most 640 MiB of HBM per device.

```python
import math
import jax
import jax.numpy as jnp
from jax import lax

D = 384
HEADS = 6
HEAD_DIM = 64
FF = 1536
LAYERS = 2
GRID_H = 32
GRID_W = 32
WIN = 4
IMG_DEV = 8
IMAGES = 128
RELPOS = 567


def draw_valid_mask(key, part):
    key = jax.random.fold_in(key, 7)
    height_key, width_key, pick_key = jax.random.split(key, 3)
    heights = jax.random.randint(height_key, (IMAGES // IMG_DEV, IMG_DEV), GRID_H // 4, GRID_H + 1)
    widths = jax.random.randint(width_key, (IMAGES,), GRID_W // 4, GRID_W + 1)
    chosen = jax.random.randint(pick_key, (IMAGES // IMG_DEV, 1), 0, IMG_DEV)
    heights = jnp.where(jnp.arange(IMG_DEV, dtype=jnp.int32)[None, :] == chosen, GRID_H, heights).reshape(IMAGES)
    row_index = jnp.arange(GRID_H, dtype=jnp.int32)[None, :, None]
    col_index = jnp.arange(GRID_W, dtype=jnp.int32)[None, None, :]
    inside = (row_index < heights[:, None, None]) & (col_index < widths[:, None, None])
    return inside.astype(jnp.int32)


def with_ends(values, rng, least, top_value):
    spot = [jax.random.randint(jax.random.fold_in(rng, axis), (), 0, length) for axis, length in enumerate(values.shape)]
    longest = values.shape.index(max(values.shape))
    neighbour = spot[:longest] + [(spot[longest] + 1) % values.shape[longest]] + spot[longest + 1:]
    return values.at[tuple(spot)].set(least).at[tuple(neighbour)].set(top_value)


def levels(key, shape, shards, least, top_value):
    def one(position, shards_of):
        draws = jax.random.uniform(jax.random.fold_in(jax.random.fold_in(key, 6), position), (shards_of,), jnp.float32, least / len(shards), top_value / len(shards))
        return jnp.repeat(jnp.exp(draws), shape[position] // shards_of).reshape((-1,) + (1,) * (len(shape) - position - 1))

    level = one(*shards[0])
    for cut in shards[1:]:
        level = level * one(*cut)
    return level


def scatter_about(stream_key, extent, deviation, bound, pieces=(), kind=jnp.bfloat16):
    drawn = deviation * jax.random.normal(stream_key, extent, jnp.float32)
    if pieces:
        drawn = drawn * levels(stream_key, extent, pieces, -0.22, 0.18)
    return jnp.clip(drawn, -bound, bound).astype(kind)


def setup_inputs(seed: int = 0) -> dict:
    key_of = jax.random.split(jax.random.key(seed), 19)
    return {
        "tokens": scatter_about(key_of[0], (IMAGES, GRID_H, GRID_W, D), 1.0, 6.0, ((0, 16), (1, 2))),
        "cotangent": scatter_about(key_of[1], (IMAGES, GRID_H, GRID_W, D), 1.0, 6.0, ((0, 16), (1, 2))),
        "valid_mask": draw_valid_mask(jax.random.fold_in(key_of[18], 71), 0),
        "timesteps": with_ends(jax.random.randint(key_of[3], (IMAGES,), 0, 1000), jax.random.fold_in(key_of[3], 1), 0, 999).astype(jnp.int32),
        "index_table": jax.random.permutation(key_of[4], RELPOS).astype(jnp.int32),
        "first_gain": jnp.clip(1.0 + 0.1 * jax.random.normal(key_of[5], (LAYERS, D), jnp.float32), 0.5, 1.5),
        "first_shift": scatter_about(key_of[6], (LAYERS, D), 0.2, 1.25, (), jnp.float32),
        "attend_weight": scatter_about(key_of[7], (LAYERS, D, 3 * D), D ** -0.5, 0.3125),
        "time_weight": scatter_about(key_of[8], (LAYERS, D, 2 * D), (16 * D) ** -0.5, 0.078125),
        "offset_bias": scatter_about(key_of[9], (LAYERS, HEADS, RELPOS), 1.0, 6.0, (), jnp.float32),
        "output_weight": scatter_about(key_of[10], (LAYERS, D, D), (D // 32) ** -0.5, 1.75),
        "output_bias": scatter_about(key_of[11], (LAYERS, D), 0.3, 1.75, (), jnp.float32),
        "second_gain": jnp.clip(1.0 + 0.1 * jax.random.normal(key_of[12], (LAYERS, D), jnp.float32), 0.5, 1.5),
        "second_shift": scatter_about(key_of[13], (LAYERS, D), 0.2, 1.25, (), jnp.float32),
        "expand_weight": scatter_about(key_of[14], (LAYERS, D, FF), D ** -0.5, 0.3125),
        "expand_bias": scatter_about(key_of[15], (LAYERS, FF), 0.5, 3.0, (), jnp.float32),
        "reduce_weight": scatter_about(key_of[16], (LAYERS, FF, D), FF ** -0.5, 0.15625),
        "reduce_bias": scatter_about(key_of[17], (LAYERS, D), 0.3, 1.75, (), jnp.float32),
    }


EXACT = lax.Precision.HIGHEST
NEG_FILL = -1000000000.0
EPSILON = 1e-06

@jax.custom_vjp
def low(v):
    return lax.optimization_barrier(v.astype(jnp.bfloat16)).astype(jnp.float32)

@jax.custom_vjp
def low_back(v):
    return v

def low_keep(v):
    return (low(v), None)

def low_pass(kept, grad):
    return (grad,)

def back_keep(v):
    return (v, None)

def back_low(kept, grad):
    return (low(grad),)
low.defvjp(low_keep, low_pass)
low_back.defvjp(back_keep, back_low)

def time_embedding(timesteps, width):
    half_width = width // 2
    frequency = jnp.exp(jnp.arange(half_width, dtype=jnp.int32).astype(jnp.float32) * (-math.log(10000.0) / half_width))
    angles = timesteps.astype(jnp.float32)[:, None] * frequency[None, :]
    return jnp.concatenate([jnp.sin(angles), jnp.cos(angles)], axis=-1)

def layer_norm(values, gain, shift):
    mean_value = lax.optimization_barrier(jnp.mean(values, axis=-1, keepdims=True))
    centered = values - mean_value
    inverse = lax.rsqrt(lax.optimization_barrier(jnp.mean(centered * centered, axis=-1, keepdims=True)) + EPSILON)
    return centered * inverse * gain + shift

def offset_tables(query_rows, key_rows, key_shift, grid_cols):
    row_diff = jnp.arange(key_rows, dtype=jnp.int32)[None, :] - jnp.arange(query_rows, dtype=jnp.int32)[:, None] + key_shift
    row_pick = (row_diff[:, :, None] == jnp.arange(2 * WIN + 1, dtype=jnp.int32)[None, None, :]).astype(jnp.float32)
    col_diff = jnp.arange(grid_cols, dtype=jnp.int32)[None, :] - jnp.arange(grid_cols, dtype=jnp.int32)[:, None] + grid_cols - 1
    col_pick = (col_diff[:, :, None] == jnp.arange(2 * grid_cols - 1, dtype=jnp.int32)[None, None, :]).astype(jnp.float32)
    return (row_pick, col_pick)

def position_bias(table, index_table, row_pick, col_pick):
    entries = index_table.shape[0]
    select = (index_table[:, None] == jnp.arange(entries, dtype=jnp.int32)[None, :]).astype(jnp.float32)
    per_offset = jnp.dot(table, select.T, precision=EXACT)
    per_offset = per_offset.reshape(table.shape[0], row_pick.shape[2], col_pick.shape[2])
    column_mixed = jnp.einsum('hab,ctb->hact', per_offset, col_pick, precision=EXACT)
    expanded = jnp.einsum('hact,rsa->hrcst', column_mixed, row_pick, precision=EXACT)
    return expanded.reshape(table.shape[0], row_pick.shape[0] * col_pick.shape[0], row_pick.shape[1] * col_pick.shape[1])

def block(residual, time_row, layer_weights, allowed, row_pick, col_pick, index_table):
    first_gain, first_shift, attend_matrix, time_matrix, offset_table, output_matrix, output_shift, second_gain, second_shift, expand_matrix, expand_shift, reduce_matrix, reduce_shift = layer_weights
    token_count = residual.shape[0]
    normed = low(layer_norm(residual, first_gain, first_shift))
    projected = jnp.dot(normed, attend_matrix, precision=EXACT)
    time_proj = jnp.dot(time_row, time_matrix, precision=EXACT)
    queries = low_back(low(projected[:, :D] + time_proj[:D]))
    key_heads = low_back(low(projected[:, D:2 * D]))
    values = low_back(low(projected[:, 2 * D:] + time_proj[D:]))
    bias_full = position_bias(offset_table, index_table, row_pick, col_pick)
    scores = jnp.einsum('nhe,khe->hnk', queries.reshape(token_count, HEADS, HEAD_DIM), key_heads.reshape(token_count, HEADS, HEAD_DIM), precision=EXACT) * HEAD_DIM ** (-0.5) + bias_full
    scores = low_back(jnp.where(allowed[None], scores, NEG_FILL))
    row_max = lax.optimization_barrier(jnp.max(scores, axis=-1, keepdims=True))
    exp_terms = jnp.exp(scores - row_max)
    attention = low(exp_terms / lax.optimization_barrier(jnp.sum(exp_terms, axis=-1, keepdims=True)))
    attended = jnp.einsum('hnk,khe->nhe', attention, values.reshape(token_count, HEADS, HEAD_DIM), precision=EXACT)
    attended = low_back(low(attended.reshape(token_count, D)))
    branch = low_back(jnp.dot(attended, output_matrix, precision=EXACT) + output_shift)
    middle = residual + branch
    normed_two = low(layer_norm(middle, second_gain, second_shift))
    hidden = low_back(jnp.dot(normed_two, expand_matrix, precision=EXACT) + expand_shift)
    active = low(jax.nn.gelu(hidden, approximate=True))
    return middle + low_back(jnp.dot(active, reduce_matrix, precision=EXACT) + reduce_shift)

def reference(tokens, cotangent, valid_mask, timesteps, index_table, first_gain, first_shift, attend_weight, time_weight, offset_bias, output_weight, output_bias, second_gain, second_shift, expand_weight, expand_bias, reduce_weight, reduce_bias):
    members = (first_gain, first_shift, attend_weight, time_weight, offset_bias, output_weight, output_bias, second_gain, second_shift, expand_weight, expand_bias, reduce_weight, reduce_bias)
    params = tuple((member.astype(jnp.float32) for member in members))
    row_pick, col_pick = offset_tables(GRID_H, GRID_H, WIN, GRID_W)
    grid_row = jnp.arange(GRID_H, dtype=jnp.int32)
    row_window = jnp.abs(grid_row[None, :] - grid_row[:, None]) <= WIN
    token_window = jnp.repeat(jnp.repeat(row_window, GRID_W, axis=0), GRID_W, axis=1)
    token_count = GRID_H * GRID_W
    diagonal = jnp.eye(token_count, dtype=bool)
    time_all = low(time_embedding(timesteps, D))

    def per_image(running, inputs):
        image_tokens, image_cot, image_valid, time_row = inputs
        allowed = token_window & ((image_valid.reshape(token_count) == 1)[None, :] | diagonal)

        def forward_only(weights, residual):
            for layer_index in range(LAYERS):
                residual = block(residual, time_row, tuple((member[layer_index] for member in weights)), allowed, row_pick, col_pick, index_table)
            return residual
        result, pullback = jax.vjp(forward_only, params, image_tokens.reshape(token_count, D).astype(jnp.float32))
        weight_grads, grad_tokens = pullback(image_cot.reshape(token_count, D).astype(jnp.float32))
        running = jax.tree.map(jnp.add, running, weight_grads)
        return (running, (result.astype(jnp.bfloat16).reshape(GRID_H, GRID_W, D), grad_tokens.astype(jnp.bfloat16).reshape(GRID_H, GRID_W, D)))
    initial = tuple((jnp.zeros_like(member) for member in params))
    grad_sums, outputs = lax.scan(per_image, initial, (tokens, cotangent, valid_mask, time_all))
    return (outputs[0], outputs[1], grad_sums[0], grad_sums[1], grad_sums[2], grad_sums[3], grad_sums[4], grad_sums[5], grad_sums[6], grad_sums[7], grad_sums[8], grad_sums[9], grad_sums[10], grad_sums[11], grad_sums[12])
```

```python
import functools
import math

import jax
import jax.numpy as jnp
from jax import lax
from jax.experimental import pallas as pl
from jax.experimental.pallas import tpu as pltpu
from jax.sharding import PartitionSpec as P

WIN = 4
CHUNK = 256
QBLOCK = 128
KWIN = 384
HALO = 128

EXACT = lax.Precision.HIGHEST
NEG_FILL = -1000000000.0
EPSILON = 1e-06
GELU_A = math.sqrt(2.0 / math.pi)
GELU_B = 0.044715 * GELU_A
VMEM_BYTES = 58 * 1024 * 1024

F32 = jnp.float32
BF16 = jnp.bfloat16


def dot(a, b):
    return jnp.dot(a, b, preferred_element_type=F32)


def dot_nt(a, b):
    return lax.dot_general(a, b, (((1,), (1,)), ((), ())), preferred_element_type=F32)


def norm_stats(v):
    mean = jnp.mean(v, axis=-1, keepdims=True)
    centered = v - mean
    inverse = lax.rsqrt(jnp.mean(centered * centered, axis=-1, keepdims=True) + EPSILON)
    return centered * inverse, inverse


def norm_back(gy, xh, inverse, gain):
    gs = gy * gain
    return inverse * (
        gs - jnp.mean(gs, axis=-1, keepdims=True) - xh * jnp.mean(gs * xh, axis=-1, keepdims=True)
    )


def row_sums(v):
    rows, cols = v.shape
    return jnp.sum(v.reshape(rows // 8, 8, cols), axis=0)


def split_heads(block):
    lane = lax.broadcasted_iota(jnp.int32, block.shape, 1)
    zero = jnp.zeros_like(block)
    first = lane < block.shape[1] // 2
    return jnp.concatenate(
        [jnp.where(first, block, zero), jnp.where(first, zero, block)], axis=0
    )


def join_heads(product):
    half = product.shape[0] // 2
    width = product.shape[1] // 2
    return jnp.concatenate([product[:half, :width], product[half:, width:]], axis=0).T


def forward_kernel(
    pairs,
    x_new,
    x_old,
    tproj,
    mask,
    bias,
    gain1,
    shift1,
    wqkv,
    wo,
    bo,
    gain2,
    shift2,
    w1,
    b1,
    w2,
    b2,
    qkv_out,
    p_out,
    o_out,
    mid_out,
    act_out,
    slope_out,
    x_out,
    q_ring,
    k_ring,
    vt_ring,
    o_ring,
):
    step = pl.program_id(0)
    width = x_new.shape[1]

    @pl.when(step == 0)
    def _():
        q_ring[...] = jnp.zeros_like(q_ring)
        k_ring[...] = jnp.zeros_like(k_ring)
        vt_ring[...] = jnp.zeros_like(vt_ring)
        o_ring[...] = jnp.zeros_like(o_ring)

    attended = o_ring[...]
    mid = x_old[...].astype(F32) + (dot(attended, wo[...]) + bo[...])
    mid_out[...] = mid
    xh2, _ = norm_stats(mid)
    c = (xh2 * gain2[...] + shift2[...]).astype(BF16)
    u = dot(c, w1[...]) + b1[...]
    u2 = u * u
    t = jnp.tanh(u * (GELU_A + GELU_B * u2))
    h = 0.5 + 0.5 * t
    e = u * h
    act = e.astype(BF16)
    act_out[...] = act
    slope_out[...] = (h + (e * (1.0 - t)) * (GELU_A + (3.0 * GELU_B) * u2)).astype(BF16)
    x_out[...] = (mid + (dot(act, w2[...]) + b2[...])).astype(x_out.dtype)

    queries = q_ring[...]
    xh1, _ = norm_stats(x_new[...].astype(F32))
    a = (xh1 * gain1[...] + shift1[...]).astype(BF16)
    qkv = (dot(a, wqkv[...]) + tproj[0]).astype(BF16)
    qkv_out[...] = qkv
    q_ring[...] = qkv[:, :width] * jnp.asarray(0.125, BF16)
    k_ring[:HALO, :] = k_ring[CHUNK : CHUNK + HALO, :]
    k_ring[HALO : HALO + CHUNK, :] = k_ring[HALO + CHUNK :, :]
    k_ring[HALO + CHUNK :, :] = qkv[:, width : 2 * width]
    vt_ring[:, :HALO] = vt_ring[:, CHUNK : CHUNK + HALO]
    vt_ring[:, HALO : HALO + CHUNK] = vt_ring[:, HALO + CHUNK :]
    vt_ring[:, HALO + CHUNK :] = qkv[:, 2 * width :].T

    key_index = lax.broadcasted_iota(jnp.int32, (KWIN, QBLOCK), 0)
    query_index = lax.broadcasted_iota(jnp.int32, (KWIN, QBLOCK), 1)
    diagonal = key_index == query_index + HALO
    for blk in range(CHUNK // QBLOCK):
        low = blk * QBLOCK
        row = mask[0, :, low : low + KWIN]
        column = jnp.broadcast_to(row, (QBLOCK, KWIN)).T
        extra = jnp.where(diagonal, 0.0, column)
        extra = jnp.concatenate([extra, extra], axis=1)
        for pair in range(pairs):
            feat = slice(pair * 128, (pair + 1) * 128)
            split_q = split_heads(queries[low : low + QBLOCK, feat])
            s = dot_nt(k_ring[low : low + KWIN, feat], split_q) + bias[pair] + extra
            top = jnp.max(s, axis=0, keepdims=True)
            ex = jnp.exp(s - top)
            total = jnp.sum(ex, axis=0, keepdims=True)
            p = (ex * (1.0 / total)).astype(BF16)
            p_out[blk, pair] = p
            o = join_heads(dot(vt_ring[feat, low : low + KWIN], p)).astype(BF16)
            o_ring[low : low + QBLOCK, feat] = o
            o_out[low : low + QBLOCK, feat] = o


def const_spec(shape):
    zeros = (0,) * len(shape)
    return pl.BlockSpec(shape, lambda g: zeros, pipeline_mode=pl.Buffered(1))


def forward_layer(x, x_lead, chunks, chunks_per_image, tproj, mask, bias, weights, out_dtype):
    width = x.shape[1]
    hidden = weights[7].shape[1]
    pairs = width // 128
    steps = chunks + 2

    def at(lead, least=0):
        def index(g):
            return jnp.clip(g - lead, least, chunks - 1)

        return index

    new_at, attn_at, old_at = at(0), at(1), at(2)
    row = pl.BlockSpec((CHUNK, width), lambda g: (g, 0))
    wide = pl.BlockSpec((CHUNK, hidden), lambda g: (g, 0))
    rows = steps * CHUNK
    gain1, shift1, wqkv, wo, bo, gain2, shift2, w1, b1, w2, b2 = weights
    consts = [gain1, shift1, wqkv, wo, bo, gain2, shift2, w1, b1, w2, b2]
    return pl.pallas_call(
        functools.partial(forward_kernel, pairs),
        grid=(steps,),
        in_specs=[
            pl.BlockSpec((CHUNK, width), lambda g: (new_at(g) + x_lead, 0)),
            pl.BlockSpec((CHUNK, width), lambda g: (old_at(g) + x_lead, 0)),
            pl.BlockSpec((1, 1, 3 * width), lambda g: (new_at(g) // chunks_per_image, 0, 0)),
            pl.BlockSpec((1, 1, CHUNK + 2 * HALO), lambda g: (attn_at(g), 0, 0)),
            const_spec(bias.shape),
        ]
        + [const_spec(w.shape) for w in consts],
        out_specs=[
            pl.BlockSpec((CHUNK, 3 * width), lambda g: (new_at(g), 0)),
            pl.BlockSpec((CHUNK // QBLOCK, pairs, KWIN, 2 * QBLOCK), lambda g: (g, 0, 0, 0)),
            row,
            row,
            wide,
            wide,
            row,
        ],
        out_shape=[
            jax.ShapeDtypeStruct((chunks * CHUNK, 3 * width), BF16),
            jax.ShapeDtypeStruct((steps * (CHUNK // QBLOCK), pairs, KWIN, 2 * QBLOCK), BF16),
            jax.ShapeDtypeStruct((rows, width), BF16),
            jax.ShapeDtypeStruct((rows, width), F32),
            jax.ShapeDtypeStruct((rows, hidden), BF16),
            jax.ShapeDtypeStruct((rows, hidden), BF16),
            jax.ShapeDtypeStruct((rows, width), out_dtype),
        ],
        scratch_shapes=[
            pltpu.VMEM((CHUNK, width), BF16),
            pltpu.VMEM((HALO + 2 * CHUNK, width), BF16),
            pltpu.VMEM((width, HALO + 2 * CHUNK), BF16),
            pltpu.VMEM((CHUNK, width), BF16),
        ],
        compiler_params=pltpu.CompilerParams(vmem_limit_bytes=VMEM_BYTES),
        name="block_forward",
    )(x, x, tproj, mask, bias, *consts)


def feed_back_kernel(
    gx,
    mid,
    act,
    slope,
    o,
    gain2,
    shift2,
    w1t,
    w2t,
    wot,
    gmid_out,
    go_out,
    gw2t,
    gw1,
    gwo,
    sums,
    gb1,
):
    step = pl.program_id(0)

    @pl.when(step == 0)
    def _():
        for ref in (gw2t, gw1, gwo, sums, gb1):
            ref[...] = jnp.zeros_like(ref)

    grad = gx[...].astype(F32)
    gr = grad.astype(BF16)
    gw2t[...] += dot(gr.T, act[...])
    ge = dot(gr, w2t[...])
    gu = (ge * slope[...].astype(F32)).astype(BF16)
    gb1[...] += row_sums(gu.astype(F32))
    xh, inverse = norm_stats(mid[...])
    c = (xh * gain2[...] + shift2[...]).astype(BF16)
    gw1[...] += dot(c.T, gu)
    gc = dot(gu, w1t[...])
    gmid = grad + norm_back(gc, xh, inverse, gain2[...])
    gmid_out[...] = gmid
    gb = gmid.astype(BF16)
    gwo[...] += dot(o[...].T, gb)
    go_out[...] = dot(gb, wot[...]).astype(BF16)
    sums[0] += row_sums(gr.astype(F32))
    sums[1] += row_sums(gb.astype(F32))
    sums[2] += row_sums(gc * xh)
    sums[3] += row_sums(gc)


def feed_back(gx, gx_lead, chunks, mid, act, slope, o, gain2, shift2, w1t, w2t, wot):
    width = mid.shape[1]
    hidden = act.shape[1]

    def rows(cols, lead):
        return pl.BlockSpec((CHUNK, cols), lambda g: (g + lead, 0))

    def kept(shape):
        zeros = (0,) * len(shape)
        return pl.BlockSpec(shape, lambda g: zeros)

    grads = [(width, hidden), (width, hidden), (width, width), (4, 8, width), (8, hidden)]
    return pl.pallas_call(
        feed_back_kernel,
        grid=(chunks,),
        in_specs=[
            rows(width, gx_lead),
            rows(width, 2),
            rows(hidden, 2),
            rows(hidden, 2),
            rows(width, 1),
        ]
        + [const_spec(w.shape) for w in (gain2, shift2, w1t, w2t, wot)],
        out_specs=[rows(width, 0), rows(width, 0)] + [kept(shape) for shape in grads],
        out_shape=[
            jax.ShapeDtypeStruct((chunks * CHUNK, width), F32),
            jax.ShapeDtypeStruct((chunks * CHUNK, width), BF16),
        ]
        + [jax.ShapeDtypeStruct(shape, F32) for shape in grads],
        compiler_params=pltpu.CompilerParams(vmem_limit_bytes=VMEM_BYTES),
        name="feed_back",
    )(gx, mid, act, slope, o, gain2, shift2, w1t, w2t, wot)


def attend_back_kernel(
    pairs,
    chunks,
    chunks_per_image,
    prev,
    cur,
    nxt,
    p_in,
    go_in,
    o_in,
    gmid,
    x,
    gain1,
    shift1,
    wqkvt,
    gx_out,
    gwqkv,
    gbias,
    gtime,
    sums,
    gq_ring,
    gkv_ring,
):
    step = pl.program_id(0)
    width = x.shape[1]

    @pl.when(step == 0)
    def _():
        for ref in (gwqkv, gbias, gtime, sums, gq_ring, gkv_ring):
            ref[...] = jnp.zeros_like(ref)

    gq_old = gq_ring[...]
    live = (step < chunks).astype(BF16)
    go = go_in[...] * live
    qkv = cur[...]
    queries = qkv[:, :width] * jnp.asarray(0.125, BF16)
    keys = jnp.concatenate(
        [prev[:, width : 2 * width], qkv[:, width : 2 * width], nxt[:, width : 2 * width]], axis=0
    )
    keys_t = keys.T
    values = jnp.concatenate([prev[:, 2 * width :], qkv[:, 2 * width :], nxt[:, 2 * width :]], axis=0)
    dots = (go.astype(F32) * o_in[...].astype(F32)).T
    for blk in range(CHUNK // QBLOCK):
        low = blk * QBLOCK
        for pair in range(pairs):
            feat = slice(pair * 128, (pair + 1) * 128)
            own = dots[feat, low : low + QBLOCK]
            row_dot = jnp.concatenate(
                [
                    jnp.sum(own[:64], axis=0, keepdims=True),
                    jnp.sum(own[64:], axis=0, keepdims=True),
                ],
                axis=1,
            )
            p = p_in[blk, pair]
            split_go = split_heads(go[low : low + QBLOCK, feat])
            split_q = split_heads(queries[low : low + QBLOCK, feat])
            gp = dot_nt(values[low : low + KWIN, feat], split_go)
            gs = p.astype(F32) * (gp - row_dot)
            gbias[pair] += gs
            gs = gs.astype(BF16)
            at = HALO + low
            gkv_ring[at : at + KWIN, feat] += dot(gs, split_q)
            vfeat = slice(width + pair * 128, width + (pair + 1) * 128)
            gkv_ring[at : at + KWIN, vfeat] += dot(p, split_go)
            gq = join_heads(dot(keys_t[feat, low : low + KWIN], gs)) * 0.125
            gq_ring[low : low + QBLOCK, feat] = gq.astype(BF16)

    done = jnp.concatenate([gq_old, gkv_ring[:CHUNK, :].astype(BF16)], axis=1)
    gkv_ring[:CHUNK, :] = gkv_ring[CHUNK : 2 * CHUNK, :]
    gkv_ring[CHUNK : CHUNK + HALO, :] = gkv_ring[2 * CHUNK :, :]
    gkv_ring[CHUNK + HALO :, :] = jnp.zeros((CHUNK, 2 * width), F32)
    xh, inverse = norm_stats(x[...].astype(F32))
    a = (xh * gain1[...] + shift1[...]).astype(BF16)
    gwqkv[...] += dot(a.T, done)
    ga = dot(done, wqkvt[...])
    gx_out[...] = (gmid[...] + norm_back(ga, xh, inverse, gain1[...])).astype(gx_out.dtype)
    sums[0] += row_sums(ga * xh)
    sums[1] += row_sums(ga)
    first = lax.rem(step + chunks_per_image - 1, chunks_per_image) == 0
    before = jnp.where(first, jnp.zeros(gtime.shape[1:], F32), gtime[0])
    summed = row_sums(done.astype(F32))
    gtime[0] = before + jnp.concatenate([summed[:, :width], summed[:, 2 * width :]], axis=1)


def attend_back(
    qkv, p, go, o, gmid, x, x_lead, chunks, chunks_per_image, gain1, shift1, wqkvt, out_dtype
):
    width = x.shape[1]
    pairs = width // 128
    steps = chunks + 1
    halves = CHUNK // HALO

    def now(g):
        return jnp.minimum(g, chunks - 1)

    def late(g):
        return jnp.maximum(g - 1, 0)

    def rows(cols, lead, index):
        return pl.BlockSpec((CHUNK, cols), lambda g: (index(g) + lead, 0))

    def kept(shape):
        zeros = (0,) * len(shape)
        return pl.BlockSpec(shape, lambda g: zeros)

    images = chunks // chunks_per_image
    return pl.pallas_call(
        functools.partial(attend_back_kernel, pairs, chunks, chunks_per_image),
        grid=(steps,),
        in_specs=[
            pl.BlockSpec((HALO, 3 * width), lambda g: (jnp.maximum(halves * now(g) - 1, 0), 0)),
            rows(3 * width, 0, now),
            pl.BlockSpec(
                (HALO, 3 * width),
                lambda g: (jnp.minimum(halves * (now(g) + 1), halves * chunks - 1), 0),
            ),
            pl.BlockSpec(
                (CHUNK // QBLOCK, pairs, KWIN, 2 * QBLOCK), lambda g: (now(g) + 1, 0, 0, 0)
            ),
            rows(width, 0, now),
            rows(width, 1, now),
            rows(width, 0, late),
            rows(width, x_lead, late),
        ]
        + [const_spec(w.shape) for w in (gain1, shift1, wqkvt)],
        out_specs=[
            rows(width, 0, lambda g: g),
            kept((width, 3 * width)),
            kept((pairs, KWIN, 2 * QBLOCK)),
            pl.BlockSpec((1, 8, 2 * width), lambda g: (late(g) // chunks_per_image, 0, 0)),
            kept((2, 8, width)),
        ],
        out_shape=[
            jax.ShapeDtypeStruct((steps * CHUNK, width), out_dtype),
            jax.ShapeDtypeStruct((width, 3 * width), F32),
            jax.ShapeDtypeStruct((pairs, KWIN, 2 * QBLOCK), F32),
            jax.ShapeDtypeStruct((images, 8, 2 * width), F32),
            jax.ShapeDtypeStruct((2, 8, width), F32),
        ],
        scratch_shapes=[
            pltpu.VMEM((CHUNK, width), BF16),
            pltpu.VMEM((2 * CHUNK + HALO, 2 * width), F32),
        ],
        compiler_params=pltpu.CompilerParams(vmem_limit_bytes=VMEM_BYTES),
        name="attend_back",
    )(qkv, qkv, qkv, p, go, o, gmid, x, gain1, shift1, wqkvt)


def time_embedding(timesteps, width):
    half_width = width // 2
    frequency = jnp.exp(
        jnp.arange(half_width, dtype=jnp.int32).astype(F32) * (-math.log(10000.0) / half_width)
    )
    angles = timesteps.astype(F32)[:, None] * frequency[None, :]
    return jnp.concatenate([jnp.sin(angles), jnp.cos(angles)], axis=-1)


def column_table(grid_cols):
    col = jnp.arange(grid_cols, dtype=jnp.int32)
    col_diff = col[None, :] - col[:, None] + grid_cols - 1
    return (
        col_diff[:, :, None] == jnp.arange(2 * grid_cols - 1, dtype=jnp.int32)[None, None, :]
    ).astype(F32)


def bias_tiles(offset_bias, index_table, grid_cols):
    layers, heads, entries = offset_bias.shape
    span = 2 * WIN + 1
    query_rows = QBLOCK // grid_cols
    key_rows = KWIN // grid_cols
    select = (index_table[:, None] == jnp.arange(entries, dtype=jnp.int32)[None, :]).astype(F32)
    table = offset_bias.reshape(layers * heads, entries)
    per_offset = jnp.dot(table, select.T, precision=EXACT)
    per_offset = per_offset.reshape(layers * heads, span, 2 * grid_cols - 1)
    mixed = jnp.einsum("hab,ctb->hatc", per_offset, column_table(grid_cols), precision=EXACT)
    placed = [
        jnp.pad(
            mixed,
            ((0, 0), (row, key_rows - row - span), (0, 0), (0, 0)),
            constant_values=NEG_FILL,
        )
        for row in range(query_rows)
    ]
    tile = jnp.stack(placed, axis=3).reshape(layers, heads // 2, 2, KWIN, QBLOCK)
    return tile.transpose(0, 1, 3, 2, 4).reshape(layers, heads // 2, KWIN, 2 * QBLOCK)


def bias_pull(grad, index_table, grid_cols):
    pairs = grad.shape[0]
    entries = index_table.shape[0]
    span = 2 * WIN + 1
    query_rows = QBLOCK // grid_cols
    key_rows = KWIN // grid_cols
    parts = grad.reshape(pairs, key_rows, grid_cols, 2, query_rows, grid_cols)
    mixed = sum(parts[:, row : row + span, :, :, row, :] for row in range(query_rows))
    per_offset = jnp.einsum("pathc,ctb->phab", mixed, column_table(grid_cols), precision=EXACT)
    per_offset = per_offset.reshape(2 * pairs, entries)
    select = (index_table[:, None] == jnp.arange(entries, dtype=jnp.int32)[None, :]).astype(F32)
    return jnp.dot(per_offset, select, precision=EXACT)


def body(
    tokens,
    cotangent,
    valid_mask,
    timesteps,
    index_table,
    first_gain,
    first_shift,
    attend_weight,
    time_weight,
    offset_bias,
    output_weight,
    output_bias,
    second_gain,
    second_shift,
    expand_weight,
    expand_bias,
    reduce_weight,
    reduce_bias,
):
    images, band_rows, grid_cols, width = tokens.shape
    layers = attend_weight.shape[0]
    bands = lax.axis_size("band")
    me = lax.axis_index("band")
    own = images // bands
    part = band_rows * grid_cols
    patches = bands * part
    per_image = patches // CHUNK
    chunks = own * per_image

    def to_images(shard):
        shard = shard.reshape(bands, own, part, width)
        whole = jnp.zeros((own, bands, part, width), shard.dtype)
        for by in range(bands):
            piece = lax.dynamic_index_in_dim(shard, (me + by) % bands, 0, keepdims=False)
            if by:
                pairs = [(i, (i + by) % bands) for i in range(bands)]
                piece = lax.ppermute(piece, "band", pairs)
            whole = lax.dynamic_update_index_in_dim(whole, piece, (me - by) % bands, 1)
        return whole.reshape(own * patches, width)

    def to_bands(whole):
        whole = whole.reshape(own, bands, part, width)
        shard = jnp.zeros((bands, own, part, width), whole.dtype)
        for by in range(bands):
            piece = lax.dynamic_index_in_dim(whole, (me + by) % bands, 1, keepdims=False)
            if by:
                pairs = [(i, (i + by) % bands) for i in range(bands)]
                piece = lax.ppermute(piece, "band", pairs)
            shard = lax.dynamic_update_index_in_dim(shard, piece, (me - by) % bands, 0)
        return shard.reshape(images, band_rows, grid_cols, width)

    x0 = to_images(tokens)
    cot = to_images(cotangent)

    mine = lax.dynamic_slice_in_dim(valid_mask, me * own, own, 0).reshape(own, patches)
    fill = jnp.where(mine == 1, 0.0, NEG_FILL).astype(F32)
    fill = jnp.pad(fill, ((0, 0), (HALO, HALO)), constant_values=NEG_FILL)
    mask = jnp.stack(
        [fill[:, c * CHUNK : (c + 1) * CHUNK + 2 * HALO] for c in range(per_image)], axis=1
    ).reshape(chunks, 1, CHUNK + 2 * HALO)

    time_low = time_embedding(
        lax.dynamic_slice_in_dim(timesteps, me * own, own, 0), width
    ).astype(BF16)
    biases = bias_tiles(offset_bias, index_table, grid_cols)

    def row(v):
        return v.reshape(1, -1)

    x, x_lead = x0, 0
    kept = []
    for layer in range(layers):
        tp = jnp.dot(time_low, time_weight[layer], preferred_element_type=F32)
        tproj = jnp.concatenate([tp[:, :width], jnp.zeros_like(tp[:, :width]), tp[:, width:]], axis=1)
        weights = (
            row(first_gain[layer]),
            row(first_shift[layer]),
            attend_weight[layer],
            output_weight[layer],
            row(output_bias[layer]),
            row(second_gain[layer]),
            row(second_shift[layer]),
            expand_weight[layer],
            row(expand_bias[layer]),
            reduce_weight[layer],
            row(reduce_bias[layer]),
        )
        qkv, p, o, mid, act, slope, nxt = forward_layer(
            x,
            x_lead,
            chunks,
            per_image,
            tproj[:, None, :],
            mask,
            biases[layer],
            weights,
            F32 if layer < layers - 1 else BF16,
        )
        kept.append((x, x_lead, qkv, p, o, mid, act, slope))
        x, x_lead = nxt, 2
    output = to_bands(x[x_lead * CHUNK :])

    gx, gx_lead = cot, 0
    grads = [None] * layers
    for layer in reversed(range(layers)):
        x, x_lead, qkv, p, o, mid, act, slope = kept[layer]
        gmid, go, gw2t, gw1, gwo, sums2, gb1 = feed_back(
            gx,
            gx_lead,
            chunks,
            mid,
            act,
            slope,
            o,
            row(second_gain[layer]),
            row(second_shift[layer]),
            expand_weight[layer].T,
            reduce_weight[layer].T,
            output_weight[layer].T,
        )
        gx, gwqkv, gbias, gtime, sums1 = attend_back(
            qkv,
            p,
            go,
            o,
            gmid,
            x,
            x_lead,
            chunks,
            per_image,
            row(first_gain[layer]),
            row(first_shift[layer]),
            attend_weight[layer].T,
            F32 if layer else BF16,
        )
        gx_lead = 1
        sums1 = jnp.sum(sums1, axis=1)
        sums2 = jnp.sum(sums2, axis=1)
        gtime = jnp.sum(gtime, axis=1)
        gtw = jnp.sum(time_low.astype(F32)[:, :, None] * gtime[:, None, :], axis=0)
        grads[layer] = (
            sums1[0],
            sums1[1],
            gwqkv,
            gtw,
            bias_pull(gbias, index_table, grid_cols),
            gwo,
            sums2[1],
            sums2[2],
            sums2[3],
            gw1,
            jnp.sum(gb1, axis=0),
            gw2t.T,
            sums2[0],
        )
    input_grad = to_bands(gx[gx_lead * CHUNK :])
    stacked = tuple(jnp.stack([g[member] for g in grads]) for member in range(13))
    return (output, input_grad) + tuple(lax.psum(stacked, ("img", "band")))


def solution(mesh):
    split = P("img", "band", None, None)
    placed = (split, split, P("img", None, None), P("img")) + (P(),) * 14
    return jax.shard_map(
        body,
        mesh=mesh,
        in_specs=placed,
        out_specs=(split, split) + (P(),) * 13,
        check_vma=False,
    )
```

```python
import functools
import math

import jax
import jax.numpy as jnp
from jax import lax
from jax.experimental import pallas as pl
from jax.experimental.pallas import tpu as pltpu
from jax.sharding import PartitionSpec as P

WIN = 4
CHUNK = 256
QBLOCK = 128
KWIN = 384
HALO = 128
FEED = 512

EXACT = lax.Precision.HIGHEST
NEG_FILL = -1000000000.0
EPSILON = 1e-06
GELU_A = math.sqrt(2.0 / math.pi)
GELU_B = 0.044715 * GELU_A
VMEM_BYTES = 58 * 1024 * 1024

F32 = jnp.float32
BF16 = jnp.bfloat16


def dot(a, b):
    return jnp.dot(a, b, preferred_element_type=F32)


def dot_nt(a, b):
    return lax.dot_general(a, b, (((1,), (1,)), ((), ())), preferred_element_type=F32)


def norm_stats(v):
    mean = jnp.mean(v, axis=-1, keepdims=True)
    centered = v - mean
    inverse = lax.rsqrt(jnp.mean(centered * centered, axis=-1, keepdims=True) + EPSILON)
    return centered * inverse, inverse


def norm_back(gy, xh, inverse, gain):
    gs = gy * gain
    return inverse * (
        gs - jnp.mean(gs, axis=-1, keepdims=True) - xh * jnp.mean(gs * xh, axis=-1, keepdims=True)
    )


def row_sums(v):
    rows, cols = v.shape
    return jnp.sum(v.reshape(rows // 8, 8, cols), axis=0)


def split_heads(block):
    lane = lax.broadcasted_iota(jnp.int32, block.shape, 1)
    zero = jnp.zeros_like(block)
    first = lane < block.shape[1] // 2
    return jnp.concatenate(
        [jnp.where(first, block, zero), jnp.where(first, zero, block)], axis=0
    )


def join_heads(product):
    half = product.shape[0] // 2
    width = product.shape[1] // 2
    return jnp.concatenate([product[:half, :width], product[half:, width:]], axis=0).T


def fold(v, op):
    return op(v.reshape(v.shape[0] // 8, 8, v.shape[1]), axis=0)


def unroll_bias(rows, bias):
    pairs, keys, lanes = bias.shape
    grid_cols = QBLOCK // 4
    key_rows = keys // grid_cols
    lane = lax.broadcasted_iota(jnp.int32, (grid_cols, QBLOCK), 1)
    even = lax.rem(lane // grid_cols, 2) == 0
    for pair in range(pairs):
        for head in range(2):
            for key_row in range(key_rows):
                turned = [
                    pltpu.roll(
                        jnp.broadcast_to(
                            rows[pl.ds(((pair * 2 + head) * 2 + odd) * key_rows + key_row, 1), :],
                            (grid_cols, QBLOCK),
                        ),
                        0,
                        1,
                        stride=1,
                        stride_axis=0,
                    )
                    for odd in range(2)
                ]
                bias[
                    pair,
                    key_row * grid_cols : (key_row + 1) * grid_cols,
                    head * QBLOCK : (head + 1) * QBLOCK,
                ] = jnp.where(even, turned[0], turned[1])


def gather_bias(grads):
    pairs, keys, lanes = grads.shape
    grid_cols = QBLOCK // 4
    lane = lax.broadcasted_iota(jnp.int32, (keys, QBLOCK), 1)
    column = lax.rem(lax.broadcasted_iota(jnp.int32, (keys, QBLOCK), 0), grid_cols)
    parity = lax.rem(lane // grid_cols, 2)
    sums = []
    for pair in range(pairs):
        for head in range(2):
            for odd in range(2):
                v = grads[pair, :, head * QBLOCK : (head + 1) * QBLOCK]
                v = jnp.where(parity == odd, v, 0.0)
                for bit in (1, 2, 4, 8, 16):
                    turned = pltpu.roll(v, QBLOCK - bit, 1)
                    v = jnp.where(lax.rem(column // bit, 2) == 1, turned, v)
                sums.append(jnp.sum(v.reshape(keys // grid_cols, grid_cols, QBLOCK), axis=1))
    return jnp.concatenate(sums, axis=0)


def forward_kernel(
    pairs,
    x_new,
    x_old,
    tproj,
    mask,
    bias_rows,
    gain1,
    shift1,
    wqkv,
    wo,
    bo,
    gain2,
    shift2,
    w1,
    b1,
    w2,
    b2,
    qkv_out,
    p_out,
    o_out,
    mid_out,
    act_out,
    slope_out,
    x_out,
    bias,
    q_ring,
    k_ring,
    vt_ring,
    o_ring,
    s_scr,
):
    step = pl.program_id(0)
    width = x_new.shape[1]

    @pl.when(step == 0)
    def _():
        unroll_bias(bias_rows, bias)
        q_ring[...] = jnp.zeros_like(q_ring)
        k_ring[...] = jnp.zeros_like(k_ring)
        vt_ring[...] = jnp.zeros_like(vt_ring)
        o_ring[...] = jnp.zeros_like(o_ring)

    attended = o_ring[...]
    mid = x_old[...].astype(F32) + (dot(attended, wo[...]) + bo[...])
    mid_out[...] = mid
    xh2, _ = norm_stats(mid)
    c = (xh2 * gain2[...] + shift2[...]).astype(BF16)
    parts = 2 * pairs
    tile = w1.shape[1] // parts

    def feed(part):
        cols = slice(part * tile, (part + 1) * tile)
        whole = dot(c, w1[:, cols])
        for low in range(0, CHUNK, 64):
            u = whole[low : low + 64] + b1[:, cols]
            u2 = u * u
            t = jnp.tanh(u * (GELU_A + GELU_B * u2))
            h = 0.5 + 0.5 * t
            e = u * h
            act_out[low : low + 64, cols] = e.astype(BF16)
            slope_out[low : low + 64, cols] = (
                h + (e * (1.0 - t)) * (GELU_A + (3.0 * GELU_B) * u2)
            ).astype(BF16)

    queries = q_ring[...]
    xh1, _ = norm_stats(x_new[...].astype(F32))
    a = (xh1 * gain1[...] + shift1[...]).astype(BF16)
    qkv = (dot(a, wqkv[...]) + tproj[0]).astype(BF16)
    qkv_out[...] = qkv
    q_ring[...] = qkv[:, :width] * jnp.asarray(0.125, BF16)
    k_ring[:HALO, :] = k_ring[CHUNK : CHUNK + HALO, :]
    k_ring[HALO : HALO + CHUNK, :] = k_ring[HALO + CHUNK :, :]
    k_ring[HALO + CHUNK :, :] = qkv[:, width : 2 * width]
    vt_ring[:, :HALO] = vt_ring[:, CHUNK : CHUNK + HALO]
    vt_ring[:, HALO : HALO + CHUNK] = vt_ring[:, HALO + CHUNK :]
    vt_ring[:, HALO + CHUNK :] = qkv[:, 2 * width :].T

    key_index = lax.broadcasted_iota(jnp.int32, (KWIN, QBLOCK), 0)
    query_index = lax.broadcasted_iota(jnp.int32, (KWIN, QBLOCK), 1)
    diagonal = key_index == query_index + HALO
    extras = []
    for blk in range(CHUNK // QBLOCK):
        line = mask[0, :, blk * QBLOCK : blk * QBLOCK + KWIN]
        column = jnp.broadcast_to(line, (QBLOCK, KWIN)).T
        extras.append(jnp.where(diagonal, 0.0, column))
    todo = [(blk, pair) for blk in range(CHUNK // QBLOCK) for pair in range(pairs)]
    cells = [(k * 128, h * 128) for k in range(KWIN // 128) for h in range(2)]
    tops = {}

    def score(blk, pair):
        low = blk * QBLOCK
        feat = slice(pair * 128, (pair + 1) * 128)
        split_q = split_heads(queries[low : low + QBLOCK, feat])
        best = [None, None]
        for k in range(0, KWIN, 128):
            s = dot_nt(k_ring[low + k : low + k + 128, feat], split_q)
            for h in range(2):
                lane = slice(h * 128, h * 128 + 128)
                v = s[:, lane] + bias[pair, k : k + 128, lane] + extras[blk][k : k + 128]
                s_scr[blk, pair, k : k + 128, lane] = v
                top = fold(v, jnp.max)
                best[h] = top if best[h] is None else jnp.maximum(best[h], top)
        tops[blk, pair] = [jnp.max(v, axis=0, keepdims=True) for v in best]

    def soften(blk, pair):
        sums = [None, None]
        for k, lane in cells:
            at = (blk, pair, slice(k, k + 128), slice(lane, lane + 128))
            h = lane // 128
            ex = jnp.exp(s_scr[at] - tops[blk, pair][h])
            total = fold(ex, jnp.sum)
            sums[h] = total if sums[h] is None else sums[h] + total
            s_scr[at] = ex
        inverse = [1.0 / jnp.sum(v, axis=0, keepdims=True) for v in sums]
        for k, lane in cells:
            at = (blk, pair, slice(k, k + 128), slice(lane, lane + 128))
            p_out[at] = (s_scr[at] * inverse[lane // 128]).astype(BF16)

    def attend(blk, pair):
        low = blk * QBLOCK
        feat = slice(pair * 128, (pair + 1) * 128)
        o = join_heads(dot(vt_ring[feat, low : low + KWIN], p_out[blk, pair])).astype(BF16)
        o_ring[low : low + QBLOCK, feat] = o
        o_out[low : low + QBLOCK, feat] = o

    for i in range(len(todo) + 2):
        if i < len(todo):
            score(*todo[i])
            feed(i)
        if 1 <= i <= len(todo):
            soften(*todo[i - 1])
        if i >= 2:
            attend(*todo[i - 2])
    x_out[...] = (mid_out[...] + (dot(act_out[...], w2[...]) + b2[...])).astype(x_out.dtype)


def const_spec(shape):
    zeros = (0,) * len(shape)
    return pl.BlockSpec(shape, lambda g: zeros, pipeline_mode=pl.Buffered(1))


def forward_layer(x, x_lead, chunks, chunks_per_image, tproj, mask, bias_rows, weights, out_dtype):
    width = x.shape[1]
    hidden = weights[7].shape[1]
    pairs = width // 128
    steps = chunks + 2

    def at(lead, least=0):
        def index(g):
            return jnp.clip(g - lead, least, chunks - 1)

        return index

    new_at, attn_at, old_at = at(0), at(1), at(2)
    row = pl.BlockSpec((CHUNK, width), lambda g: (g, 0))
    wide = pl.BlockSpec((CHUNK, hidden), lambda g: (g, 0))
    rows = steps * CHUNK
    gain1, shift1, wqkv, wo, bo, gain2, shift2, w1, b1, w2, b2 = weights
    consts = [gain1, shift1, wqkv, wo, bo, gain2, shift2, w1, b1, w2, b2]
    return pl.pallas_call(
        functools.partial(forward_kernel, pairs),
        grid=(steps,),
        in_specs=[
            pl.BlockSpec((CHUNK, width), lambda g: (new_at(g) + x_lead, 0)),
            pl.BlockSpec((CHUNK, width), lambda g: (old_at(g) + x_lead, 0)),
            pl.BlockSpec((1, 1, 3 * width), lambda g: (new_at(g) // chunks_per_image, 0, 0)),
            pl.BlockSpec((1, 1, CHUNK + 2 * HALO), lambda g: (attn_at(g), 0, 0)),
            const_spec(bias_rows.shape),
        ]
        + [const_spec(w.shape) for w in consts],
        out_specs=[
            pl.BlockSpec((CHUNK, 3 * width), lambda g: (new_at(g), 0)),
            pl.BlockSpec((CHUNK // QBLOCK, pairs, KWIN, 2 * QBLOCK), lambda g: (g, 0, 0, 0)),
            pl.BlockSpec((CHUNK, width), lambda g: (g + 1, 0)),
            row,
            wide,
            wide,
            row,
        ],
        out_shape=[
            jax.ShapeDtypeStruct((chunks * CHUNK, 3 * width), BF16),
            jax.ShapeDtypeStruct((steps * (CHUNK // QBLOCK), pairs, KWIN, 2 * QBLOCK), BF16),
            jax.ShapeDtypeStruct((rows + CHUNK, width), BF16),
            jax.ShapeDtypeStruct((rows, width), F32),
            jax.ShapeDtypeStruct((rows, hidden), BF16),
            jax.ShapeDtypeStruct((rows, hidden), BF16),
            jax.ShapeDtypeStruct((rows, width), out_dtype),
        ],
        scratch_shapes=[
            pltpu.VMEM((pairs, KWIN, 2 * QBLOCK), F32),
            pltpu.VMEM((CHUNK, width), BF16),
            pltpu.VMEM((HALO + 2 * CHUNK, width), BF16),
            pltpu.VMEM((width, HALO + 2 * CHUNK), BF16),
            pltpu.VMEM((CHUNK, width), BF16),
            pltpu.VMEM((CHUNK // QBLOCK, pairs, KWIN, 2 * QBLOCK), F32),
        ],
        compiler_params=pltpu.CompilerParams(vmem_limit_bytes=VMEM_BYTES),
        name="block_forward",
    )(x, x, tproj, mask, bias_rows, *consts)


def put_tiles(out, first, acc):
    width = acc.shape[0]
    for j in range(acc.shape[1] // 128):
        at = (first + j) * width
        out[at : at + width, :] = acc[:, j * 128 : (j + 1) * 128].astype(out.dtype)


def put_rows(out, at, vectors):
    lines = [v[:, j : j + 128] for v in vectors for j in range(0, v.shape[1], 128)]
    lines += [jnp.zeros((1, 128), F32)] * (-len(lines) % 16)
    out[at : at + len(lines), :] = jnp.concatenate(lines, axis=0).astype(out.dtype)


def feed_back_kernel(
    gx,
    mid,
    act,
    slope,
    o,
    gain2,
    shift2,
    w1,
    w2,
    wo,
    gmid_out,
    go_out,
    grads_out,
    gw2t,
    gw1,
    gwo,
    sums,
    gb1,
    gu_scr,
):
    step = pl.program_id(0)

    @pl.when(step == 0)
    def _():
        for ref in (gw2t, gw1, gwo, sums, gb1):
            ref[...] = jnp.zeros_like(ref)

    grad = gx[...].astype(F32)
    gr = grad.astype(BF16)
    gr_t = gr.T
    xh, inverse = norm_stats(mid[...])
    c_t = (xh * gain2[...] + shift2[...]).astype(BF16).T
    hidden = act.shape[1]
    tile = 256
    for low in range(0, hidden, tile):
        cols = slice(low, low + tile)
        ge = dot_nt(gr, w2[cols, :])
        gu = (ge * slope[:, cols].astype(F32)).astype(BF16)
        gu_scr[:, cols] = gu
        gb1[:, cols] += row_sums(gu.astype(F32))
        gw2t[:, cols] += dot(gr_t, act[:, cols])
        gw1[:, cols] += dot(c_t, gu)
    gc = dot_nt(gu_scr[...], w1[...])
    gmid = grad + norm_back(gc, xh, inverse, gain2[...])
    gmid_out[...] = gmid
    gb = gmid.astype(BF16)
    gwo[...] += dot(o[...].T, gb)
    go_out[...] = dot_nt(gb, wo[...]).astype(BF16)
    sums[0] += row_sums(gr.astype(F32))
    sums[1] += row_sums(gb.astype(F32))
    sums[2] += row_sums(gc * xh)
    sums[3] += row_sums(gc)

    @pl.when(step == pl.num_programs(0) - 1)
    def _():
        tiles = hidden // 128
        put_tiles(grads_out, 0, gw2t)
        put_tiles(grads_out, tiles, gw1)
        put_tiles(grads_out, 2 * tiles, gwo)
        whole = [jnp.sum(sums[i], axis=0, keepdims=True) for i in range(4)]
        whole.append(jnp.sum(gb1[...], axis=0, keepdims=True))
        at = (2 * tiles + gwo.shape[1] // 128) * gwo.shape[0]
        put_rows(grads_out, at, whole)


def feed_rows(width, hidden):
    tiles = (2 * hidden + width) // 128
    return tiles * width, -(-(4 * width + hidden) // 128 // 16) * 16


def feed_back(gx, gx_lead, patches, mid, act, slope, o, gain2, shift2, w1, w2, wo):
    width = mid.shape[1]
    hidden = act.shape[1]

    def rows(cols, lead):
        return pl.BlockSpec((FEED, cols), lambda g: (g + lead, 0))

    grad_rows = sum(feed_rows(width, hidden))
    return pl.pallas_call(
        feed_back_kernel,
        grid=(patches // FEED,),
        in_specs=[
            rows(width, gx_lead),
            rows(width, 1),
            rows(hidden, 1),
            rows(hidden, 1),
            rows(width, 1),
        ]
        + [const_spec(w.shape) for w in (gain2, shift2, w1, w2, wo)],
        out_specs=[rows(width, 0), rows(width, 0), const_spec((grad_rows, 128))],
        out_shape=[
            jax.ShapeDtypeStruct((patches, width), F32),
            jax.ShapeDtypeStruct((patches, width), BF16),
            jax.ShapeDtypeStruct((grad_rows, 128), BF16),
        ],
        scratch_shapes=[
            pltpu.VMEM((width, hidden), F32),
            pltpu.VMEM((width, hidden), F32),
            pltpu.VMEM((width, width), F32),
            pltpu.VMEM((4, 8, width), F32),
            pltpu.VMEM((8, hidden), F32),
            pltpu.VMEM((FEED, hidden), BF16),
        ],
        compiler_params=pltpu.CompilerParams(vmem_limit_bytes=VMEM_BYTES),
        name="feed_back",
    )(gx, mid, act, slope, o, gain2, shift2, w1, w2, wo)


def attend_back_kernel(
    pairs,
    chunks,
    chunks_per_image,
    prev,
    cur,
    nxt,
    p_in,
    go_in,
    o_in,
    gmid,
    x,
    gain1,
    shift1,
    wqkv,
    gx_out,
    gtime,
    grads_out,
    gwqkv,
    gbias,
    sums,
    gq_ring,
    gkv_ring,
    gs_scr,
):
    step = pl.program_id(0)
    width = x.shape[1]

    @pl.when(step == 0)
    def _():
        for ref in (gwqkv, gbias, gtime, sums, gq_ring, gkv_ring):
            ref[...] = jnp.zeros_like(ref)

    gq_old = gq_ring[...]
    live = (step < chunks).astype(BF16)
    go = go_in[...] * live
    qkv = cur[...]
    queries = qkv[:, :width] * jnp.asarray(0.125, BF16)
    keys = jnp.concatenate(
        [prev[:, width : 2 * width], qkv[:, width : 2 * width], nxt[:, width : 2 * width]], axis=0
    )
    keys_t = keys.T
    values = jnp.concatenate([prev[:, 2 * width :], qkv[:, 2 * width :], nxt[:, 2 * width :]], axis=0)
    dots = (go.astype(F32) * o_in[...].astype(F32)).T
    blocks = CHUNK // QBLOCK
    todo = [(blk, pair) for pair in range(pairs) for blk in range(blocks)]

    def spread(blk, pair):
        low = blk * QBLOCK
        feat = slice(pair * 128, (pair + 1) * 128)
        split_go = split_heads(go[low : low + QBLOCK, feat])
        own = dots[feat, low : low + QBLOCK]
        row_dot = [jnp.sum(own[h * 64 : h * 64 + 64], axis=0, keepdims=True) for h in range(2)]
        for k in range(0, KWIN, 128):
            gp = dot_nt(values[low + k : low + k + 128, feat], split_go)
            for h in range(2):
                lane = slice(h * 128, h * 128 + 128)
                gs = p_in[blk, pair, k : k + 128, lane].astype(F32) * (gp[:, lane] - row_dot[h])
                gbias[pair, k : k + 128, lane] += gs
                gs_scr[blk, pair, k : k + 128, lane] = gs.astype(BF16)

    def pull(blk, pair):
        low = blk * QBLOCK
        feat = slice(pair * 128, (pair + 1) * 128)
        vfeat = slice(width + pair * 128, width + (pair + 1) * 128)
        gs = gs_scr[blk, pair]
        at = HALO + low
        gkv_ring[at : at + KWIN, feat] += dot(gs, split_heads(queries[low : low + QBLOCK, feat]))
        gkv_ring[at : at + KWIN, vfeat] += dot(
            p_in[blk, pair], split_heads(go[low : low + QBLOCK, feat])
        )
        gq = join_heads(dot(keys_t[feat, low : low + KWIN], gs)) * 0.125
        gq_ring[low : low + QBLOCK, feat] = gq.astype(BF16)

    for i in range(len(todo) + 1):
        if i < len(todo):
            spread(*todo[i])
        if i >= 1:
            pull(*todo[i - 1])

    done = jnp.concatenate([gq_old, gkv_ring[:CHUNK, :].astype(BF16)], axis=1)
    gkv_ring[:CHUNK, :] = gkv_ring[CHUNK : 2 * CHUNK, :]
    gkv_ring[CHUNK : CHUNK + HALO, :] = gkv_ring[2 * CHUNK :, :]
    gkv_ring[CHUNK + HALO :, :] = jnp.zeros((CHUNK, 2 * width), F32)
    xh, inverse = norm_stats(x[...].astype(F32))
    a = (xh * gain1[...] + shift1[...]).astype(BF16)
    gwqkv[...] += dot(a.T, done)
    ga = dot_nt(done, wqkv[...])
    gx_out[...] = (gmid[...] + norm_back(ga, xh, inverse, gain1[...])).astype(gx_out.dtype)
    sums[0] += row_sums(ga * xh)
    sums[1] += row_sums(ga)
    first = lax.rem(step + chunks_per_image - 1, chunks_per_image) == 0
    before = jnp.where(first, jnp.zeros(gtime.shape[1:], F32), gtime[0])
    summed = row_sums(done.astype(F32))
    gtime[0] = before + jnp.concatenate([summed[:, :width], summed[:, 2 * width :]], axis=1)

    @pl.when(step == chunks)
    def _():
        put_tiles(grads_out, 0, gwqkv)
        tiles = gwqkv.shape[1] // 128
        lines = attend_rows(width)[2]
        grads_out[tiles * width : tiles * width + lines, :] = gather_bias(gbias).astype(BF16)
        put_rows(
            grads_out,
            tiles * width + lines,
            [jnp.sum(sums[i], axis=0, keepdims=True) for i in range(2)],
        )


def attend_rows(width):
    lines = 2 * (width // 128) * (KWIN * 4 // QBLOCK) * 2
    small = -(-2 * width // 128 // 16) * 16
    return 3 * width // 128 * width, 3 * width // 128 * width + lines + small, lines


def attend_back(
    qkv, p, go, o, gmid, x, x_lead, chunks, chunks_per_image, gain1, shift1, wqkv, out_dtype
):
    width = x.shape[1]
    pairs = width // 128
    steps = chunks + 1
    halves = CHUNK // HALO

    def now(g):
        return jnp.minimum(g, chunks - 1)

    def late(g):
        return jnp.maximum(g - 1, 0)

    def rows(cols, lead, index):
        return pl.BlockSpec((CHUNK, cols), lambda g: (index(g) + lead, 0))

    images = chunks // chunks_per_image
    grad_rows = attend_rows(width)[1]
    return pl.pallas_call(
        functools.partial(attend_back_kernel, pairs, chunks, chunks_per_image),
        grid=(steps,),
        in_specs=[
            pl.BlockSpec((HALO, 3 * width), lambda g: (jnp.maximum(halves * now(g) - 1, 0), 0)),
            rows(3 * width, 0, now),
            pl.BlockSpec(
                (HALO, 3 * width),
                lambda g: (jnp.minimum(halves * (now(g) + 1), halves * chunks - 1), 0),
            ),
            pl.BlockSpec(
                (CHUNK // QBLOCK, pairs, KWIN, 2 * QBLOCK), lambda g: (now(g) + 1, 0, 0, 0)
            ),
            rows(width, 0, now),
            rows(width, 2, now),
            rows(width, 0, late),
            rows(width, x_lead, late),
        ]
        + [const_spec(w.shape) for w in (gain1, shift1, wqkv)],
        out_specs=[
            rows(width, 1, lambda g: g),
            pl.BlockSpec((1, 8, 2 * width), lambda g: (late(g) // chunks_per_image, 0, 0)),
            const_spec((grad_rows, 128)),
        ],
        out_shape=[
            jax.ShapeDtypeStruct(((steps + 1) * CHUNK, width), out_dtype),
            jax.ShapeDtypeStruct((images, 8, 2 * width), F32),
            jax.ShapeDtypeStruct((grad_rows, 128), BF16),
        ],
        scratch_shapes=[
            pltpu.VMEM((width, 3 * width), F32),
            pltpu.VMEM((pairs, KWIN, 2 * QBLOCK), F32),
            pltpu.VMEM((2, 8, width), F32),
            pltpu.VMEM((CHUNK, width), BF16),
            pltpu.VMEM((2 * CHUNK + HALO, 2 * width), F32),
            pltpu.VMEM((CHUNK // QBLOCK, pairs, KWIN, 2 * QBLOCK), BF16),
        ],
        compiler_params=pltpu.CompilerParams(vmem_limit_bytes=VMEM_BYTES),
        name="attend_back",
    )(qkv, qkv, qkv, p, go, o, gmid, x, gain1, shift1, wqkv)


def share_rows(rows):
    return max(n for n in range(16, 257, 16) if rows % n == 0)


def add_rows(total, at, others, rows):
    share = share_rows(rows)

    def one(i, carry):
        low = pl.multiple_of(i * share, 16)
        here = pl.ds(pl.multiple_of(at + low, 16), share)
        v = total[here, :].astype(F32)
        for ref, row in others:
            v = v + ref[pl.ds(pl.multiple_of(row + low, 16), share), :].astype(F32)
        total[here, :] = v.astype(total.dtype)
        return carry

    lax.fori_loop(0, rows // share, one, 0)


def cut(ref, at, rows):
    return ref.at[pl.ds(pl.multiple_of(at, 16), rows), :]


class Places:
    def __init__(self, plan):
        self.xs, self.bs, self.zs = plan
        self.img = lax.axis_index("img")
        self.b = lax.axis_index("band")
        self.c = lax.rem(self.img, 2)
        self.x = lax.rem(self.img // 2, self.xs)
        self.z = self.img // (2 * self.xs)

    def core(self, by):
        return (self.img + 1 - 2 * self.c, self.b)

    def along_x(self, by):
        return ((self.z * self.xs + lax.rem(self.x + by, self.xs)) * 2 + self.c, self.b)

    def along_b(self, by):
        return (self.img, lax.rem(self.b + by, self.bs))

    def along_z(self, by):
        return ((lax.rem(self.z + by, self.zs) * self.xs + self.x) * 2 + self.c, self.b)

    def greet(self):
        barrier = pltpu.get_barrier_semaphore()
        peers = [self.core(1)]
        peers += [self.along_x(by) for by in range(1, self.xs)]
        peers += [self.along_b(by) for by in range(1, self.bs)]
        peers += [self.along_z(by) for by in range(1, self.zs)]
        for peer in peers:
            pl.semaphore_signal(barrier, inc=1, device_id=peer, device_id_type=pl.DeviceIdType.MESH)
        pl.semaphore_wait(barrier, len(peers))


class Lane:
    def __init__(self, plan, sems):
        self.plan, self.sems, self.steps = plan, sems, []

    def add(self, copies, then=None):
        count = [0, 0]
        here = Places(self.plan)
        for src, dst, peer in copies(here):
            count[peer is None] += 1
        base = (self.sems.sent, self.sems.kept)
        self.sems.sent += count[0]
        self.sems.kept += count[1]
        self.steps.append((copies, then, base))

    def described(self, step):
        copies, _, (sent, kept) = self.steps[step]
        made = []
        for src, dst, peer in copies(Places(self.plan)):
            if peer is None:
                made.append(pltpu.make_async_copy(src, dst, self.sems.own.at[kept]))
                kept += 1
            else:
                made.append(
                    pltpu.make_async_remote_copy(
                        src_ref=src,
                        dst_ref=dst,
                        send_sem=self.sems.send.at[sent],
                        recv_sem=self.sems.recv.at[sent],
                        device_id=peer,
                        device_id_type=pl.DeviceIdType.MESH,
                    )
                )
                sent += 1
        return made

    def part(self, i):
        if i > 0:
            for copy in self.described(i - 1):
                copy.wait()
            if self.steps[i - 1][1] is not None:
                self.steps[i - 1][1](Places(self.plan))
        if i < len(self.steps):
            for copy in self.described(i):
                copy.start()


class Sems:
    def __init__(self, send, recv, own):
        self.send, self.recv, self.own = send, recv, own
        self.sent = self.kept = 0


def scatter_lane(lane, grad, held, chunk=None):
    acc, r1, r2a, r2b, r3a, r3b, r4 = held
    xs, bs, zs = lane.plan
    half = grad.shape[0] // 2
    quarter = half // 2
    nx, nb, n2 = quarter // xs, quarter // bs, quarter // (xs * bs)
    n = n2 // zs

    def core_copies(at):
        return [
            (cut(grad, at.c * half, half), acc, None),
            (cut(grad, half - at.c * half, half), r1, at.core(1)),
        ]

    lane.add(core_copies, lambda at: add_rows(acc, 0, [(r1, 0)], half))

    def wide_copies(at):
        made = []
        for by in range(1, xs):
            there = lax.rem(at.x + by, xs)
            made.append((cut(acc, there * nx, nx), cut(r2a, (by - 1) * nx, nx), at.along_x(by)))
        for by in range(1, bs):
            there = quarter + lax.rem(at.b + by, bs) * nb
            made.append((cut(acc, there, nb), cut(r2b, (by - 1) * nb, nb), at.along_b(by)))
        return made

    def wide_add(at):
        add_rows(acc, at.x * nx, [(r2a, k * nx) for k in range(xs - 1)], nx)
        add_rows(acc, quarter + at.b * nb, [(r2b, k * nb) for k in range(bs - 1)], nb)

    lane.add(wide_copies, wide_add)

    def cross_copies(at):
        made = []
        for by in range(1, bs):
            there = at.x * nx + lax.rem(at.b + by, bs) * n2
            made.append((cut(acc, there, n2), cut(r3a, (by - 1) * n2, n2), at.along_b(by)))
        for by in range(1, xs):
            there = quarter + at.b * nb + lax.rem(at.x + by, xs) * n2
            made.append((cut(acc, there, n2), cut(r3b, (by - 1) * n2, n2), at.along_x(by)))
        return made

    def plane(at):
        return at.x * nx + at.b * n2, quarter + at.b * nb + at.x * n2

    def cross_add(at):
        first, second = plane(at)
        add_rows(acc, first, [(r3a, k * n2) for k in range(bs - 1)], n2)
        add_rows(acc, second, [(r3b, k * n2) for k in range(xs - 1)], n2)

    lane.add(cross_copies, cross_add)

    def deep_copies(at):
        made = []
        for by in range(1, zs):
            there = lax.rem(at.z + by, zs) * n
            for k, low in enumerate(plane(at)):
                slot = (2 * (by - 1) + k) * n
                made.append((cut(acc, low + there, n), cut(r4, slot, n), at.along_z(by)))
        return made

    def deep_add(at):
        for k, low in enumerate(plane(at)):
            add_rows(acc, low + at.z * n, [(r4, (2 * i + k) * n) for i in range(zs - 1)], n)

    lane.add(deep_copies, deep_add)

    def ends(at):
        return [cut(acc, low + at.z * n, n) for low in plane(at)]

    if chunk is None:
        return ends
    lane.add(lambda at: [(ref, cut(chunk, k * n, n), None) for k, ref in enumerate(ends(at))])


def collect_lane(lane, ends, out):
    xs, bs, zs = lane.plan
    half = out.shape[0] // 2
    quarter = half // 2
    nx, nb, n2 = quarter // xs, quarter // bs, quarter // (xs * bs)
    n = n2 // zs

    def plane(at):
        base = at.c * half
        return base + at.x * nx + at.b * n2, base + quarter + at.b * nb + at.x * n2

    def deep(at):
        made = []
        for ref, low in zip(ends(at), plane(at)):
            there = cut(out, low + at.z * n, n)
            made.append((ref, there, None))
            made += [(ref, there, at.along_z(by)) for by in range(1, zs)]
        return made

    def cross(at):
        first, second = plane(at)
        a, b = cut(out, first, n2), cut(out, second, n2)
        made = [(a, a, at.along_b(by)) for by in range(1, bs)]
        return made + [(b, b, at.along_x(by)) for by in range(1, xs)]

    def wide(at):
        a = cut(out, at.c * half + at.x * nx, nx)
        b = cut(out, at.c * half + quarter + at.b * nb, nb)
        made = [(a, a, at.along_x(by)) for by in range(1, xs)]
        return made + [(b, b, at.along_b(by)) for by in range(1, bs)]

    def core(at):
        whole = cut(out, at.c * half, half)
        return [(whole, whole, at.core(1))]

    for copies in (deep, cross, wide, core):
        lane.add(copies)


def extra_lane(lane, extra, out):
    xs, bs, zs = lane.plan
    rows = extra.shape[0]

    def deep(at):
        there = cut(out, (((at.c * xs + at.x) * bs + at.b) * zs + at.z) * rows, rows)
        return [(extra, there, None)] + [(extra, there, at.along_z(by)) for by in range(1, zs)]

    def cross(at):
        there = cut(out, ((at.c * xs + at.x) * bs + at.b) * zs * rows, zs * rows)
        return [(there, there, at.along_b(by)) for by in range(1, bs)]

    def wide(at):
        there = cut(out, (at.c * xs + at.x) * bs * zs * rows, bs * zs * rows)
        return [(there, there, at.along_x(by)) for by in range(1, xs)]

    def core(at):
        there = cut(out, at.c * xs * bs * zs * rows, xs * bs * zs * rows)
        return [(there, there, at.core(1))]

    for copies in (deep, cross, wide, core):
        lane.add(copies)


def bands_lane(lane, whole, lead, out):
    bs = lane.plan[1]
    rows, width = out.shape[2:]
    own = out.shape[1]

    def copies(at):
        made = []
        for by in range(bs):
            there = lax.rem(at.b + by, bs)
            for i in range(own):
                src = cut(whole, lead + (i * bs + there) * rows, rows)
                made.append((src, out.at[at.b, i], at.along_b(by) if by else None))
        return made

    lane.add(copies)


def link_plan():
    pairs = lax.axis_size("img") // 2
    xs = 2 if pairs % 2 == 0 else 1
    return xs, lax.axis_size("band"), pairs // xs


def held_shapes(plan, rows):
    xs, bs, zs = plan
    quarter = rows // 4
    sizes = [
        rows // 2,
        rows // 2,
        (xs - 1) * quarter // xs,
        (bs - 1) * quarter // bs,
        (bs - 1) * quarter // (xs * bs),
        (xs - 1) * quarter // (xs * bs),
        (zs - 1) * 2 * quarter // (xs * bs * zs),
    ]
    return [pltpu.VMEM((max(n, 16), 128), BF16) for n in sizes]


def sems_shapes(plan, lanes, moved=0):
    xs, bs, zs = plan
    count = lanes * (1 + 2 * (xs - 1 + bs - 1) + 2 * (zs - 1)) + moved
    return [
        pltpu.SemaphoreType.DMA((count,)),
        pltpu.SemaphoreType.DMA((count,)),
        pltpu.SemaphoreType.DMA((2 * lanes + moved + 1,)),
    ]


def final_kernel(plan, count, lead, *refs):
    grads, extra, whole = refs[:count], refs[count], refs[count + 1]
    outs, extra_out, bands_out = refs[count + 2 : 2 * count + 2], refs[2 * count + 2], refs[2 * count + 3]
    scratch = refs[2 * count + 4 :]
    sems = Sems(*scratch[-3:])
    each = 7
    Places(plan).greet()
    lanes = []
    for i in range(count):
        lane = Lane(plan, sems)
        ends = scatter_lane(lane, grads[i], scratch[i * each : (i + 1) * each])
        collect_lane(lane, ends, outs[i])
        lanes.append(lane)
    lane = Lane(plan, sems)
    extra_lane(lane, extra, extra_out)
    lanes.append(lane)
    late = Lane(plan, sems)
    bands_lane(late, whole, lead, bands_out)
    late.part(0)
    for i in range(max(len(lane.steps) for lane in lanes) + 1):
        for lane in lanes:
            if i <= len(lane.steps):
                lane.part(i)
    late.part(1)


def final_exchange(grads, extra, whole, lead, own, part):
    plan = link_plan()
    xs, bs, zs = plan
    count = len(grads)
    held = []
    for grad in grads:
        held += held_shapes(plan, grad.shape[0])
    anywhere = pl.BlockSpec(memory_space=pl.ANY)
    out = pl.pallas_call(
        functools.partial(final_kernel, plan, count, lead),
        in_specs=[anywhere] * (count + 2),
        out_specs=[anywhere] * (count + 2),
        out_shape=[jax.ShapeDtypeStruct(grad.shape, BF16) for grad in grads]
        + [
            jax.ShapeDtypeStruct((2 * xs * bs * zs * extra.shape[0], 128), BF16),
            jax.ShapeDtypeStruct((bs, own, part, whole.shape[1]), BF16),
        ],
        scratch_shapes=held + sems_shapes(plan, 2 * count + 1, bs * own),
        compiler_params=pltpu.CompilerParams(
            vmem_limit_bytes=VMEM_BYTES, collective_id=0, has_side_effects=True
        ),
        name="final_exchange",
    )(*grads, extra, whole)
    return out[:count], out[count], out[count + 1]


def unpack_kernel(layers, *refs):
    ins = [refs[4 * i : 4 * i + 4] for i in range(layers)]
    w2_out, w1_out, attend_out, wo_out = refs[4 * layers :]
    width = w1_out.shape[1]
    for layer, (w2t, w1, attend, wo) in enumerate(ins):
        for j in range(w1.shape[0] // width):
            rows = slice(j * width, (j + 1) * width)
            cols = slice(j * 128, (j + 1) * 128)
            w2_out[layer, cols, :] = w2t[rows, :].astype(F32).T
            w1_out[layer, :, cols] = w1[rows, :].astype(F32)
            attend_out[layer, :, cols] = attend[rows, :].astype(F32)
            wo_out[layer, :, cols] = wo[rows, :].astype(F32)


def unpack(fulls, width, hidden):
    layers = len(fulls)
    wide = width // 128
    steps = hidden // width
    rows = wide * width
    last = 3 * width // width - 1
    block = (rows, 128)

    def spec(first, top):
        return pl.BlockSpec(block, lambda g: (first + jnp.minimum(g, top), 0))

    ins = [
        spec(0, steps),
        spec(steps, steps),
        spec(2 * steps + 1, last),
        spec(2 * steps, 0),
    ]
    return pl.pallas_call(
        functools.partial(unpack_kernel, layers),
        grid=(steps,),
        in_specs=ins * layers,
        out_specs=[
            pl.BlockSpec((layers, width, width), lambda g: (0, g, 0)),
            pl.BlockSpec((layers, width, width), lambda g: (0, 0, g)),
            pl.BlockSpec((layers, width, width), lambda g: (0, 0, jnp.minimum(g, last))),
            pl.BlockSpec((layers, width, width), lambda g: (0, 0, 0)),
        ],
        out_shape=[
            jax.ShapeDtypeStruct((layers, hidden, width), F32),
            jax.ShapeDtypeStruct((layers, width, hidden), F32),
            jax.ShapeDtypeStruct((layers, width, 3 * width), F32),
            jax.ShapeDtypeStruct((layers, width, width), F32),
        ],
        compiler_params=pltpu.CompilerParams(vmem_limit_bytes=VMEM_BYTES),
        name="unpack",
    )(*[full for full in fulls for _ in range(4)])


def time_embedding(timesteps, width):
    half_width = width // 2
    frequency = jnp.exp(
        jnp.arange(half_width, dtype=jnp.int32).astype(F32) * (-math.log(10000.0) / half_width)
    )
    angles = timesteps.astype(F32)[:, None] * frequency[None, :]
    return jnp.concatenate([jnp.sin(angles), jnp.cos(angles)], axis=-1)


def bias_rows(table, index_table, grid_cols):
    heads, entries = table.shape
    span = 2 * WIN + 1
    offsets = 2 * grid_cols - 1
    turned = index_table.reshape(span, offsets)[:, ::-1].reshape(entries)
    select = (turned[None, :] == jnp.arange(entries, dtype=jnp.int32)[:, None]).astype(F32)
    rows = jnp.dot(table, select, precision=EXACT).reshape(heads, span, offsets)
    key_rows = KWIN // grid_cols
    a0, a1, a2, a3 = [
        jnp.pad(
            rows, ((0, 0), (q, key_rows - span - q), (0, 0)), constant_values=NEG_FILL
        )
        for q in range(QBLOCK // grid_cols)
    ]
    gap = jnp.full((heads, key_rows, 1), NEG_FILL, F32)
    even = jnp.concatenate(
        [a0[..., grid_cols - 1 :], gap, a2, gap, a0[..., : grid_cols - 1]], axis=-1
    )
    odd = jnp.concatenate([gap, a1, gap, a3], axis=-1)
    return jnp.stack([even, odd], axis=1)


def body(
    tokens,
    cotangent,
    valid_mask,
    timesteps,
    index_table,
    first_gain,
    first_shift,
    attend_weight,
    time_weight,
    offset_bias,
    output_weight,
    output_bias,
    second_gain,
    second_shift,
    expand_weight,
    expand_bias,
    reduce_weight,
    reduce_bias,
):
    images, band_rows, grid_cols, width = tokens.shape
    layers = attend_weight.shape[0]
    bands = lax.axis_size("band")
    me = lax.axis_index("band")
    own = images // bands
    part = band_rows * grid_cols
    patches = bands * part
    per_image = patches // CHUNK
    chunks = own * per_image

    def to_images(shard):
        shard = shard.reshape(bands, own, part, width)
        whole = jnp.zeros((own, bands, part, width), shard.dtype)
        for by in range(bands):
            piece = lax.dynamic_index_in_dim(shard, (me + by) % bands, 0, keepdims=False)
            if by:
                pairs = [(i, (i + by) % bands) for i in range(bands)]
                piece = lax.ppermute(piece, "band", pairs)
            whole = lax.dynamic_update_index_in_dim(whole, piece, (me - by) % bands, 1)
        return whole.reshape(own * patches, width)

    def to_bands(whole):
        whole = whole.reshape(own, bands, part, width)
        shard = jnp.zeros((bands, own, part, width), whole.dtype)
        for by in range(bands):
            piece = lax.dynamic_index_in_dim(whole, (me + by) % bands, 1, keepdims=False)
            if by:
                pairs = [(i, (i + by) % bands) for i in range(bands)]
                piece = lax.ppermute(piece, "band", pairs)
            shard = lax.dynamic_update_index_in_dim(shard, piece, (me - by) % bands, 0)
        return shard.reshape(images, band_rows, grid_cols, width)

    x0 = to_images(tokens)
    x0, late = lax.optimization_barrier((x0, cotangent))
    cot = to_images(late)

    mine = lax.dynamic_slice_in_dim(valid_mask, me * own, own, 0).reshape(own, patches)
    fill = jnp.where(mine == 1, 0.0, NEG_FILL).astype(F32)
    fill = jnp.pad(fill, ((0, 0), (HALO, HALO)), constant_values=NEG_FILL)
    mask = jnp.stack(
        [fill[:, c * CHUNK : (c + 1) * CHUNK + 2 * HALO] for c in range(per_image)], axis=1
    ).reshape(chunks, 1, CHUNK + 2 * HALO)

    time_low = time_embedding(
        lax.dynamic_slice_in_dim(timesteps, me * own, own, 0), width
    ).astype(BF16)
    heads, entries = offset_bias.shape[1:]

    def make_rows(table):
        return bias_rows(table, index_table, grid_cols)

    biases, bias_pull = jax.vjp(make_rows, offset_bias.reshape(layers * heads, entries))
    biases = biases.reshape(layers, -1, QBLOCK)

    def row(v):
        return v.reshape(1, -1)

    x, x_lead = x0, 0
    kept = []
    for layer in range(layers):
        tp = jnp.dot(time_low, time_weight[layer], preferred_element_type=F32)
        tproj = jnp.concatenate([tp[:, :width], jnp.zeros_like(tp[:, :width]), tp[:, width:]], axis=1)
        weights = (
            row(first_gain[layer]),
            row(first_shift[layer]),
            attend_weight[layer],
            output_weight[layer],
            row(output_bias[layer]),
            row(second_gain[layer]),
            row(second_shift[layer]),
            expand_weight[layer],
            row(expand_bias[layer]),
            reduce_weight[layer],
            row(reduce_bias[layer]),
        )
        qkv, p, o, mid, act, slope, nxt = forward_layer(
            x,
            x_lead,
            chunks,
            per_image,
            tproj[:, None, :],
            mask,
            biases[layer],
            weights,
            F32 if layer < layers - 1 else BF16,
        )
        kept.append((x, x_lead, qkv, p, o, mid, act, slope))
        x, x_lead = nxt, 2
    output = to_bands(x[x_lead * CHUNK :])

    gx, gx_lead = cot, 0
    devices = bands * lax.axis_size("img")
    big, feed_small = feed_rows(width, expand_weight.shape[2])
    attend_big, attend_all, lines = attend_rows(width)
    used = big + feed_small + attend_all
    buckets = [None] * layers
    extra = [time_low]
    for layer in reversed(range(layers)):
        x, x_lead, qkv, p, o, mid, act, slope = kept[layer]
        gmid, go, feed_grads = feed_back(
            gx,
            gx_lead,
            own * patches,
            mid,
            act,
            slope,
            o,
            row(second_gain[layer]),
            row(second_shift[layer]),
            expand_weight[layer],
            reduce_weight[layer],
            output_weight[layer],
        )
        if layer == layers - 1:
            gmid, output = lax.optimization_barrier((gmid, output))
        gx, gtime, attend_grads = attend_back(
            qkv,
            p,
            go,
            o,
            gmid,
            x,
            x_lead,
            chunks,
            per_image,
            row(first_gain[layer]),
            row(first_shift[layer]),
            attend_weight[layer],
            F32 if layer else BF16,
        )
        gx_lead = 1
        spare = jnp.zeros((-used % (devices * 32), 128), BF16)
        buckets[layer] = jnp.concatenate(
            [feed_grads[:big], attend_grads[:attend_big], feed_grads[big:], attend_grads[attend_big:], spare]
        )
        extra.append(jnp.sum(gtime, axis=1).astype(BF16))
    extra = jnp.concatenate(extra, axis=1).reshape(-1, 128)
    lead = extra.shape[0]
    extra = jnp.pad(extra, ((0, -lead % 16), (0, 0)))
    fulls, gathered, input_grad = final_exchange(buckets, extra, gx, 2 * CHUNK, own, part)
    input_grad = input_grad.reshape(tokens.shape)
    gathered = gathered.reshape(devices, -1, 128)[:, :lead].reshape(devices * own, -1)
    grad_time = jnp.stack(
        [
            lax.dot_general(
                gathered[:, :width],
                gathered[:, width * (1 + 2 * turn) : width * (3 + 2 * turn)],
                (((0,), (0,)), ((), ())),
                preferred_element_type=F32,
            )
            for turn in reversed(range(layers))
        ]
    )
    grad_reduce, grad_expand, grad_attend, grad_output = unpack(fulls, width, expand_weight.shape[2])
    small = jnp.stack([full[big + attend_big : used] for full in fulls]).astype(F32)
    each = width // 128

    def vector(at, count):
        return small[:, at : at + count].reshape(layers, count * 128)

    grad_rows = small[:, feed_small : feed_small + lines]
    (grad_offset,) = bias_pull(grad_rows.reshape(layers * heads, 2, -1, QBLOCK))
    tail = feed_small + lines
    return (
        output,
        input_grad,
        vector(tail, each),
        vector(tail + each, each),
        grad_attend,
        grad_time,
        grad_offset.reshape(layers, heads, entries),
        grad_output,
        vector(each, each),
        vector(2 * each, each),
        vector(3 * each, each),
        grad_expand,
        vector(4 * each, expand_weight.shape[2] // 128),
        grad_reduce,
        vector(0, each),
    )


def solution(mesh):
    split = P("img", "band", None, None)
    placed = (split, split, P("img", None, None), P("img")) + (P(),) * 14
    return jax.shard_map(
        body,
        mesh=mesh,
        in_specs=placed,
        out_specs=(split, split) + (P(),) * 13,
        check_vma=False,
    )
```

```python
import functools
import math

import jax
import jax.numpy as jnp
from jax import lax
from jax.experimental import pallas as pl
from jax.experimental.pallas import tpu as pltpu
from jax.sharding import PartitionSpec as P

WIN = 4
CHUNK = 256
QBLOCK = 128
KWIN = 384
HALO = 128
FEED = 512

EXACT = lax.Precision.HIGHEST
NEG_FILL = -1000000000.0
EPSILON = 1e-06
GELU_A = math.sqrt(2.0 / math.pi)
GELU_B = 0.044715 * GELU_A
VMEM_BYTES = 58 * 1024 * 1024

F32 = jnp.float32
BF16 = jnp.bfloat16


def dot(a, b):
    return jnp.dot(a, b, preferred_element_type=F32)


def dot_nt(a, b):
    return lax.dot_general(a, b, (((1,), (1,)), ((), ())), preferred_element_type=F32)


def norm_stats(v):
    mean = jnp.mean(v, axis=-1, keepdims=True)
    centered = v - mean
    inverse = lax.rsqrt(jnp.mean(centered * centered, axis=-1, keepdims=True) + EPSILON)
    return centered * inverse, inverse


def norm_back(gy, xh, inverse, gain):
    gs = gy * gain
    return inverse * (
        gs - jnp.mean(gs, axis=-1, keepdims=True) - xh * jnp.mean(gs * xh, axis=-1, keepdims=True)
    )


def row_sums(v):
    rows, cols = v.shape
    return jnp.sum(v.reshape(rows // 8, 8, cols), axis=0)


def split_heads(block):
    lane = lax.broadcasted_iota(jnp.int32, block.shape, 1)
    zero = jnp.zeros_like(block)
    first = lane < block.shape[1] // 2
    return jnp.concatenate(
        [jnp.where(first, block, zero), jnp.where(first, zero, block)], axis=0
    )


def join_heads(product):
    half = product.shape[0] // 2
    width = product.shape[1] // 2
    return jnp.concatenate([product[:half, :width], product[half:, width:]], axis=0).T


def share_rows(rows):
    return max(n for n in range(16, 257, 16) if rows % n == 0)


def add_rows(total, at, others, rows):
    share = share_rows(rows)

    def one(i, carry):
        low = pl.multiple_of(i * share, 16)
        here = pl.ds(pl.multiple_of(at + low, 16), share)
        v = total[here, :].astype(F32)
        for ref, row in others:
            v = v + ref[pl.ds(pl.multiple_of(row + low, 16), share), :].astype(F32)
        total[here, :] = v.astype(total.dtype)
        return carry

    lax.fori_loop(0, rows // share, one, 0)


def cut(ref, at, rows):
    return ref.at[pl.ds(pl.multiple_of(at, 16), rows), :]


class Places:
    def __init__(self, plan):
        self.xs, self.bs, self.zs = plan
        self.img = lax.axis_index("img")
        self.b = lax.axis_index("band")
        self.c = lax.rem(self.img, 2)
        self.x = lax.rem(self.img // 2, self.xs)
        self.z = self.img // (2 * self.xs)

    def core(self, by):
        return (self.img + 1 - 2 * self.c, self.b)

    def along_x(self, by):
        return ((self.z * self.xs + lax.rem(self.x + by, self.xs)) * 2 + self.c, self.b)

    def along_b(self, by):
        return (self.img, lax.rem(self.b + by, self.bs))

    def along_z(self, by):
        return ((lax.rem(self.z + by, self.zs) * self.xs + self.x) * 2 + self.c, self.b)

    def greet(self):
        barrier = pltpu.get_barrier_semaphore()
        peers = [self.core(1)]
        peers += [self.along_x(by) for by in range(1, self.xs)]
        peers += [self.along_b(by) for by in range(1, self.bs)]
        peers += [self.along_z(by) for by in range(1, self.zs)]
        for peer in peers:
            pl.semaphore_signal(barrier, inc=1, device_id=peer, device_id_type=pl.DeviceIdType.MESH)
        pl.semaphore_wait(barrier, len(peers))


class Lane:
    def __init__(self, plan, sems):
        self.plan, self.sems, self.steps = plan, sems, []

    def add(self, copies, then=None):
        count = [0, 0]
        here = Places(self.plan)
        for src, dst, peer in copies(here):
            count[peer is None] += 1
        base = (self.sems.sent, self.sems.kept)
        self.sems.sent += count[0]
        self.sems.kept += count[1]
        self.steps.append((copies, then, base))

    def described(self, step):
        copies, _, (sent, kept) = self.steps[step]
        made = []
        for src, dst, peer in copies(Places(self.plan)):
            if peer is None:
                made.append(pltpu.make_async_copy(src, dst, self.sems.own.at[kept]))
                kept += 1
            else:
                made.append(
                    pltpu.make_async_remote_copy(
                        src_ref=src,
                        dst_ref=dst,
                        send_sem=self.sems.send.at[sent],
                        recv_sem=self.sems.recv.at[sent],
                        device_id=peer,
                        device_id_type=pl.DeviceIdType.MESH,
                    )
                )
                sent += 1
        return made

    def part(self, i):
        if i > 0:
            for copy in self.described(i - 1):
                copy.wait()
            if self.steps[i - 1][1] is not None:
                self.steps[i - 1][1](Places(self.plan))
        if i < len(self.steps):
            for copy in self.described(i):
                copy.start()


class Sems:
    def __init__(self, send, recv, own):
        self.send, self.recv, self.own = send, recv, own
        self.sent = self.kept = 0


def scatter_lane(lane, grad, held, chunk=None):
    acc, r1, r2a, r2b, r3a, r3b, r4 = held
    xs, bs, zs = lane.plan
    half = grad.shape[0] // 2
    quarter = half // 2
    nx, nb, n2 = quarter // xs, quarter // bs, quarter // (xs * bs)
    n = n2 // zs

    def core_copies(at):
        return [
            (cut(grad, at.c * half, half), acc, None),
            (cut(grad, half - at.c * half, half), r1, at.core(1)),
        ]

    lane.add(core_copies, lambda at: add_rows(acc, 0, [(r1, 0)], half))

    def wide_copies(at):
        made = []
        for by in range(1, xs):
            there = lax.rem(at.x + by, xs)
            made.append((cut(acc, there * nx, nx), cut(r2a, (by - 1) * nx, nx), at.along_x(by)))
        for by in range(1, bs):
            there = quarter + lax.rem(at.b + by, bs) * nb
            made.append((cut(acc, there, nb), cut(r2b, (by - 1) * nb, nb), at.along_b(by)))
        return made

    def wide_add(at):
        add_rows(acc, at.x * nx, [(r2a, k * nx) for k in range(xs - 1)], nx)
        add_rows(acc, quarter + at.b * nb, [(r2b, k * nb) for k in range(bs - 1)], nb)

    lane.add(wide_copies, wide_add)

    def cross_copies(at):
        made = []
        for by in range(1, bs):
            there = at.x * nx + lax.rem(at.b + by, bs) * n2
            made.append((cut(acc, there, n2), cut(r3a, (by - 1) * n2, n2), at.along_b(by)))
        for by in range(1, xs):
            there = quarter + at.b * nb + lax.rem(at.x + by, xs) * n2
            made.append((cut(acc, there, n2), cut(r3b, (by - 1) * n2, n2), at.along_x(by)))
        return made

    def plane(at):
        return at.x * nx + at.b * n2, quarter + at.b * nb + at.x * n2

    def cross_add(at):
        first, second = plane(at)
        add_rows(acc, first, [(r3a, k * n2) for k in range(bs - 1)], n2)
        add_rows(acc, second, [(r3b, k * n2) for k in range(xs - 1)], n2)

    lane.add(cross_copies, cross_add)

    def deep_copies(at):
        made = []
        for by in range(1, zs):
            there = lax.rem(at.z + by, zs) * n
            for k, low in enumerate(plane(at)):
                slot = (2 * (by - 1) + k) * n
                made.append((cut(acc, low + there, n), cut(r4, slot, n), at.along_z(by)))
        return made

    def deep_add(at):
        for k, low in enumerate(plane(at)):
            add_rows(acc, low + at.z * n, [(r4, (2 * i + k) * n) for i in range(zs - 1)], n)

    lane.add(deep_copies, deep_add)

    def ends(at):
        return [cut(acc, low + at.z * n, n) for low in plane(at)]

    if chunk is None:
        return ends
    lane.add(lambda at: [(ref, cut(chunk, k * n, n), None) for k, ref in enumerate(ends(at))])


def collect_lane(lane, ends, out):
    xs, bs, zs = lane.plan
    half = out.shape[0] // 2
    quarter = half // 2
    nx, nb, n2 = quarter // xs, quarter // bs, quarter // (xs * bs)
    n = n2 // zs

    def plane(at):
        base = at.c * half
        return base + at.x * nx + at.b * n2, base + quarter + at.b * nb + at.x * n2

    def deep(at):
        made = []
        for ref, low in zip(ends(at), plane(at)):
            there = cut(out, low + at.z * n, n)
            made.append((ref, there, None))
            made += [(ref, there, at.along_z(by)) for by in range(1, zs)]
        return made

    def cross(at):
        first, second = plane(at)
        a, b = cut(out, first, n2), cut(out, second, n2)
        made = [(a, a, at.along_b(by)) for by in range(1, bs)]
        return made + [(b, b, at.along_x(by)) for by in range(1, xs)]

    def wide(at):
        a = cut(out, at.c * half + at.x * nx, nx)
        b = cut(out, at.c * half + quarter + at.b * nb, nb)
        made = [(a, a, at.along_x(by)) for by in range(1, xs)]
        return made + [(b, b, at.along_b(by)) for by in range(1, bs)]

    def core(at):
        whole = cut(out, at.c * half, half)
        return [(whole, whole, at.core(1))]

    for copies in (deep, cross, wide, core):
        lane.add(copies)


def extra_lane(lane, extra, out):
    xs, bs, zs = lane.plan
    rows = extra.shape[0]

    def deep(at):
        there = cut(out, (((at.c * xs + at.x) * bs + at.b) * zs + at.z) * rows, rows)
        return [(extra, there, None)] + [(extra, there, at.along_z(by)) for by in range(1, zs)]

    def cross(at):
        there = cut(out, ((at.c * xs + at.x) * bs + at.b) * zs * rows, zs * rows)
        return [(there, there, at.along_b(by)) for by in range(1, bs)]

    def wide(at):
        there = cut(out, (at.c * xs + at.x) * bs * zs * rows, bs * zs * rows)
        return [(there, there, at.along_x(by)) for by in range(1, xs)]

    def core(at):
        there = cut(out, at.c * xs * bs * zs * rows, xs * bs * zs * rows)
        return [(there, there, at.core(1))]

    for copies in (deep, cross, wide, core):
        lane.add(copies)


def bands_lane(lane, whole, lead, out):
    bs = lane.plan[1]
    rows, width = out.shape[2:]
    own = out.shape[1]

    def copies(at):
        made = []
        for by in range(bs):
            there = lax.rem(at.b + by, bs)
            for i in range(own):
                src = cut(whole, lead + (i * bs + there) * rows, rows)
                made.append((src, out.at[at.b, i], at.along_b(by) if by else None))
        return made

    lane.add(copies)


def link_plan():
    pairs = lax.axis_size("img") // 2
    xs = 2 if pairs % 2 == 0 else 1
    return xs, lax.axis_size("band"), pairs // xs


def padded_rows(rows):
    xs, bs, zs = link_plan()
    return -(-rows // (64 * xs * bs * zs)) * (64 * xs * bs * zs)


def held_shapes(plan, rows):
    xs, bs, zs = plan
    quarter = rows // 4
    sizes = [
        rows // 2,
        rows // 2,
        (xs - 1) * quarter // xs,
        (bs - 1) * quarter // bs,
        (bs - 1) * quarter // (xs * bs),
        (xs - 1) * quarter // (xs * bs),
        (zs - 1) * 2 * quarter // (xs * bs * zs),
    ]
    return [pltpu.VMEM((max(n, 16), 128), BF16) for n in sizes]


def sems_shapes(plan, lanes, moved=0):
    xs, bs, zs = plan
    count = lanes * (1 + 2 * (xs - 1 + bs - 1) + 2 * (zs - 1)) + moved
    return [
        pltpu.SemaphoreType.DMA((count,)),
        pltpu.SemaphoreType.DMA((count,)),
        pltpu.SemaphoreType.DMA((2 * lanes + moved + 1,)),
    ]


class Links:
    def __init__(self, jobs):
        self.jobs = jobs
        self.plan = link_plan()
        xs, bs, zs = self.plan
        self.devices = 2 * xs * bs * zs
        self.arrays = [job[1] for job in jobs]
        self.shapes, self.scratch = [], []
        for job in jobs:
            if job[0] == "scatter":
                rows = job[1].shape[0] // self.devices
                self.scratch += held_shapes(self.plan, job[1].shape[0])
            else:
                rows = job[2]
            self.shapes.append(jax.ShapeDtypeStruct((rows, 128), BF16))
        if jobs:
            self.scratch += sems_shapes(self.plan, len(jobs))
        self.specs = [pl.BlockSpec(memory_space=pl.ANY)] * len(jobs)

    def host(self, kernel, ins, outs, scratch):
        if not self.jobs:
            return kernel

        def run(*refs):
            count = len(self.jobs)
            a, b, c = ins, ins + count, ins + count + outs
            d, e = c + count, c + count + scratch
            step = pl.program_id(0)
            self.carry(step, refs[a:b], refs[c:d], refs[e:])
            kernel(*refs[:a], *refs[b:c], *refs[d:e])

        return run

    def carry(self, step, given, made, scratch):
        sems = Sems(*scratch[-3:])
        held = list(scratch[:-3])
        parts = {}
        for job, ref, out in zip(self.jobs, given, made):
            lane = Lane(self.plan, sems)
            if job[0] == "scatter":
                scatter_lane(lane, ref, held[:7], out)
                held = held[7:]
            else:
                rows = ref.shape[0] // 2
                collect_lane(
                    lane, lambda at, ref=ref, rows=rows: [cut(ref, k * rows, rows) for k in range(2)], out
                )
            assert len(job[-1]) == len(lane.steps) + 1
            for part, when in enumerate(job[-1]):
                parts.setdefault(when, []).append((lane, part))
        for when in sorted(parts):

            @pl.when(step == when)
            def _(when=when):
                if when == 0:
                    Places(self.plan).greet()
                for lane, part in parts[when]:
                    lane.part(part)

    def params(self, number):
        if not self.jobs:
            return pltpu.CompilerParams(vmem_limit_bytes=VMEM_BYTES)
        return pltpu.CompilerParams(
            vmem_limit_bytes=VMEM_BYTES, collective_id=number, has_side_effects=True
        )


def fold(v, op):
    return op(v.reshape(v.shape[0] // 8, 8, v.shape[1]), axis=0)


def unroll_bias(rows, bias):
    pairs, keys, lanes = bias.shape
    grid_cols = QBLOCK // 4
    key_rows = keys // grid_cols
    lane = lax.broadcasted_iota(jnp.int32, (grid_cols, QBLOCK), 1)
    even = lax.rem(lane // grid_cols, 2) == 0
    for pair in range(pairs):
        for head in range(2):
            for key_row in range(key_rows):
                turned = [
                    pltpu.roll(
                        jnp.broadcast_to(
                            rows[pl.ds(((pair * 2 + head) * 2 + odd) * key_rows + key_row, 1), :],
                            (grid_cols, QBLOCK),
                        ),
                        0,
                        1,
                        stride=1,
                        stride_axis=0,
                    )
                    for odd in range(2)
                ]
                bias[
                    pair,
                    key_row * grid_cols : (key_row + 1) * grid_cols,
                    head * QBLOCK : (head + 1) * QBLOCK,
                ] = jnp.where(even, turned[0], turned[1])


def gather_bias(grads):
    pairs, keys, lanes = grads.shape
    grid_cols = QBLOCK // 4
    lane = lax.broadcasted_iota(jnp.int32, (keys, QBLOCK), 1)
    column = lax.rem(lax.broadcasted_iota(jnp.int32, (keys, QBLOCK), 0), grid_cols)
    parity = lax.rem(lane // grid_cols, 2)
    sums = []
    for pair in range(pairs):
        for head in range(2):
            for odd in range(2):
                v = grads[pair, :, head * QBLOCK : (head + 1) * QBLOCK]
                v = jnp.where(parity == odd, v, 0.0)
                for bit in (1, 2, 4, 8, 16):
                    turned = pltpu.roll(v, QBLOCK - bit, 1)
                    v = jnp.where(lax.rem(column // bit, 2) == 1, turned, v)
                sums.append(jnp.sum(v.reshape(keys // grid_cols, grid_cols, QBLOCK), axis=1))
    return jnp.concatenate(sums, axis=0)


def forward_kernel(
    pairs,
    x_new,
    x_old,
    tproj,
    mask,
    bias_rows,
    gain1,
    shift1,
    wqkv,
    wo,
    bo,
    gain2,
    shift2,
    w1,
    b1,
    w2,
    b2,
    qkv_out,
    p_out,
    o_out,
    mid_out,
    act_out,
    slope_out,
    x_out,
    bias,
    q_ring,
    k_ring,
    vt_ring,
    o_ring,
    s_scr,
):
    step = pl.program_id(0)
    width = x_new.shape[1]

    @pl.when(step == 0)
    def _():
        unroll_bias(bias_rows, bias)
        q_ring[...] = jnp.zeros_like(q_ring)
        k_ring[...] = jnp.zeros_like(k_ring)
        vt_ring[...] = jnp.zeros_like(vt_ring)
        o_ring[...] = jnp.zeros_like(o_ring)

    attended = o_ring[...]
    mid = x_old[...].astype(F32) + (dot(attended, wo[...]) + bo[...])
    mid_out[...] = mid
    xh2, _ = norm_stats(mid)
    c = (xh2 * gain2[...] + shift2[...]).astype(BF16)
    parts = 2 * pairs
    tile = w1.shape[1] // parts

    def feed(part):
        cols = slice(part * tile, (part + 1) * tile)
        whole = dot(c, w1[:, cols])
        for low in range(0, CHUNK, 64):
            u = whole[low : low + 64] + b1[:, cols]
            u2 = u * u
            t = jnp.tanh(u * (GELU_A + GELU_B * u2))
            h = 0.5 + 0.5 * t
            e = u * h
            act_out[low : low + 64, cols] = e.astype(BF16)
            slope_out[low : low + 64, cols] = (
                h + (e * (1.0 - t)) * (GELU_A + (3.0 * GELU_B) * u2)
            ).astype(BF16)

    queries = q_ring[...]
    xh1, _ = norm_stats(x_new[...].astype(F32))
    a = (xh1 * gain1[...] + shift1[...]).astype(BF16)
    qkv = (dot(a, wqkv[...]) + tproj[0]).astype(BF16)
    qkv_out[...] = qkv
    q_ring[...] = qkv[:, :width] * jnp.asarray(0.125, BF16)
    k_ring[:HALO, :] = k_ring[CHUNK : CHUNK + HALO, :]
    k_ring[HALO : HALO + CHUNK, :] = k_ring[HALO + CHUNK :, :]
    k_ring[HALO + CHUNK :, :] = qkv[:, width : 2 * width]
    vt_ring[:, :HALO] = vt_ring[:, CHUNK : CHUNK + HALO]
    vt_ring[:, HALO : HALO + CHUNK] = vt_ring[:, HALO + CHUNK :]
    vt_ring[:, HALO + CHUNK :] = qkv[:, 2 * width :].T

    key_index = lax.broadcasted_iota(jnp.int32, (KWIN, QBLOCK), 0)
    query_index = lax.broadcasted_iota(jnp.int32, (KWIN, QBLOCK), 1)
    diagonal = key_index == query_index + HALO
    extras = []
    for blk in range(CHUNK // QBLOCK):
        line = mask[0, :, blk * QBLOCK : blk * QBLOCK + KWIN]
        column = jnp.broadcast_to(line, (QBLOCK, KWIN)).T
        extras.append(jnp.where(diagonal, 0.0, column))
    todo = [(blk, pair) for blk in range(CHUNK // QBLOCK) for pair in range(pairs)]
    cells = [(k * 128, h * 128) for k in range(KWIN // 128) for h in range(2)]
    tops = {}

    def score(blk, pair):
        low = blk * QBLOCK
        feat = slice(pair * 128, (pair + 1) * 128)
        split_q = split_heads(queries[low : low + QBLOCK, feat])
        best = [None, None]
        for k in range(0, KWIN, 128):
            s = dot_nt(k_ring[low + k : low + k + 128, feat], split_q)
            for h in range(2):
                lane = slice(h * 128, h * 128 + 128)
                v = s[:, lane] + bias[pair, k : k + 128, lane] + extras[blk][k : k + 128]
                s_scr[blk, pair, k : k + 128, lane] = v
                top = fold(v, jnp.max)
                best[h] = top if best[h] is None else jnp.maximum(best[h], top)
        tops[blk, pair] = [jnp.max(v, axis=0, keepdims=True) for v in best]

    def soften(blk, pair):
        sums = [None, None]
        for k, lane in cells:
            at = (blk, pair, slice(k, k + 128), slice(lane, lane + 128))
            h = lane // 128
            ex = jnp.exp(s_scr[at] - tops[blk, pair][h])
            total = fold(ex, jnp.sum)
            sums[h] = total if sums[h] is None else sums[h] + total
            s_scr[at] = ex
        inverse = [1.0 / jnp.sum(v, axis=0, keepdims=True) for v in sums]
        for k, lane in cells:
            at = (blk, pair, slice(k, k + 128), slice(lane, lane + 128))
            p_out[at] = (s_scr[at] * inverse[lane // 128]).astype(BF16)

    def attend(blk, pair):
        low = blk * QBLOCK
        feat = slice(pair * 128, (pair + 1) * 128)
        o = join_heads(dot(vt_ring[feat, low : low + KWIN], p_out[blk, pair])).astype(BF16)
        o_ring[low : low + QBLOCK, feat] = o
        o_out[low : low + QBLOCK, feat] = o

    for i in range(len(todo) + 2):
        if i < len(todo):
            score(*todo[i])
            feed(i)
        if 1 <= i <= len(todo):
            soften(*todo[i - 1])
        if i >= 2:
            attend(*todo[i - 2])
    x_out[...] = (mid_out[...] + (dot(act_out[...], w2[...]) + b2[...])).astype(x_out.dtype)


def const_spec(shape):
    zeros = (0,) * len(shape)
    return pl.BlockSpec(shape, lambda g: zeros, pipeline_mode=pl.Buffered(1))


def forward_layer(x, x_lead, chunks, chunks_per_image, tproj, mask, bias_rows, weights, out_dtype):
    width = x.shape[1]
    hidden = weights[7].shape[1]
    pairs = width // 128
    steps = chunks + 2

    def at(lead, least=0):
        def index(g):
            return jnp.clip(g - lead, least, chunks - 1)

        return index

    new_at, attn_at, old_at = at(0), at(1), at(2)
    row = pl.BlockSpec((CHUNK, width), lambda g: (g, 0))
    wide = pl.BlockSpec((CHUNK, hidden), lambda g: (g, 0))
    rows = steps * CHUNK
    gain1, shift1, wqkv, wo, bo, gain2, shift2, w1, b1, w2, b2 = weights
    consts = [gain1, shift1, wqkv, wo, bo, gain2, shift2, w1, b1, w2, b2]
    return pl.pallas_call(
        functools.partial(forward_kernel, pairs),
        grid=(steps,),
        in_specs=[
            pl.BlockSpec((CHUNK, width), lambda g: (new_at(g) + x_lead, 0)),
            pl.BlockSpec((CHUNK, width), lambda g: (old_at(g) + x_lead, 0)),
            pl.BlockSpec((1, 1, 3 * width), lambda g: (new_at(g) // chunks_per_image, 0, 0)),
            pl.BlockSpec((1, 1, CHUNK + 2 * HALO), lambda g: (attn_at(g), 0, 0)),
            const_spec(bias_rows.shape),
        ]
        + [const_spec(w.shape) for w in consts],
        out_specs=[
            pl.BlockSpec((CHUNK, 3 * width), lambda g: (new_at(g), 0)),
            pl.BlockSpec((CHUNK // QBLOCK, pairs, KWIN, 2 * QBLOCK), lambda g: (g, 0, 0, 0)),
            pl.BlockSpec((CHUNK, width), lambda g: (g + 1, 0)),
            row,
            wide,
            wide,
            row,
        ],
        out_shape=[
            jax.ShapeDtypeStruct((chunks * CHUNK, 3 * width), BF16),
            jax.ShapeDtypeStruct((steps * (CHUNK // QBLOCK), pairs, KWIN, 2 * QBLOCK), BF16),
            jax.ShapeDtypeStruct((rows + CHUNK, width), BF16),
            jax.ShapeDtypeStruct((rows, width), F32),
            jax.ShapeDtypeStruct((rows, hidden), BF16),
            jax.ShapeDtypeStruct((rows, hidden), BF16),
            jax.ShapeDtypeStruct((rows, width), out_dtype),
        ],
        scratch_shapes=[
            pltpu.VMEM((pairs, KWIN, 2 * QBLOCK), F32),
            pltpu.VMEM((CHUNK, width), BF16),
            pltpu.VMEM((HALO + 2 * CHUNK, width), BF16),
            pltpu.VMEM((width, HALO + 2 * CHUNK), BF16),
            pltpu.VMEM((CHUNK, width), BF16),
            pltpu.VMEM((CHUNK // QBLOCK, pairs, KWIN, 2 * QBLOCK), F32),
        ],
        compiler_params=pltpu.CompilerParams(vmem_limit_bytes=VMEM_BYTES),
        name="block_forward",
    )(x, x, tproj, mask, bias_rows, *consts)


def put_tiles(out, first, acc):
    width = acc.shape[0]
    for j in range(acc.shape[1] // 128):
        at = (first + j) * width
        out[at : at + width, :] = acc[:, j * 128 : (j + 1) * 128].astype(out.dtype)


def put_rows(out, at, vectors):
    lines = [v[:, j : j + 128] for v in vectors for j in range(0, v.shape[1], 128)]
    lines += [jnp.zeros((1, 128), F32)] * (-len(lines) % 16)
    out[at : at + len(lines), :] = jnp.concatenate(lines, axis=0).astype(out.dtype)


def feed_back_kernel(
    gx,
    mid,
    act,
    slope,
    o,
    gain2,
    shift2,
    w1,
    w2,
    wo,
    gmid_out,
    go_out,
    grads_out,
    gw2t,
    gw1,
    gwo,
    sums,
    gb1,
    gu_scr,
):
    step = pl.program_id(0)

    @pl.when(step == 0)
    def _():
        for ref in (gw2t, gw1, gwo, sums, gb1):
            ref[...] = jnp.zeros_like(ref)

    grad = gx[...].astype(F32)
    gr = grad.astype(BF16)
    gr_t = gr.T
    xh, inverse = norm_stats(mid[...])
    c_t = (xh * gain2[...] + shift2[...]).astype(BF16).T
    hidden = act.shape[1]
    tile = 256
    for low in range(0, hidden, tile):
        cols = slice(low, low + tile)
        ge = dot_nt(gr, w2[cols, :])
        gu = (ge * slope[:, cols].astype(F32)).astype(BF16)
        gu_scr[:, cols] = gu
        gb1[:, cols] += row_sums(gu.astype(F32))
        gw2t[:, cols] += dot(gr_t, act[:, cols])
        gw1[:, cols] += dot(c_t, gu)
    gc = dot_nt(gu_scr[...], w1[...])
    gmid = grad + norm_back(gc, xh, inverse, gain2[...])
    gmid_out[...] = gmid
    gb = gmid.astype(BF16)
    gwo[...] += dot(o[...].T, gb)
    go_out[...] = dot_nt(gb, wo[...]).astype(BF16)
    sums[0] += row_sums(gr.astype(F32))
    sums[1] += row_sums(gb.astype(F32))
    sums[2] += row_sums(gc * xh)
    sums[3] += row_sums(gc)

    @pl.when(step == pl.num_programs(0) - 1)
    def _():
        tiles = hidden // 128
        put_tiles(grads_out, 0, gw2t)
        put_tiles(grads_out, tiles, gw1)
        put_tiles(grads_out, 2 * tiles, gwo)
        whole = [jnp.sum(sums[i], axis=0, keepdims=True) for i in range(4)]
        whole.append(jnp.sum(gb1[...], axis=0, keepdims=True))
        at = (2 * tiles + gwo.shape[1] // 128) * gwo.shape[0]
        put_rows(grads_out, at, whole)
        used = sum(feed_rows(gwo.shape[0], hidden))
        spare = grads_out.shape[0] - used
        if spare:
            grads_out[used:, :] = jnp.zeros((spare, 128), grads_out.dtype)


def feed_rows(width, hidden):
    tiles = (2 * hidden + width) // 128
    return tiles * width, -(-(4 * width + hidden) // 128 // 16) * 16


def feed_back(gx, gx_lead, patches, mid, act, slope, o, gain2, shift2, w1, w2, wo, links, number):
    width = mid.shape[1]
    hidden = act.shape[1]

    def rows(cols, lead):
        return pl.BlockSpec((FEED, cols), lambda g: (g + lead, 0))

    grad_rows = padded_rows(sum(feed_rows(width, hidden)))
    return pl.pallas_call(
        links.host(feed_back_kernel, 10, 3, 6),
        grid=(patches // FEED,),
        in_specs=[
            rows(width, gx_lead),
            rows(width, 1),
            rows(hidden, 1),
            rows(hidden, 1),
            rows(width, 1),
        ]
        + [const_spec(w.shape) for w in (gain2, shift2, w1, w2, wo)]
        + links.specs,
        out_specs=[rows(width, 0), rows(width, 0), const_spec((grad_rows, 128))] + links.specs,
        out_shape=[
            jax.ShapeDtypeStruct((patches, width), F32),
            jax.ShapeDtypeStruct((patches, width), BF16),
            jax.ShapeDtypeStruct((grad_rows, 128), BF16),
        ]
        + links.shapes,
        scratch_shapes=[
            pltpu.VMEM((width, hidden), F32),
            pltpu.VMEM((width, hidden), F32),
            pltpu.VMEM((width, width), F32),
            pltpu.VMEM((4, 8, width), F32),
            pltpu.VMEM((8, hidden), F32),
            pltpu.VMEM((FEED, hidden), BF16),
        ]
        + links.scratch,
        compiler_params=links.params(number),
        name="feed_back",
    )(gx, mid, act, slope, o, gain2, shift2, w1, w2, wo, *links.arrays)


def attend_back_kernel(
    pairs,
    chunks,
    chunks_per_image,
    prev,
    cur,
    nxt,
    p_in,
    go_in,
    o_in,
    gmid,
    x,
    gain1,
    shift1,
    wqkv,
    gx_out,
    gtime,
    grads_out,
    gwqkv,
    gbias,
    sums,
    gq_ring,
    gkv_ring,
    gs_scr,
):
    step = pl.program_id(0)
    width = x.shape[1]

    @pl.when(step == 0)
    def _():
        for ref in (gwqkv, gbias, gtime, sums, gq_ring, gkv_ring):
            ref[...] = jnp.zeros_like(ref)

    gq_old = gq_ring[...]
    live = (step < chunks).astype(BF16)
    go = go_in[...] * live
    qkv = cur[...]
    queries = qkv[:, :width] * jnp.asarray(0.125, BF16)
    keys = jnp.concatenate(
        [prev[:, width : 2 * width], qkv[:, width : 2 * width], nxt[:, width : 2 * width]], axis=0
    )
    keys_t = keys.T
    values = jnp.concatenate([prev[:, 2 * width :], qkv[:, 2 * width :], nxt[:, 2 * width :]], axis=0)
    dots = (go.astype(F32) * o_in[...].astype(F32)).T
    blocks = CHUNK // QBLOCK
    todo = [(blk, pair) for pair in range(pairs) for blk in range(blocks)]

    def spread(blk, pair):
        low = blk * QBLOCK
        feat = slice(pair * 128, (pair + 1) * 128)
        split_go = split_heads(go[low : low + QBLOCK, feat])
        own = dots[feat, low : low + QBLOCK]
        row_dot = [jnp.sum(own[h * 64 : h * 64 + 64], axis=0, keepdims=True) for h in range(2)]
        for k in range(0, KWIN, 128):
            gp = dot_nt(values[low + k : low + k + 128, feat], split_go)
            for h in range(2):
                lane = slice(h * 128, h * 128 + 128)
                gs = p_in[blk, pair, k : k + 128, lane].astype(F32) * (gp[:, lane] - row_dot[h])
                gbias[pair, k : k + 128, lane] += gs
                gs_scr[blk, pair, k : k + 128, lane] = gs.astype(BF16)

    def pull(blk, pair):
        low = blk * QBLOCK
        feat = slice(pair * 128, (pair + 1) * 128)
        vfeat = slice(width + pair * 128, width + (pair + 1) * 128)
        gs = gs_scr[blk, pair]
        at = HALO + low
        gkv_ring[at : at + KWIN, feat] += dot(gs, split_heads(queries[low : low + QBLOCK, feat]))
        gkv_ring[at : at + KWIN, vfeat] += dot(
            p_in[blk, pair], split_heads(go[low : low + QBLOCK, feat])
        )
        gq = join_heads(dot(keys_t[feat, low : low + KWIN], gs)) * 0.125
        gq_ring[low : low + QBLOCK, feat] = gq.astype(BF16)

    for i in range(len(todo) + 1):
        if i < len(todo):
            spread(*todo[i])
        if i >= 1:
            pull(*todo[i - 1])

    done = jnp.concatenate([gq_old, gkv_ring[:CHUNK, :].astype(BF16)], axis=1)
    gkv_ring[:CHUNK, :] = gkv_ring[CHUNK : 2 * CHUNK, :]
    gkv_ring[CHUNK : CHUNK + HALO, :] = gkv_ring[2 * CHUNK :, :]
    gkv_ring[CHUNK + HALO :, :] = jnp.zeros((CHUNK, 2 * width), F32)
    xh, inverse = norm_stats(x[...].astype(F32))
    a = (xh * gain1[...] + shift1[...]).astype(BF16)
    gwqkv[...] += dot(a.T, done)
    ga = dot_nt(done, wqkv[...])
    gx_out[...] = (gmid[...] + norm_back(ga, xh, inverse, gain1[...])).astype(gx_out.dtype)
    sums[0] += row_sums(ga * xh)
    sums[1] += row_sums(ga)
    first = lax.rem(step + chunks_per_image - 1, chunks_per_image) == 0
    before = jnp.where(first, jnp.zeros(gtime.shape[1:], F32), gtime[0])
    summed = row_sums(done.astype(F32))
    gtime[0] = before + jnp.concatenate([summed[:, :width], summed[:, 2 * width :]], axis=1)

    @pl.when(step == chunks)
    def _():
        put_tiles(grads_out, 0, gwqkv)
        tiles = gwqkv.shape[1] // 128
        lines = attend_rows(width)[2]
        grads_out[tiles * width : tiles * width + lines, :] = gather_bias(gbias).astype(BF16)
        put_rows(
            grads_out,
            tiles * width + lines,
            [jnp.sum(sums[i], axis=0, keepdims=True) for i in range(2)],
        )
        used = attend_rows(width)[1]
        spare = grads_out.shape[0] - used
        if spare:
            grads_out[used:, :] = jnp.zeros((spare, 128), grads_out.dtype)


def attend_rows(width):
    lines = 2 * (width // 128) * (KWIN * 4 // QBLOCK) * 2
    small = -(-2 * width // 128 // 16) * 16
    return 3 * width // 128 * width, 3 * width // 128 * width + lines + small, lines


def attend_back(
    qkv,
    p,
    go,
    o,
    gmid,
    x,
    x_lead,
    chunks,
    chunks_per_image,
    gain1,
    shift1,
    wqkv,
    out_dtype,
    links,
    number,
):
    width = x.shape[1]
    pairs = width // 128
    steps = chunks + 1
    halves = CHUNK // HALO

    def now(g):
        return jnp.minimum(g, chunks - 1)

    def late(g):
        return jnp.maximum(g - 1, 0)

    def rows(cols, lead, index):
        return pl.BlockSpec((CHUNK, cols), lambda g: (index(g) + lead, 0))

    images = chunks // chunks_per_image
    grad_rows = padded_rows(attend_rows(width)[1])
    kernel = functools.partial(attend_back_kernel, pairs, chunks, chunks_per_image)
    return pl.pallas_call(
        links.host(kernel, 11, 3, 6),
        grid=(steps,),
        in_specs=[
            pl.BlockSpec((HALO, 3 * width), lambda g: (jnp.maximum(halves * now(g) - 1, 0), 0)),
            rows(3 * width, 0, now),
            pl.BlockSpec(
                (HALO, 3 * width),
                lambda g: (jnp.minimum(halves * (now(g) + 1), halves * chunks - 1), 0),
            ),
            pl.BlockSpec(
                (CHUNK // QBLOCK, pairs, KWIN, 2 * QBLOCK), lambda g: (now(g) + 1, 0, 0, 0)
            ),
            rows(width, 0, now),
            rows(width, 2, now),
            rows(width, 0, late),
            rows(width, x_lead, late),
        ]
        + [const_spec(w.shape) for w in (gain1, shift1, wqkv)]
        + links.specs,
        out_specs=[
            rows(width, 1, lambda g: g),
            pl.BlockSpec((1, 8, 2 * width), lambda g: (late(g) // chunks_per_image, 0, 0)),
            const_spec((grad_rows, 128)),
        ]
        + links.specs,
        out_shape=[
            jax.ShapeDtypeStruct(((steps + 1) * CHUNK, width), out_dtype),
            jax.ShapeDtypeStruct((images, 8, 2 * width), F32),
            jax.ShapeDtypeStruct((grad_rows, 128), BF16),
        ]
        + links.shapes,
        scratch_shapes=[
            pltpu.VMEM((width, 3 * width), F32),
            pltpu.VMEM((pairs, KWIN, 2 * QBLOCK), F32),
            pltpu.VMEM((2, 8, width), F32),
            pltpu.VMEM((CHUNK, width), BF16),
            pltpu.VMEM((2 * CHUNK + HALO, 2 * width), F32),
            pltpu.VMEM((CHUNK // QBLOCK, pairs, KWIN, 2 * QBLOCK), BF16),
        ]
        + links.scratch,
        compiler_params=links.params(number),
        name="attend_back",
    )(qkv, qkv, qkv, p, go, o, gmid, x, gain1, shift1, wqkv, *links.arrays)


def final_kernel(plan, lead, *refs):
    chunk, grad, extra, whole = refs[:4]
    feed_out, attend_out, extra_out, bands_out = refs[4:8]
    scratch = refs[8:]
    sems = Sems(*scratch[-3:])
    Places(plan).greet()
    lanes = [Lane(plan, sems) for _ in range(3)]
    rows = chunk.shape[0] // 2
    ends = scatter_lane(lanes[0], grad, scratch[:-3])
    collect_lane(lanes[0], ends, attend_out)
    collect_lane(lanes[1], lambda at: [cut(chunk, k * rows, rows) for k in range(2)], feed_out)
    extra_lane(lanes[2], extra, extra_out)
    late = Lane(plan, sems)
    bands_lane(late, whole, lead, bands_out)
    late.part(0)
    for i in range(max(len(lane.steps) for lane in lanes) + 1):
        for lane in lanes:
            if i <= len(lane.steps):
                lane.part(i)
    late.part(1)


def final_exchange(chunk, feed_rows_all, grad, extra, whole, lead, own, part):
    plan = link_plan()
    xs, bs, zs = plan
    anywhere = pl.BlockSpec(memory_space=pl.ANY)
    return pl.pallas_call(
        functools.partial(final_kernel, plan, lead),
        in_specs=[anywhere] * 4,
        out_specs=[anywhere] * 4,
        out_shape=[
            jax.ShapeDtypeStruct((feed_rows_all, 128), BF16),
            jax.ShapeDtypeStruct(grad.shape, BF16),
            jax.ShapeDtypeStruct((2 * xs * bs * zs * extra.shape[0], 128), BF16),
            jax.ShapeDtypeStruct((bs, own, part, whole.shape[1]), BF16),
        ],
        scratch_shapes=held_shapes(plan, grad.shape[0]) + sems_shapes(plan, 4, bs * own),
        compiler_params=pltpu.CompilerParams(
            vmem_limit_bytes=VMEM_BYTES, collective_id=0, has_side_effects=True
        ),
        name="final_exchange",
    )(chunk, grad, extra, whole)


def unpack_kernel(layers, *refs):
    ins = [refs[4 * i : 4 * i + 4] for i in range(layers)]
    w2_out, w1_out, attend_out, wo_out = refs[4 * layers :]
    width = w1_out.shape[1]
    for layer, (w2t, w1, attend, wo) in enumerate(ins):
        for j in range(w1.shape[0] // width):
            rows = slice(j * width, (j + 1) * width)
            cols = slice(j * 128, (j + 1) * 128)
            w2_out[layer, cols, :] = w2t[rows, :].astype(F32).T
            w1_out[layer, :, cols] = w1[rows, :].astype(F32)
            attend_out[layer, :, cols] = attend[rows, :].astype(F32)
            wo_out[layer, :, cols] = wo[rows, :].astype(F32)


def unpack(fulls, width, hidden):
    layers = len(fulls)
    wide = width // 128
    steps = hidden // width
    rows = wide * width
    last = 3 * width // width - 1
    block = (rows, 128)

    def spec(first, top):
        return pl.BlockSpec(block, lambda g: (first + jnp.minimum(g, top), 0))

    ins = [
        spec(0, steps),
        spec(steps, steps),
        spec(0, last),
        spec(2 * steps, 0),
    ]
    return pl.pallas_call(
        functools.partial(unpack_kernel, layers),
        grid=(steps,),
        in_specs=ins * layers,
        out_specs=[
            pl.BlockSpec((layers, width, width), lambda g: (0, g, 0)),
            pl.BlockSpec((layers, width, width), lambda g: (0, 0, g)),
            pl.BlockSpec((layers, width, width), lambda g: (0, 0, jnp.minimum(g, last))),
            pl.BlockSpec((layers, width, width), lambda g: (0, 0, 0)),
        ],
        out_shape=[
            jax.ShapeDtypeStruct((layers, hidden, width), F32),
            jax.ShapeDtypeStruct((layers, width, hidden), F32),
            jax.ShapeDtypeStruct((layers, width, 3 * width), F32),
            jax.ShapeDtypeStruct((layers, width, width), F32),
        ],
        compiler_params=pltpu.CompilerParams(vmem_limit_bytes=VMEM_BYTES),
        name="unpack",
    )(*[ref for feed, attend in fulls for ref in (feed, feed, attend, feed)])


def time_embedding(timesteps, width):
    half_width = width // 2
    frequency = jnp.exp(
        jnp.arange(half_width, dtype=jnp.int32).astype(F32) * (-math.log(10000.0) / half_width)
    )
    angles = timesteps.astype(F32)[:, None] * frequency[None, :]
    return jnp.concatenate([jnp.sin(angles), jnp.cos(angles)], axis=-1)


def bias_rows(table, index_table, grid_cols):
    heads, entries = table.shape
    span = 2 * WIN + 1
    offsets = 2 * grid_cols - 1
    turned = index_table.reshape(span, offsets)[:, ::-1].reshape(entries)
    select = (turned[None, :] == jnp.arange(entries, dtype=jnp.int32)[:, None]).astype(F32)
    rows = jnp.dot(table, select, precision=EXACT).reshape(heads, span, offsets)
    key_rows = KWIN // grid_cols
    a0, a1, a2, a3 = [
        jnp.pad(
            rows, ((0, 0), (q, key_rows - span - q), (0, 0)), constant_values=NEG_FILL
        )
        for q in range(QBLOCK // grid_cols)
    ]
    gap = jnp.full((heads, key_rows, 1), NEG_FILL, F32)
    even = jnp.concatenate(
        [a0[..., grid_cols - 1 :], gap, a2, gap, a0[..., : grid_cols - 1]], axis=-1
    )
    odd = jnp.concatenate([gap, a1, gap, a3], axis=-1)
    return jnp.stack([even, odd], axis=1)


def spaced(parts, steps):
    return [i * (steps - 1) // (parts - 1) for i in range(parts)]


def body(
    tokens,
    cotangent,
    valid_mask,
    timesteps,
    index_table,
    first_gain,
    first_shift,
    attend_weight,
    time_weight,
    offset_bias,
    output_weight,
    output_bias,
    second_gain,
    second_shift,
    expand_weight,
    expand_bias,
    reduce_weight,
    reduce_bias,
):
    images, band_rows, grid_cols, width = tokens.shape
    layers = attend_weight.shape[0]
    bands = lax.axis_size("band")
    me = lax.axis_index("band")
    own = images // bands
    part = band_rows * grid_cols
    patches = bands * part
    per_image = patches // CHUNK
    chunks = own * per_image

    def to_images(shard):
        shard = shard.reshape(bands, own, part, width)
        whole = jnp.zeros((own, bands, part, width), shard.dtype)
        for by in range(bands):
            piece = lax.dynamic_index_in_dim(shard, (me + by) % bands, 0, keepdims=False)
            if by:
                pairs = [(i, (i + by) % bands) for i in range(bands)]
                piece = lax.ppermute(piece, "band", pairs)
            whole = lax.dynamic_update_index_in_dim(whole, piece, (me - by) % bands, 1)
        return whole.reshape(own * patches, width)

    def to_bands(whole):
        whole = whole.reshape(own, bands, part, width)
        shard = jnp.zeros((bands, own, part, width), whole.dtype)
        for by in range(bands):
            piece = lax.dynamic_index_in_dim(whole, (me + by) % bands, 1, keepdims=False)
            if by:
                pairs = [(i, (i + by) % bands) for i in range(bands)]
                piece = lax.ppermute(piece, "band", pairs)
            shard = lax.dynamic_update_index_in_dim(shard, piece, (me - by) % bands, 0)
        return shard.reshape(images, band_rows, grid_cols, width)

    x0 = to_images(tokens)
    x0, late = lax.optimization_barrier((x0, cotangent))
    cot = to_images(late)

    mine = lax.dynamic_slice_in_dim(valid_mask, me * own, own, 0).reshape(own, patches)
    fill = jnp.where(mine == 1, 0.0, NEG_FILL).astype(F32)
    fill = jnp.pad(fill, ((0, 0), (HALO, HALO)), constant_values=NEG_FILL)
    mask = jnp.stack(
        [fill[:, c * CHUNK : (c + 1) * CHUNK + 2 * HALO] for c in range(per_image)], axis=1
    ).reshape(chunks, 1, CHUNK + 2 * HALO)

    time_low = time_embedding(
        lax.dynamic_slice_in_dim(timesteps, me * own, own, 0), width
    ).astype(BF16)
    heads, entries = offset_bias.shape[1:]

    def make_rows(table):
        return bias_rows(table, index_table, grid_cols)

    biases, bias_pull = jax.vjp(make_rows, offset_bias.reshape(layers * heads, entries))
    biases = biases.reshape(layers, -1, QBLOCK)

    def row(v):
        return v.reshape(1, -1)

    x, x_lead = x0, 0
    kept = []
    for layer in range(layers):
        tp = jnp.dot(time_low, time_weight[layer], preferred_element_type=F32)
        tproj = jnp.concatenate([tp[:, :width], jnp.zeros_like(tp[:, :width]), tp[:, width:]], axis=1)
        weights = (
            row(first_gain[layer]),
            row(first_shift[layer]),
            attend_weight[layer],
            output_weight[layer],
            row(output_bias[layer]),
            row(second_gain[layer]),
            row(second_shift[layer]),
            expand_weight[layer],
            row(expand_bias[layer]),
            reduce_weight[layer],
            row(reduce_bias[layer]),
        )
        qkv, p, o, mid, act, slope, nxt = forward_layer(
            x,
            x_lead,
            chunks,
            per_image,
            tproj[:, None, :],
            mask,
            biases[layer],
            weights,
            F32 if layer < layers - 1 else BF16,
        )
        kept.append((x, x_lead, qkv, p, o, mid, act, slope))
        x, x_lead = nxt, 2
    output = to_bands(x[x_lead * CHUNK :])

    gx, gx_lead = cot, 0
    devices = bands * lax.axis_size("img")
    feed_big = feed_rows(width, expand_weight.shape[2])[0]
    attend_big, _, lines = attend_rows(width)
    fulls = [[None, None] for _ in range(layers)]
    extra = [time_low]
    feed_part = attend_grads = None
    for layer in reversed(range(layers)):
        x, x_lead, qkv, p, o, mid, act, slope = kept[layer]
        later = layer + 1 < layers
        jobs = []
        if later:
            steps = own * patches // FEED
            jobs = [
                ("collect", feed_part, feed_count, spaced(5, steps)),
                ("scatter", attend_grads, spaced(6, steps)),
            ]
        gmid, go, feed_grads, *sent = feed_back(
            gx,
            gx_lead,
            own * patches,
            mid,
            act,
            slope,
            o,
            row(second_gain[layer]),
            row(second_shift[layer]),
            expand_weight[layer],
            reduce_weight[layer],
            output_weight[layer],
            Links(jobs),
            1 + 2 * layer,
        )
        feed_count = feed_grads.shape[0]
        jobs = [("scatter", feed_grads, spaced(6, chunks + 1))]
        if later:
            fulls[layer + 1][0], attend_part = sent
            jobs.append(("collect", attend_part, attend_grads.shape[0], spaced(5, chunks + 1)))
        if layer == layers - 1:
            gmid, output = lax.optimization_barrier((gmid, output))
        gx, gtime, attend_grads, feed_part, *sent = attend_back(
            qkv,
            p,
            go,
            o,
            gmid,
            x,
            x_lead,
            chunks,
            per_image,
            row(first_gain[layer]),
            row(first_shift[layer]),
            attend_weight[layer],
            F32 if layer else BF16,
            Links(jobs),
            2 + 2 * layer,
        )
        if later:
            fulls[layer + 1][1] = sent[0]
        gx_lead = 1
        extra.append(jnp.sum(gtime, axis=1).astype(BF16))

    extra = jnp.concatenate(extra, axis=1).reshape(-1, 128)
    lead = extra.shape[0]
    extra = jnp.pad(extra, ((0, -lead % 16), (0, 0)))
    fulls[0][0], fulls[0][1], gathered, input_grad = final_exchange(
        feed_part, feed_count, attend_grads, extra, gx, 2 * CHUNK, own, part
    )
    input_grad = input_grad.reshape(tokens.shape)
    gathered = gathered.reshape(devices, -1, 128)[:, :lead].reshape(devices * own, -1)
    grad_time = jnp.stack(
        [
            lax.dot_general(
                gathered[:, :width],
                gathered[:, width * (1 + 2 * turn) : width * (3 + 2 * turn)],
                (((0,), (0,)), ((), ())),
                preferred_element_type=F32,
            )
            for turn in reversed(range(layers))
        ]
    )
    grad_reduce, grad_expand, grad_attend, grad_output = unpack(fulls, width, expand_weight.shape[2])
    feed_small = jnp.stack([full[0][feed_big : feed_big + 32] for full in fulls]).astype(F32)
    attend_small = jnp.stack([full[1][attend_big : attend_big + lines + 16] for full in fulls])
    attend_small = attend_small.astype(F32)
    each = width // 128

    def vector(small, at, count):
        return small[:, at : at + count].reshape(layers, count * 128)

    (grad_offset,) = bias_pull(attend_small[:, :lines].reshape(layers * heads, 2, -1, QBLOCK))
    return (
        output,
        input_grad,
        vector(attend_small, lines, each),
        vector(attend_small, lines + each, each),
        grad_attend,
        grad_time,
        grad_offset.reshape(layers, heads, entries),
        grad_output,
        vector(feed_small, each, each),
        vector(feed_small, 2 * each, each),
        vector(feed_small, 3 * each, each),
        grad_expand,
        vector(feed_small, 4 * each, expand_weight.shape[2] // 128),
        grad_reduce,
        vector(feed_small, 0, each),
    )


def solution(mesh):
    split = P("img", "band", None, None)
    placed = (split, split, P("img", None, None), P("img")) + (P(),) * 14
    return jax.shard_map(
        body,
        mesh=mesh,
        in_specs=placed,
        out_specs=(split, split) + (P(),) * 13,
        check_vma=False,
    )
```

```python
import functools
import math

import jax
import jax.numpy as jnp
from jax import lax
from jax.experimental import pallas as pl
from jax.experimental.pallas import tpu as pltpu
from jax.sharding import PartitionSpec as P

WIN = 4
CHUNK = 256
QBLOCK = 128
KWIN = 384
HALO = 128
FEED = 512

EXACT = lax.Precision.HIGHEST
NEG_FILL = -1000000000.0
EPSILON = 1e-06
GELU_A = math.sqrt(2.0 / math.pi)
GELU_B = 0.044715 * GELU_A
VMEM_BYTES = 58 * 1024 * 1024

F32 = jnp.float32
BF16 = jnp.bfloat16


def dot(a, b):
    return jnp.dot(a, b, preferred_element_type=F32)


def dot_nt(a, b):
    return lax.dot_general(a, b, (((1,), (1,)), ((), ())), preferred_element_type=F32)


def norm_stats(v):
    mean = jnp.mean(v, axis=-1, keepdims=True)
    centered = v - mean
    inverse = lax.rsqrt(jnp.mean(centered * centered, axis=-1, keepdims=True) + EPSILON)
    return centered * inverse, inverse


def norm_back(gy, xh, inverse, gain):
    gs = gy * gain
    return inverse * (
        gs - jnp.mean(gs, axis=-1, keepdims=True) - xh * jnp.mean(gs * xh, axis=-1, keepdims=True)
    )


def row_sums(v):
    rows, cols = v.shape
    return jnp.sum(v.reshape(rows // 8, 8, cols), axis=0)


def split_heads(block):
    lane = lax.broadcasted_iota(jnp.int32, block.shape, 1)
    zero = jnp.zeros_like(block)
    first = lane < block.shape[1] // 2
    return jnp.concatenate(
        [jnp.where(first, block, zero), jnp.where(first, zero, block)], axis=0
    )


def join_heads(product):
    half = product.shape[0] // 2
    width = product.shape[1] // 2
    return jnp.concatenate([product[:half, :width], product[half:, width:]], axis=0).T


def share_rows(rows):
    return max(n for n in range(16, 257, 16) if rows % n == 0)


def add_rows(total, at, others, rows):
    share = share_rows(rows)

    def one(i, carry):
        low = pl.multiple_of(i * share, 16)
        here = pl.ds(pl.multiple_of(at + low, 16), share)
        v = total[here, :].astype(F32)
        for ref, row in others:
            v = v + ref[pl.ds(pl.multiple_of(row + low, 16), share), :].astype(F32)
        total[here, :] = v.astype(total.dtype)
        return carry

    lax.fori_loop(0, rows // share, one, 0)


def cut(ref, at, rows):
    return ref.at[pl.ds(pl.multiple_of(at, 16), rows), :]


def both(first, second):
    first()
    second()


def dispatch(step, acts):
    whens = sorted(acts)
    if len(whens) <= 1:
        for when in whens:
            pl.when(step == when)(acts[when])
        return
    middle = whens[len(whens) // 2]
    low = {when: acts[when] for when in whens if when < middle}
    high = {when: acts[when] for when in whens if when >= middle}
    pl.when(step < middle)(lambda: dispatch(step, low))
    pl.when(step >= middle)(lambda: dispatch(step, high))


def mod(v, n):
    return jnp.bitwise_and(v, n - 1) if n & (n - 1) == 0 else lax.rem(v, n)


def halved(v, n):
    return jnp.right_shift(v, n.bit_length() - 1) if n & (n - 1) == 0 else v // n


class Places:
    def __init__(self, plan):
        self.xs, self.bs, self.zs = plan
        self.img = lax.axis_index("img")
        self.b = lax.axis_index("band")
        self.c = mod(self.img, 2)
        self.x = mod(halved(self.img, 2), self.xs)
        self.z = halved(self.img, 2 * self.xs)

    def core(self, by):
        return (self.img + 1 - 2 * self.c, self.b)

    def along_x(self, by):
        return ((self.z * self.xs + mod(self.x + by, self.xs)) * 2 + self.c, self.b)

    def along_b(self, by):
        return (self.img, mod(self.b + by, self.bs))

    def along_z(self, by):
        return ((mod(self.z + by, self.zs) * self.xs + self.x) * 2 + self.c, self.b)

    def greet(self):
        barrier = pltpu.get_barrier_semaphore()
        peers = [self.core(1)]
        peers += [self.along_x(by) for by in range(1, self.xs)]
        peers += [self.along_b(by) for by in range(1, self.bs)]
        peers += [self.along_z(by) for by in range(1, self.zs)]
        for peer in peers:
            pl.semaphore_signal(barrier, inc=1, device_id=peer, device_id_type=pl.DeviceIdType.MESH)
        pl.semaphore_wait(barrier, len(peers))


class Lane:
    def __init__(self, plan, sems):
        self.plan, self.sems, self.steps = plan, sems, []

    def add(self, copies, then=None):
        count = [0, 0]
        here = Places(self.plan)
        for src, dst, peer in copies(here):
            count[peer is None] += 1
        base = (self.sems.sent, self.sems.kept)
        self.sems.sent += count[0]
        self.sems.kept += count[1]
        self.steps.append((copies, then, base))

    def described(self, step):
        copies, _, (sent, kept) = self.steps[step]
        made = []
        for src, dst, peer in copies(Places(self.plan)):
            if peer is None:
                made.append(pltpu.make_async_copy(src, dst, self.sems.own.at[kept]))
                kept += 1
            else:
                made.append(
                    pltpu.make_async_remote_copy(
                        src_ref=src,
                        dst_ref=dst,
                        send_sem=self.sems.send.at[sent],
                        recv_sem=self.sems.recv.at[sent],
                        device_id=peer,
                        device_id_type=pl.DeviceIdType.MESH,
                    )
                )
                sent += 1
        return made

    def part(self, i):
        if i > 0:
            for copy in self.described(i - 1):
                copy.wait()
            if self.steps[i - 1][1] is not None:
                self.steps[i - 1][1](Places(self.plan))
        if i < len(self.steps):
            for copy in self.described(i):
                copy.start()


class Sems:
    def __init__(self, send, recv, own):
        self.send, self.recv, self.own = send, recv, own
        self.sent = self.kept = 0


def scatter_lane(lane, grad, held, chunk=None):
    acc, r1, r2a, r2b, r3a, r3b, r4 = held
    xs, bs, zs = lane.plan
    half = grad.shape[0] // 2
    quarter = half // 2
    nx, nb, n2 = quarter // xs, quarter // bs, quarter // (xs * bs)
    n = n2 // zs

    def core_copies(at):
        return [
            (cut(grad, at.c * half, half), acc, None),
            (cut(grad, half - at.c * half, half), r1, at.core(1)),
        ]

    lane.add(core_copies, lambda at: add_rows(acc, 0, [(r1, 0)], half))

    def wide_copies(at):
        made = []
        for by in range(1, xs):
            there = mod(at.x + by, xs)
            made.append((cut(acc, there * nx, nx), cut(r2a, (by - 1) * nx, nx), at.along_x(by)))
        for by in range(1, bs):
            there = quarter + mod(at.b + by, bs) * nb
            made.append((cut(acc, there, nb), cut(r2b, (by - 1) * nb, nb), at.along_b(by)))
        return made

    def wide_add(at):
        add_rows(acc, at.x * nx, [(r2a, k * nx) for k in range(xs - 1)], nx)
        add_rows(acc, quarter + at.b * nb, [(r2b, k * nb) for k in range(bs - 1)], nb)

    lane.add(wide_copies, wide_add)

    def cross_copies(at):
        made = []
        for by in range(1, bs):
            there = at.x * nx + mod(at.b + by, bs) * n2
            made.append((cut(acc, there, n2), cut(r3a, (by - 1) * n2, n2), at.along_b(by)))
        for by in range(1, xs):
            there = quarter + at.b * nb + mod(at.x + by, xs) * n2
            made.append((cut(acc, there, n2), cut(r3b, (by - 1) * n2, n2), at.along_x(by)))
        return made

    def plane(at):
        return at.x * nx + at.b * n2, quarter + at.b * nb + at.x * n2

    def cross_add(at):
        first, second = plane(at)
        add_rows(acc, first, [(r3a, k * n2) for k in range(bs - 1)], n2)
        add_rows(acc, second, [(r3b, k * n2) for k in range(xs - 1)], n2)

    lane.add(cross_copies, cross_add)

    def deep_copies(at):
        made = []
        for by in range(1, zs):
            there = mod(at.z + by, zs) * n
            for k, low in enumerate(plane(at)):
                slot = (2 * (by - 1) + k) * n
                made.append((cut(acc, low + there, n), cut(r4, slot, n), at.along_z(by)))
        return made

    def deep_add(at):
        for k, low in enumerate(plane(at)):
            add_rows(acc, low + at.z * n, [(r4, (2 * i + k) * n) for i in range(zs - 1)], n)

    lane.add(deep_copies, deep_add)

    def ends(at):
        return [cut(acc, low + at.z * n, n) for low in plane(at)]

    if chunk is None:
        return ends
    lane.add(lambda at: [(ref, cut(chunk, k * n, n), None) for k, ref in enumerate(ends(at))])


def collect_lane(lane, ends, out):
    xs, bs, zs = lane.plan
    half = out.shape[0] // 2
    quarter = half // 2
    nx, nb, n2 = quarter // xs, quarter // bs, quarter // (xs * bs)
    n = n2 // zs

    def plane(at):
        base = at.c * half
        return base + at.x * nx + at.b * n2, base + quarter + at.b * nb + at.x * n2

    def deep(at):
        made = []
        for ref, low in zip(ends(at), plane(at)):
            there = cut(out, low + at.z * n, n)
            made.append((ref, there, None))
            made += [(ref, there, at.along_z(by)) for by in range(1, zs)]
        return made

    def cross(at):
        first, second = plane(at)
        a, b = cut(out, first, n2), cut(out, second, n2)
        made = [(a, a, at.along_b(by)) for by in range(1, bs)]
        return made + [(b, b, at.along_x(by)) for by in range(1, xs)]

    def wide(at):
        a = cut(out, at.c * half + at.x * nx, nx)
        b = cut(out, at.c * half + quarter + at.b * nb, nb)
        made = [(a, a, at.along_x(by)) for by in range(1, xs)]
        return made + [(b, b, at.along_b(by)) for by in range(1, bs)]

    def core(at):
        whole = cut(out, at.c * half, half)
        return [(whole, whole, at.core(1))]

    for copies in (deep, cross, wide, core):
        lane.add(copies)


def extra_lane(lane, extra, out):
    xs, bs, zs = lane.plan
    rows = extra.shape[0]

    def deep(at):
        there = cut(out, (((at.c * xs + at.x) * bs + at.b) * zs + at.z) * rows, rows)
        return [(extra, there, None)] + [(extra, there, at.along_z(by)) for by in range(1, zs)]

    def cross(at):
        there = cut(out, ((at.c * xs + at.x) * bs + at.b) * zs * rows, zs * rows)
        return [(there, there, at.along_b(by)) for by in range(1, bs)]

    def wide(at):
        there = cut(out, (at.c * xs + at.x) * bs * zs * rows, bs * zs * rows)
        return [(there, there, at.along_x(by)) for by in range(1, xs)]

    def core(at):
        there = cut(out, at.c * xs * bs * zs * rows, xs * bs * zs * rows)
        return [(there, there, at.core(1))]

    for copies in (deep, cross, wide, core):
        lane.add(copies)


def link_plan():
    pairs = lax.axis_size("img") // 2
    xs = 2 if pairs % 2 == 0 else 1
    return xs, lax.axis_size("band"), pairs // xs


def padded_rows(rows):
    xs, bs, zs = link_plan()
    return -(-rows // (64 * xs * bs * zs)) * (64 * xs * bs * zs)


def held_shapes(plan, rows):
    xs, bs, zs = plan
    quarter = rows // 4
    sizes = [
        rows // 2,
        rows // 2,
        (xs - 1) * quarter // xs,
        (bs - 1) * quarter // bs,
        (bs - 1) * quarter // (xs * bs),
        (xs - 1) * quarter // (xs * bs),
        (zs - 1) * 2 * quarter // (xs * bs * zs),
    ]
    return [pltpu.VMEM((max(n, 16), 128), BF16) for n in sizes]


def sems_shapes(plan, lanes, moved=0):
    xs, bs, zs = plan
    count = lanes * (1 + 2 * (xs - 1 + bs - 1) + 2 * (zs - 1)) + moved
    return [
        pltpu.SemaphoreType.DMA((count,)),
        pltpu.SemaphoreType.DMA((count,)),
        pltpu.SemaphoreType.DMA((2 * lanes + moved + 1,)),
    ]


def images_copies(shard, at, own, part, images):
    made = []
    for by in range(at.bs):
        there = mod(at.b + by, at.bs)
        for i in images:
            made.append(((there * own + i) * part, (i * at.bs + at.b) * part, by))
    return made


class Links:
    def __init__(self, jobs):
        self.jobs = jobs
        self.plan = link_plan()
        xs, bs, zs = self.plan
        self.arrays = [job[1] for job in jobs]
        self.shapes, self.scratch = [], []
        remote = local = 0
        for job in jobs:
            if job[0] == "sum":
                for _, rows in self.runs(job):
                    self.scratch += held_shapes(self.plan, rows)
                    remote += 2 * (1 + 2 * (xs - 1 + bs - 1) + 2 * (zs - 1))
                    local += 3
                self.shapes.append(jax.ShapeDtypeStruct(job[1].shape, BF16))
                continue
            width = job[1].shape[1]
            own, part = job[2][-2:]
            shape = (bs, own, part, width) if job[0] == "bands" else (own * bs * part, width)
            self.shapes.append(jax.ShapeDtypeStruct(shape, BF16))
            self.scratch.append(pltpu.VMEM((own, part, width), BF16))
            remote += (bs - 1) * own
            local += 2 * own
        if jobs:
            self.scratch += [
                pltpu.SemaphoreType.DMA((max(remote, 1),)),
                pltpu.SemaphoreType.DMA((max(remote, 1),)),
                pltpu.SemaphoreType.DMA((local,)),
            ]
        self.specs = [pl.BlockSpec(memory_space=pl.ANY)] * len(jobs)

    def runs(self, job):
        unit = padded_rows(1)
        units = job[1].shape[0] // unit
        lanes = min(len(job[-1]), units)
        ends = [units * i // lanes * unit for i in range(lanes + 1)]
        return [(low, high - low) for low, high in zip(ends, ends[1:])]

    def host(self, kernel, ins, outs, scratch):
        def run(*refs):
            count = len(self.jobs)
            a, b, c = ins, ins + count, ins + count + outs
            d, e = c + count, c + count + scratch
            step = pl.program_id(0)
            acts = kernel(*refs[:a], *refs[b:c], *refs[d:e]) or {}
            if self.jobs:
                parts = self.parts(refs[a:b], refs[c:d], refs[e:])
                parts.setdefault(0, [])
                for when in sorted(parts):

                    def act(when=when):
                        if when == 0:
                            Places(self.plan).greet()
                        for lane, part in parts[when]:
                            lane.part(part)

                    at = min(when, pl.num_programs(0) - 1)
                    before = acts.get(at)
                    acts[at] = act if before is None else functools.partial(both, before, act)
            dispatch(step, acts)

        return run

    def parts(self, given, made, scratch):
        sems = Sems(*scratch[-3:])
        held = list(scratch[:-3])
        parts = {}
        lanes = []
        for job, ref, out in zip(self.jobs, given, made):
            if job[0] == "sum":
                for (low, rows), whens in zip(self.runs(job), job[-1]):
                    lane = Lane(self.plan, sems)
                    part_in, part_out = ref.at[pl.ds(low, rows), :], out.at[pl.ds(low, rows), :]
                    collect_lane(lane, scatter_lane(lane, part_in, held[:7]), part_out)
                    held = held[7:]
                    lanes.append((lane, whens))
                continue
            own, part = job[2][-2:]
            lead = job[2][0] if job[0] == "bands" else 0

            def copies(at, kind=job[0], ref=ref, out=out, own=own, part=part, lead=lead):
                made = []
                for i in range(own):
                    for by in range(self.plan[1]):
                        there = mod(at.b + by, self.plan[1])
                        if kind == "bands":
                            src = cut(ref, lead + (i * self.plan[1] + there) * part, part)
                            dst = out.at[at.b, i]
                        else:
                            src = cut(ref, (there * own + i) * part, part)
                            dst = cut(out, (i * self.plan[1] + at.b) * part, part)
                        made.append((i, src, dst, at.along_b(by) if by else None))
                return made

            lane = Lane(self.plan, sems)
            lane.add(lambda at, f=copies: [c[1:] for c in f(at) if c[3] is not None])
            lanes.append((lane, [job[-1][0], job[-1][-1]]))
            lane = Lane(self.plan, sems)
            here = held[0]
            held = held[1:]
            lane.add(lambda at, f=copies, h=here: [(c[1], h.at[c[0]], None) for c in f(at) if c[3] is None])
            lane.add(lambda at, f=copies, h=here: [(h.at[c[0]], c[2], None) for c in f(at) if c[3] is None])
            lanes.append((lane, job[-1]))
        for lane, whens in lanes:
            assert len(whens) == len(lane.steps) + 1
            for part, when in enumerate(whens):
                parts.setdefault(when, []).append((lane, part))
        return parts

    def params(self, number):
        if not self.jobs:
            return pltpu.CompilerParams(vmem_limit_bytes=VMEM_BYTES)
        return pltpu.CompilerParams(
            vmem_limit_bytes=VMEM_BYTES, collective_id=number, has_side_effects=True
        )


def fold(v, op):
    return op(v.reshape(v.shape[0] // 8, 8, v.shape[1]), axis=0)


def unroll_bias(rows, bias):
    pairs, keys, lanes = bias.shape
    grid_cols = QBLOCK // 4
    key_rows = keys // grid_cols
    lane = lax.broadcasted_iota(jnp.int32, (grid_cols, QBLOCK), 1)
    even = lax.rem(lane // grid_cols, 2) == 0
    for pair in range(pairs):
        for head in range(2):
            for key_row in range(key_rows):
                turned = [
                    pltpu.roll(
                        jnp.broadcast_to(
                            rows[pl.ds(((pair * 2 + head) * 2 + odd) * key_rows + key_row, 1), :],
                            (grid_cols, QBLOCK),
                        ),
                        0,
                        1,
                        stride=1,
                        stride_axis=0,
                    )
                    for odd in range(2)
                ]
                bias[
                    pair,
                    key_row * grid_cols : (key_row + 1) * grid_cols,
                    head * QBLOCK : (head + 1) * QBLOCK,
                ] = jnp.where(even, turned[0], turned[1])


def gather_bias(grads):
    pairs, keys, lanes = grads.shape
    grid_cols = QBLOCK // 4
    lane = lax.broadcasted_iota(jnp.int32, (keys, QBLOCK), 1)
    column = lax.rem(lax.broadcasted_iota(jnp.int32, (keys, QBLOCK), 0), grid_cols)
    parity = lax.rem(lane // grid_cols, 2)
    sums = []
    for pair in range(pairs):
        for head in range(2):
            for odd in range(2):
                v = grads[pair, :, head * QBLOCK : (head + 1) * QBLOCK]
                v = jnp.where(parity == odd, v, 0.0)
                for bit in (1, 2, 4, 8, 16):
                    turned = pltpu.roll(v, QBLOCK - bit, 1)
                    v = jnp.where(lax.rem(column // bit, 2) == 1, turned, v)
                sums.append(jnp.sum(v.reshape(keys // grid_cols, grid_cols, QBLOCK), axis=1))
    return jnp.concatenate(sums, axis=0)


def forward_kernel(
    pairs,
    x_new,
    x_old,
    tproj,
    mask,
    bias_rows,
    gain1,
    shift1,
    wqkv,
    wo,
    bo,
    gain2,
    shift2,
    w1,
    b1,
    w2,
    b2,
    qkv_out,
    p_out,
    o_out,
    mid_out,
    act_out,
    slope_out,
    x_out,
    bias,
    q_ring,
    k_ring,
    vt_ring,
    o_ring,
    s_scr,
):
    step = pl.program_id(0)
    width = x_new.shape[1]

    @pl.when(step == 0)
    def _():
        unroll_bias(bias_rows, bias)
        q_ring[...] = jnp.zeros_like(q_ring)
        k_ring[...] = jnp.zeros_like(k_ring)
        vt_ring[...] = jnp.zeros_like(vt_ring)
        o_ring[...] = jnp.zeros_like(o_ring)

    attended = o_ring[...]
    mid = x_old[...].astype(F32) + (dot(attended, wo[...]) + bo[...])
    mid_out[...] = mid
    xh2, _ = norm_stats(mid)
    c = (xh2 * gain2[...] + shift2[...]).astype(BF16)
    parts = 2 * pairs
    tile = w1.shape[1] // parts

    def feed(part):
        cols = slice(part * tile, (part + 1) * tile)
        whole = dot(c, w1[:, cols])
        for low in range(0, CHUNK, 64):
            u = whole[low : low + 64] + b1[:, cols]
            u2 = u * u
            t = jnp.tanh(u * (GELU_A + GELU_B * u2))
            h = 0.5 + 0.5 * t
            e = u * h
            act_out[low : low + 64, cols] = e.astype(BF16)
            slope_out[low : low + 64, cols] = (
                h + (e * (1.0 - t)) * (GELU_A + (3.0 * GELU_B) * u2)
            ).astype(BF16)

    queries = q_ring[...]
    xh1, _ = norm_stats(x_new[...].astype(F32))
    a = (xh1 * gain1[...] + shift1[...]).astype(BF16)
    qkv = (dot(a, wqkv[...]) + tproj[0]).astype(BF16)
    qkv_out[...] = qkv
    q_ring[...] = qkv[:, :width] * jnp.asarray(0.125, BF16)
    k_ring[:HALO, :] = k_ring[CHUNK : CHUNK + HALO, :]
    k_ring[HALO : HALO + CHUNK, :] = k_ring[HALO + CHUNK :, :]
    k_ring[HALO + CHUNK :, :] = qkv[:, width : 2 * width]
    vt_ring[:, :HALO] = vt_ring[:, CHUNK : CHUNK + HALO]
    vt_ring[:, HALO : HALO + CHUNK] = vt_ring[:, HALO + CHUNK :]
    vt_ring[:, HALO + CHUNK :] = qkv[:, 2 * width :].T

    key_index = lax.broadcasted_iota(jnp.int32, (KWIN, QBLOCK), 0)
    query_index = lax.broadcasted_iota(jnp.int32, (KWIN, QBLOCK), 1)
    diagonal = key_index == query_index + HALO
    extras = []
    for blk in range(CHUNK // QBLOCK):
        line = mask[0, :, blk * QBLOCK : blk * QBLOCK + KWIN]
        column = jnp.broadcast_to(line, (QBLOCK, KWIN)).T
        extras.append(jnp.where(diagonal, 0.0, column))
    todo = [(blk, pair) for blk in range(CHUNK // QBLOCK) for pair in range(pairs)]
    cells = [(k * 128, h * 128) for k in range(KWIN // 128) for h in range(2)]
    tops = {}

    def score(blk, pair):
        low = blk * QBLOCK
        feat = slice(pair * 128, (pair + 1) * 128)
        split_q = split_heads(queries[low : low + QBLOCK, feat])
        best = [None, None]
        for k in range(0, KWIN, 128):
            s = dot_nt(k_ring[low + k : low + k + 128, feat], split_q)
            for h in range(2):
                lane = slice(h * 128, h * 128 + 128)
                v = s[:, lane] + bias[pair, k : k + 128, lane] + extras[blk][k : k + 128]
                s_scr[blk, pair, k : k + 128, lane] = v
                top = fold(v, jnp.max)
                best[h] = top if best[h] is None else jnp.maximum(best[h], top)
        tops[blk, pair] = [jnp.max(v, axis=0, keepdims=True) for v in best]

    def soften(blk, pair):
        sums = [None, None]
        for k, lane in cells:
            at = (blk, pair, slice(k, k + 128), slice(lane, lane + 128))
            h = lane // 128
            ex = jnp.exp(s_scr[at] - tops[blk, pair][h])
            total = fold(ex, jnp.sum)
            sums[h] = total if sums[h] is None else sums[h] + total
            s_scr[at] = ex
        inverse = [1.0 / jnp.sum(v, axis=0, keepdims=True) for v in sums]
        for k, lane in cells:
            at = (blk, pair, slice(k, k + 128), slice(lane, lane + 128))
            p_out[at] = (s_scr[at] * inverse[lane // 128]).astype(BF16)

    def attend(blk, pair):
        low = blk * QBLOCK
        feat = slice(pair * 128, (pair + 1) * 128)
        o = join_heads(dot(vt_ring[feat, low : low + KWIN], p_out[blk, pair])).astype(BF16)
        o_ring[low : low + QBLOCK, feat] = o
        o_out[low : low + QBLOCK, feat] = o

    for i in range(len(todo) + 2):
        if i < len(todo):
            score(*todo[i])
            feed(i)
        if 1 <= i <= len(todo):
            soften(*todo[i - 1])
        if i >= 2:
            attend(*todo[i - 2])
    x_out[...] = (mid_out[...] + (dot(act_out[...], w2[...]) + b2[...])).astype(x_out.dtype)


def const_spec(shape):
    zeros = (0,) * len(shape)
    return pl.BlockSpec(shape, lambda g: zeros, pipeline_mode=pl.Buffered(1))


def layer_spec(shape, layer):
    index = (layer,) + (0,) * (len(shape) - 1)
    return pl.BlockSpec((None,) + shape[1:], lambda g: index, pipeline_mode=pl.Buffered(1))


def first_forward_kernel(pairs, plan, chunks, own, part, shard, *refs):
    ins, outs, scratch = refs[:14], refs[14:22], refs[22:]
    x_all, send_sems, recv_sems, own_sems = scratch[-4:]
    step = pl.program_id(0)
    sems = Sems(send_sems, recv_sems, own_sems)
    lanes = []
    for i in range(own):
        lane = Lane(plan, sems)

        def copies(at, i=i):
            return [
                (cut(shard, src, part), cut(x_all, dst, part), at.along_b(by) if by else None)
                for src, dst, by in images_copies(shard, at, own, part, (i,))
            ]

        lane.add(copies)
        lanes.append(lane)
    for i in range(own):

        @pl.when(step == i * (chunks // own))
        def _(i=i):
            if i == 0:
                Places(plan).greet()
                for lane in lanes:
                    lane.part(0)
            lanes[i].part(1)

    def chunk(lead):
        at = jnp.clip(step - lead, 0, chunks - 1) * CHUNK
        return x_all.at[pl.ds(pl.multiple_of(at, CHUNK), CHUNK), :]

    x_copy = outs[-1]
    x_copy[...] = chunk(0)[...]
    forward_kernel(pairs, chunk(0), chunk(2), *ins, *outs[:-1], *scratch[:-4])


def forward_layer(
    x, x_lead, chunks, chunks_per_image, tproj, mask, bias_rows, layer, weights, out_dtype, links, own, part, number
):
    width = x.shape[1]
    hidden = weights[7].shape[2]
    pairs = width // 128
    steps = chunks + 2
    first = layer == 0

    def at(lead, least=0):
        def index(g):
            return jnp.clip(g - lead, least, chunks - 1)

        return index

    new_at, attn_at, old_at = at(0), at(1), at(2)
    row = pl.BlockSpec((CHUNK, width), lambda g: (g, 0))
    wide = pl.BlockSpec((CHUNK, hidden), lambda g: (g, 0))
    rows = steps * CHUNK
    if first:
        x_specs, x_args = [pl.BlockSpec(memory_space=pl.ANY)], [x]
    else:
        x_specs = [
            pl.BlockSpec((CHUNK, width), lambda g: (new_at(g) + x_lead, 0)),
            pl.BlockSpec((CHUNK, width), lambda g: (old_at(g) + x_lead, 0)),
        ]
        x_args = [x, x]
    in_specs = x_specs + [
        pl.BlockSpec((1, 1, 3 * width), lambda g: (new_at(g) // chunks_per_image, 0, 0)),
        pl.BlockSpec((1, 1, CHUNK + 2 * HALO), lambda g: (attn_at(g), 0, 0)),
        layer_spec(bias_rows.shape, layer),
    ]
    in_specs += [layer_spec(w.shape, layer) for w in weights]
    out_specs = [
        pl.BlockSpec((CHUNK, 3 * width), lambda g: (new_at(g), 0)),
        pl.BlockSpec((CHUNK // QBLOCK, pairs, KWIN, 2 * QBLOCK), lambda g: (g, 0, 0, 0)),
        pl.BlockSpec((CHUNK, width), lambda g: (g + 1, 0)),
        row,
        wide,
        wide,
        row,
    ]
    out_shape = [
        jax.ShapeDtypeStruct((chunks * CHUNK, 3 * width), BF16),
        jax.ShapeDtypeStruct((steps * (CHUNK // QBLOCK), pairs, KWIN, 2 * QBLOCK), BF16),
        jax.ShapeDtypeStruct((rows + CHUNK, width), BF16),
        jax.ShapeDtypeStruct((rows, width), F32),
        jax.ShapeDtypeStruct((rows, hidden), BF16),
        jax.ShapeDtypeStruct((rows, hidden), BF16),
        jax.ShapeDtypeStruct((rows, width), out_dtype),
    ]
    scratch = [
        pltpu.VMEM((pairs, KWIN, 2 * QBLOCK), F32),
        pltpu.VMEM((CHUNK, width), BF16),
        pltpu.VMEM((HALO + 2 * CHUNK, width), BF16),
        pltpu.VMEM((width, HALO + 2 * CHUNK), BF16),
        pltpu.VMEM((CHUNK, width), BF16),
        pltpu.VMEM((CHUNK // QBLOCK, pairs, KWIN, 2 * QBLOCK), F32),
    ]
    params = links.params(number)
    if first:
        plan = link_plan()
        remote = max((plan[1] - 1) * own, 1)
        kernel = functools.partial(first_forward_kernel, pairs, plan, chunks, own, part)
        out_specs.append(pl.BlockSpec((CHUNK, width), lambda g: (new_at(g), 0)))
        out_shape.append(jax.ShapeDtypeStruct((chunks * CHUNK, width), BF16))
        scratch += [
            pltpu.VMEM((chunks * CHUNK, width), BF16),
            pltpu.SemaphoreType.DMA((remote,)),
            pltpu.SemaphoreType.DMA((remote,)),
            pltpu.SemaphoreType.DMA((own,)),
        ]
        params = pltpu.CompilerParams(
            vmem_limit_bytes=VMEM_BYTES, collective_id=number, has_side_effects=True
        )
    else:
        kernel = links.host(
            functools.partial(forward_kernel, pairs), len(in_specs), len(out_specs), len(scratch)
        )
    return pl.pallas_call(
        kernel,
        grid=(steps,),
        in_specs=in_specs + links.specs,
        out_specs=out_specs + links.specs,
        out_shape=out_shape + links.shapes,
        scratch_shapes=scratch + links.scratch,
        compiler_params=params,
        name="block_forward",
    )(*x_args, tproj, mask, bias_rows, *weights, *links.arrays)


def put_tiles(out, first, acc):
    width = acc.shape[0]
    for j in range(acc.shape[1] // 128):
        at = (first + j) * width
        out[at : at + width, :] = acc[:, j * 128 : (j + 1) * 128].astype(out.dtype)


def put_rows(out, at, vectors):
    lines = [v[:, j : j + 128] for v in vectors for j in range(0, v.shape[1], 128)]
    lines += [jnp.zeros((1, 128), F32)] * (-len(lines) % 16)
    out[at : at + len(lines), :] = jnp.concatenate(lines, axis=0).astype(out.dtype)


def feed_back_kernel(
    gx,
    mid,
    act,
    slope,
    o,
    gain2,
    shift2,
    w1,
    w2,
    wo,
    gmid_out,
    go_out,
    grads_out,
    gw2t,
    gw1,
    gwo,
    sums,
    gb1,
    gu_scr,
):
    step = pl.program_id(0)

    @pl.when(step == 0)
    def _():
        for ref in (gw2t, gw1, gwo, sums, gb1):
            ref[...] = jnp.zeros_like(ref)

    grad = gx[...].astype(F32)
    gr = grad.astype(BF16)
    gr_t = gr.T
    xh, inverse = norm_stats(mid[...])
    c_t = (xh * gain2[...] + shift2[...]).astype(BF16).T
    hidden = act.shape[1]
    tile = 256
    for low in range(0, hidden, tile):
        cols = slice(low, low + tile)
        ge = dot_nt(gr, w2[cols, :])
        gu = (ge * slope[:, cols].astype(F32)).astype(BF16)
        gu_scr[:, cols] = gu
        gb1[:, cols] += row_sums(gu.astype(F32))
        gw2t[:, cols] += dot(gr_t, act[:, cols])
        gw1[:, cols] += dot(c_t, gu)
    gc = dot_nt(gu_scr[...], w1[...])
    gmid = grad + norm_back(gc, xh, inverse, gain2[...])
    gmid_out[...] = gmid
    gb = gmid.astype(BF16)
    gwo[...] += dot(o[...].T, gb)
    go_out[...] = dot_nt(gb, wo[...]).astype(BF16)
    sums[0] += row_sums(gr.astype(F32))
    sums[1] += row_sums(gb.astype(F32))
    sums[2] += row_sums(gc * xh)
    sums[3] += row_sums(gc)

    @pl.when(step == pl.num_programs(0) - 1)
    def _():
        tiles = hidden // 128
        put_tiles(grads_out, 0, gw2t)
        put_tiles(grads_out, tiles, gw1)
        put_tiles(grads_out, 2 * tiles, gwo)
        whole = [jnp.sum(sums[i], axis=0, keepdims=True) for i in range(4)]
        whole.append(jnp.sum(gb1[...], axis=0, keepdims=True))
        at = (2 * tiles + gwo.shape[1] // 128) * gwo.shape[0]
        put_rows(grads_out, at, whole)
        used = sum(feed_rows(gwo.shape[0], hidden))
        spare = grads_out.shape[0] - used
        if spare:
            grads_out[used:, :] = jnp.zeros((spare, 128), grads_out.dtype)


def feed_rows(width, hidden):
    tiles = (2 * hidden + width) // 128
    return tiles * width, -(-(4 * width + hidden) // 128 // 16) * 16


def feed_back(
    gx, gx_lead, patches, mid, act, slope, o, layer, gain2, shift2, w1, w2, wo, links, number
):
    width = mid.shape[1]
    hidden = act.shape[1]

    def rows(cols, lead):
        return pl.BlockSpec((FEED, cols), lambda g: (g + lead, 0))

    grad_rows = padded_rows(sum(feed_rows(width, hidden)))
    return pl.pallas_call(
        links.host(feed_back_kernel, 10, 3, 6),
        grid=(patches // FEED,),
        in_specs=[
            rows(width, gx_lead),
            rows(width, 1),
            rows(hidden, 1),
            rows(hidden, 1),
            rows(width, 1),
        ]
        + [layer_spec(w.shape, layer) for w in (gain2, shift2, w1, w2, wo)]
        + links.specs,
        out_specs=[rows(width, 0), rows(width, 0), const_spec((grad_rows, 128))] + links.specs,
        out_shape=[
            jax.ShapeDtypeStruct((patches, width), F32),
            jax.ShapeDtypeStruct((patches, width), BF16),
            jax.ShapeDtypeStruct((grad_rows, 128), BF16),
        ]
        + links.shapes,
        scratch_shapes=[
            pltpu.VMEM((width, hidden), F32),
            pltpu.VMEM((width, hidden), F32),
            pltpu.VMEM((width, width), F32),
            pltpu.VMEM((4, 8, width), F32),
            pltpu.VMEM((8, hidden), F32),
            pltpu.VMEM((FEED, hidden), BF16),
        ]
        + links.scratch,
        compiler_params=links.params(number),
        name="feed_back",
    )(gx, mid, act, slope, o, gain2, shift2, w1, w2, wo, *links.arrays)


class Pusher:
    SLOTS = 8

    def __init__(self, plan, own, part, refs):
        self.plan, self.own, self.part = plan, own, part
        self.out, self.slots, self.send, self.recv, self.local = refs
        self.piece = min(part, CHUNK)
        self.subs = part // self.piece
        self.at = Places(plan)

    def each(self, chunk, act):
        at, bs = self.at, self.plan[1]
        whole = bs * self.part
        slot = chunk % self.SLOTS
        for k in range(CHUNK // self.piece):
            row = chunk * CHUNK + k * self.piece
            image, within = divmod(row, whole)
            target, sub = within // self.part, within % self.part // self.piece
            src = self.slots.at[slot, pl.ds(k * self.piece, self.piece), :]
            dst = self.out.at[at.b, image, pl.ds(sub * self.piece, self.piece), :]
            sem = slot * (CHUNK // self.piece) + k

            @pl.when(at.b == target)
            def _():
                act(pltpu.make_async_copy(src, dst, self.local.at[sem]), False)

            @pl.when(at.b != target)
            def _():
                by = mod(target - at.b + bs, bs)
                copy = pltpu.make_async_remote_copy(
                    src_ref=src,
                    dst_ref=dst,
                    send_sem=self.send.at[sem],
                    recv_sem=self.recv.at[((by - 1) * self.own + image) * self.subs + sub],
                    device_id=(at.img, target),
                    device_id_type=pl.DeviceIdType.MESH,
                )
                act(copy, True)

    def start(self, chunk):
        self.each(chunk, lambda copy, remote: copy.start())

    def sent(self, chunk):
        self.each(chunk, lambda copy, remote: copy.wait_send() if remote else copy.wait())

    def received(self):
        at, bs = self.at, self.plan[1]
        for by in range(1, bs):
            sender = mod(at.b - by + bs, bs)
            for image in range(self.own):
                for sub in range(self.subs):
                    pltpu.make_async_remote_copy(
                        src_ref=self.slots.at[0, pl.ds(0, self.piece), :],
                        dst_ref=self.out.at[sender, image, pl.ds(sub * self.piece, self.piece), :],
                        send_sem=self.send.at[0],
                        recv_sem=self.recv.at[((by - 1) * self.own + image) * self.subs + sub],
                        device_id=(at.img, sender),
                        device_id_type=pl.DeviceIdType.MESH,
                    ).wait_recv()


def last_attend_back_kernel(pairs, chunks, chunks_per_image, plan, own, part, *refs):
    ins, outs, scratch = refs[:11], refs[11:14], refs[14:]
    out, slots = outs[0], scratch[6]
    step = pl.program_id(0)
    pusher = Pusher(plan, own, part, (out, slots, *scratch[7:]))

    slot = slots.at[mod(step + Pusher.SLOTS - 1, Pusher.SLOTS)]
    attend_back_kernel(pairs, chunks, chunks_per_image, *ins, slot, *outs[1:], *scratch[:6])
    acts = {}
    for chunk in range(chunks):

        def act(chunk=chunk):
            pusher.start(chunk)
            if 0 <= chunk + 1 - Pusher.SLOTS and chunk < chunks - 1:
                pusher.sent(chunk + 1 - Pusher.SLOTS)
            if chunk == chunks - 1:
                for old in range(max(chunks - Pusher.SLOTS, 0), chunks):
                    pusher.sent(old)
                pusher.received()

        acts[chunk + 1] = act
    return acts


def attend_back_kernel(
    pairs,
    chunks,
    chunks_per_image,
    prev,
    cur,
    nxt,
    p_in,
    go_in,
    o_in,
    gmid,
    x,
    gain1,
    shift1,
    wqkv,
    gx_out,
    gtime,
    grads_out,
    gwqkv,
    gbias,
    sums,
    gq_ring,
    gkv_ring,
    gs_scr,
):
    step = pl.program_id(0)
    width = x.shape[1]

    @pl.when(step == 0)
    def _():
        for ref in (gwqkv, gbias, gtime, sums, gq_ring, gkv_ring):
            ref[...] = jnp.zeros_like(ref)

    gq_old = gq_ring[...]
    live = (step < chunks).astype(BF16)
    go = go_in[...] * live
    qkv = cur[...]
    queries = qkv[:, :width] * jnp.asarray(0.125, BF16)
    keys = jnp.concatenate(
        [prev[:, width : 2 * width], qkv[:, width : 2 * width], nxt[:, width : 2 * width]], axis=0
    )
    keys_t = keys.T
    values = jnp.concatenate([prev[:, 2 * width :], qkv[:, 2 * width :], nxt[:, 2 * width :]], axis=0)
    dots = (go.astype(F32) * o_in[...].astype(F32)).T
    blocks = CHUNK // QBLOCK
    todo = [(blk, pair) for pair in range(pairs) for blk in range(blocks)]

    def spread(blk, pair):
        low = blk * QBLOCK
        feat = slice(pair * 128, (pair + 1) * 128)
        split_go = split_heads(go[low : low + QBLOCK, feat])
        own = dots[feat, low : low + QBLOCK]
        row_dot = [jnp.sum(own[h * 64 : h * 64 + 64], axis=0, keepdims=True) for h in range(2)]
        for k in range(0, KWIN, 128):
            gp = dot_nt(values[low + k : low + k + 128, feat], split_go)
            for h in range(2):
                lane = slice(h * 128, h * 128 + 128)
                gs = p_in[blk, pair, k : k + 128, lane].astype(F32) * (gp[:, lane] - row_dot[h])
                gbias[pair, k : k + 128, lane] += gs
                gs_scr[blk, pair, k : k + 128, lane] = gs.astype(BF16)

    def pull(blk, pair):
        low = blk * QBLOCK
        feat = slice(pair * 128, (pair + 1) * 128)
        vfeat = slice(width + pair * 128, width + (pair + 1) * 128)
        gs = gs_scr[blk, pair]
        at = HALO + low
        gkv_ring[at : at + KWIN, feat] += dot(gs, split_heads(queries[low : low + QBLOCK, feat]))
        gkv_ring[at : at + KWIN, vfeat] += dot(
            p_in[blk, pair], split_heads(go[low : low + QBLOCK, feat])
        )
        gq = join_heads(dot(keys_t[feat, low : low + KWIN], gs)) * 0.125
        gq_ring[low : low + QBLOCK, feat] = gq.astype(BF16)

    for i in range(len(todo) + 1):
        if i < len(todo):
            spread(*todo[i])
        if i >= 1:
            pull(*todo[i - 1])

    done = jnp.concatenate([gq_old, gkv_ring[:CHUNK, :].astype(BF16)], axis=1)
    gkv_ring[:CHUNK, :] = gkv_ring[CHUNK : 2 * CHUNK, :]
    gkv_ring[CHUNK : CHUNK + HALO, :] = gkv_ring[2 * CHUNK :, :]
    gkv_ring[CHUNK + HALO :, :] = jnp.zeros((CHUNK, 2 * width), F32)
    xh, inverse = norm_stats(x[...].astype(F32))
    a = (xh * gain1[...] + shift1[...]).astype(BF16)
    gwqkv[...] += dot(a.T, done)
    ga = dot_nt(done, wqkv[...])
    gx_out[...] = (gmid[...] + norm_back(ga, xh, inverse, gain1[...])).astype(gx_out.dtype)
    sums[0] += row_sums(ga * xh)
    sums[1] += row_sums(ga)
    first = lax.rem(step + chunks_per_image - 1, chunks_per_image) == 0
    before = jnp.where(first, jnp.zeros(gtime.shape[1:], F32), gtime[0])
    summed = row_sums(done.astype(F32))
    gtime[0] = before + jnp.concatenate([summed[:, :width], summed[:, 2 * width :]], axis=1)

    @pl.when(step == chunks)
    def _():
        put_tiles(grads_out, 0, gwqkv)
        tiles = gwqkv.shape[1] // 128
        lines = attend_rows(width)[2]
        grads_out[tiles * width : tiles * width + lines, :] = gather_bias(gbias).astype(BF16)
        put_rows(
            grads_out,
            tiles * width + lines,
            [jnp.sum(sums[i], axis=0, keepdims=True) for i in range(2)],
        )
        used = attend_rows(width)[1]
        spare = grads_out.shape[0] - used
        if spare:
            grads_out[used:, :] = jnp.zeros((spare, 128), grads_out.dtype)


def attend_rows(width):
    lines = 2 * (width // 128) * (KWIN * 4 // QBLOCK) * 2
    small = -(-2 * width // 128 // 16) * 16
    return 3 * width // 128 * width, 3 * width // 128 * width + lines + small, lines


def attend_back(
    qkv,
    p,
    go,
    o,
    gmid,
    x,
    x_lead,
    chunks,
    chunks_per_image,
    layer,
    gain1,
    shift1,
    wqkv,
    own,
    part,
    links,
    number,
):
    width = x.shape[1]
    pairs = width // 128
    steps = chunks + 1
    halves = CHUNK // HALO

    def now(g):
        return jnp.minimum(g, chunks - 1)

    def late(g):
        return jnp.maximum(g - 1, 0)

    def rows(cols, lead, index):
        return pl.BlockSpec((CHUNK, cols), lambda g: (index(g) + lead, 0))

    images = chunks // chunks_per_image
    grad_rows = padded_rows(attend_rows(width)[1])
    in_specs = [
        pl.BlockSpec((HALO, 3 * width), lambda g: (jnp.maximum(halves * now(g) - 1, 0), 0)),
        rows(3 * width, 0, now),
        pl.BlockSpec(
            (HALO, 3 * width),
            lambda g: (jnp.minimum(halves * (now(g) + 1), halves * chunks - 1), 0),
        ),
        pl.BlockSpec((CHUNK // QBLOCK, pairs, KWIN, 2 * QBLOCK), lambda g: (now(g) + 1, 0, 0, 0)),
        rows(width, 0, now),
        rows(width, 2, now),
        rows(width, 0, late),
        rows(width, x_lead, late),
    ]
    in_specs += [layer_spec(w.shape, layer) for w in (gain1, shift1, wqkv)]
    out_specs = [
        rows(width, 1, lambda g: g),
        pl.BlockSpec((1, 8, 2 * width), lambda g: (late(g) // chunks_per_image, 0, 0)),
        const_spec((grad_rows, 128)),
    ]
    out_shape = [
        jax.ShapeDtypeStruct(((steps + 1) * CHUNK, width), F32),
        jax.ShapeDtypeStruct((images, 8, 2 * width), F32),
        jax.ShapeDtypeStruct((grad_rows, 128), BF16),
    ]
    scratch = [
        pltpu.VMEM((width, 3 * width), F32),
        pltpu.VMEM((pairs, KWIN, 2 * QBLOCK), F32),
        pltpu.VMEM((2, 8, width), F32),
        pltpu.VMEM((CHUNK, width), BF16),
        pltpu.VMEM((2 * CHUNK + HALO, 2 * width), F32),
        pltpu.VMEM((CHUNK // QBLOCK, pairs, KWIN, 2 * QBLOCK), BF16),
    ]
    kernel = functools.partial(attend_back_kernel, pairs, chunks, chunks_per_image)
    if layer == 0:
        plan = link_plan()
        bs = plan[1]
        piece = min(part, CHUNK)
        pieces = CHUNK // piece
        kernel = functools.partial(
            last_attend_back_kernel, pairs, chunks, chunks_per_image, plan, own, part
        )
        out_specs[0] = pl.BlockSpec(memory_space=pl.ANY)
        out_shape[0] = jax.ShapeDtypeStruct((bs, own, part, width), BF16)
        scratch += [
            pltpu.VMEM((Pusher.SLOTS, CHUNK, width), BF16),
            pltpu.SemaphoreType.DMA((Pusher.SLOTS * pieces,)),
            pltpu.SemaphoreType.DMA((max((bs - 1) * own * (part // piece), 1),)),
            pltpu.SemaphoreType.DMA((Pusher.SLOTS * pieces,)),
        ]
    return pl.pallas_call(
        links.host(kernel, len(in_specs), len(out_specs), len(scratch)),
        grid=(steps,),
        in_specs=in_specs + links.specs,
        out_specs=out_specs + links.specs,
        out_shape=out_shape + links.shapes,
        scratch_shapes=scratch + links.scratch,
        compiler_params=links.params(number),
        name="attend_back",
    )(qkv, qkv, qkv, p, go, o, gmid, x, gain1, shift1, wqkv, *links.arrays)


def final_kernel(plan, *refs):
    grad, extra = refs[:2]
    attend_out, extra_out = refs[2:4]
    scratch = refs[4:]
    sems = Sems(*scratch[-3:])
    Places(plan).greet()
    lanes = [Lane(plan, sems) for _ in range(2)]
    collect_lane(lanes[0], scatter_lane(lanes[0], grad, scratch[:-3]), attend_out)
    extra_lane(lanes[1], extra, extra_out)
    for i in range(max(len(lane.steps) for lane in lanes) + 1):
        for lane in lanes:
            if i <= len(lane.steps):
                lane.part(i)


def final_exchange(grad, extra):
    plan = link_plan()
    xs, bs, zs = plan
    anywhere = pl.BlockSpec(memory_space=pl.ANY)
    return pl.pallas_call(
        functools.partial(final_kernel, plan),
        in_specs=[anywhere] * 2,
        out_specs=[anywhere] * 2,
        out_shape=[
            jax.ShapeDtypeStruct(grad.shape, BF16),
            jax.ShapeDtypeStruct((2 * xs * bs * zs * extra.shape[0], 128), BF16),
        ],
        scratch_shapes=held_shapes(plan, grad.shape[0]) + sems_shapes(plan, 3),
        compiler_params=pltpu.CompilerParams(
            vmem_limit_bytes=VMEM_BYTES, collective_id=0, has_side_effects=True
        ),
        name="final_exchange",
    )(grad, extra)


def unpack_kernel(layers, lines, *refs):
    ins = [refs[6 * i : 6 * i + 6] for i in range(layers)]
    w2_out, w1_out, attend_out, wo_out = refs[6 * layers : 6 * layers + 4]
    small_outs = refs[6 * layers + 4 : 6 * layers + 11]
    rows_out = refs[6 * layers + 11]
    width = w1_out.shape[1]
    for layer, (w2t, w1, attend, wo, feed_small, attend_small) in enumerate(ins):
        for j in range(w1.shape[0] // width):
            rows = slice(j * width, (j + 1) * width)
            cols = slice(j * 128, (j + 1) * 128)
            w2_out[layer, cols, :] = w2t[rows, :].astype(F32).T
            w1_out[layer, :, cols] = w1[rows, :].astype(F32)
            attend_out[layer, :, cols] = attend[rows, :].astype(F32)
            wo_out[layer, :, cols] = wo[rows, :].astype(F32)
        feed = feed_small[...].astype(F32)
        tail = attend_small[...].astype(F32)
        rows_out[layer] = tail[:lines]
        at = 0
        for out in small_outs[:5]:
            for j in range(out.shape[1] // 128):
                out[layer : layer + 1, j * 128 : (j + 1) * 128] = feed[at : at + 1]
                at += 1
        at = lines
        for out in small_outs[5:]:
            for j in range(out.shape[1] // 128):
                out[layer : layer + 1, j * 128 : (j + 1) * 128] = tail[at : at + 1]
                at += 1


def unpack(fulls, width, hidden):
    layers = len(fulls)
    wide = width // 128
    steps = hidden // width
    rows = wide * width
    last = 3 * width // width - 1
    block = (rows, 128)
    feed_big, feed_small = feed_rows(width, hidden)
    attend_big, attend_all, lines = attend_rows(width)
    attend_small = attend_all - attend_big

    def spec(first, top):
        return pl.BlockSpec(block, lambda g: (first + jnp.minimum(g, top), 0))

    ins = [
        spec(0, steps),
        spec(steps, steps),
        spec(0, last),
        spec(2 * steps, 0),
        pl.BlockSpec((feed_small, 128), lambda g: (0, 0)),
        pl.BlockSpec((attend_small, 128), lambda g: (0, 0)),
    ]
    vectors = [width] * 4 + [hidden] + [width] * 2
    return pl.pallas_call(
        functools.partial(unpack_kernel, layers, lines),
        grid=(steps,),
        in_specs=ins * layers,
        out_specs=[
            pl.BlockSpec((layers, width, width), lambda g: (0, g, 0)),
            pl.BlockSpec((layers, width, width), lambda g: (0, 0, g)),
            pl.BlockSpec((layers, width, width), lambda g: (0, 0, jnp.minimum(g, last))),
            pl.BlockSpec((layers, width, width), lambda g: (0, 0, 0)),
        ]
        + [pl.BlockSpec((layers, n), lambda g: (0, 0)) for n in vectors]
        + [pl.BlockSpec((layers, lines, 128), lambda g: (0, 0, 0))],
        out_shape=[
            jax.ShapeDtypeStruct((layers, hidden, width), F32),
            jax.ShapeDtypeStruct((layers, width, hidden), F32),
            jax.ShapeDtypeStruct((layers, width, 3 * width), F32),
            jax.ShapeDtypeStruct((layers, width, width), F32),
        ]
        + [jax.ShapeDtypeStruct((layers, n), F32) for n in vectors]
        + [jax.ShapeDtypeStruct((layers, lines, 128), F32)],
        compiler_params=pltpu.CompilerParams(vmem_limit_bytes=VMEM_BYTES),
        name="unpack",
    )(
        *[
            ref
            for feed, attend in fulls
            for ref in (
                feed,
                feed,
                attend,
                feed,
                feed[feed_big : feed_big + feed_small],
                attend[attend_big:attend_all],
            )
        ]
    )


def time_embedding(timesteps, width):
    half_width = width // 2
    frequency = jnp.exp(
        jnp.arange(half_width, dtype=jnp.int32).astype(F32) * (-math.log(10000.0) / half_width)
    )
    angles = timesteps.astype(F32)[:, None] * frequency[None, :]
    return jnp.concatenate([jnp.sin(angles), jnp.cos(angles)], axis=-1)


def bias_rows(table, index_table, grid_cols):
    heads, entries = table.shape
    span = 2 * WIN + 1
    offsets = 2 * grid_cols - 1
    turned = index_table.reshape(span, offsets)[:, ::-1].reshape(entries)
    select = (turned[None, :] == jnp.arange(entries, dtype=jnp.int32)[:, None]).astype(F32)
    rows = jnp.dot(table, select, precision=EXACT).reshape(heads, span, offsets)
    key_rows = KWIN // grid_cols
    a0, a1, a2, a3 = [
        jnp.pad(
            rows, ((0, 0), (q, key_rows - span - q), (0, 0)), constant_values=NEG_FILL
        )
        for q in range(QBLOCK // grid_cols)
    ]
    gap = jnp.full((heads, key_rows, 1), NEG_FILL, F32)
    even = jnp.concatenate(
        [a0[..., grid_cols - 1 :], gap, a2, gap, a0[..., : grid_cols - 1]], axis=-1
    )
    odd = jnp.concatenate([gap, a1, gap, a3], axis=-1)
    return jnp.stack([even, odd], axis=1)


def spaced(parts, steps):
    return [i * (steps - 1) // (parts - 1) for i in range(parts)]


def body(
    tokens,
    cotangent,
    valid_mask,
    timesteps,
    index_table,
    first_gain,
    first_shift,
    attend_weight,
    time_weight,
    offset_bias,
    output_weight,
    output_bias,
    second_gain,
    second_shift,
    expand_weight,
    expand_bias,
    reduce_weight,
    reduce_bias,
):
    images, band_rows, grid_cols, width = tokens.shape
    layers = attend_weight.shape[0]
    bands = lax.axis_size("band")
    me = lax.axis_index("band")
    own = images // bands
    part = band_rows * grid_cols
    patches = bands * part
    per_image = patches // CHUNK
    chunks = own * per_image

    mine = lax.dynamic_slice_in_dim(valid_mask, me * own, own, 0).reshape(own, patches)
    fill = jnp.where(mine == 1, 0.0, NEG_FILL).astype(F32)
    fill = jnp.pad(fill, ((0, 0), (HALO, HALO)), constant_values=NEG_FILL)
    mask = jnp.stack(
        [fill[:, c * CHUNK : (c + 1) * CHUNK + 2 * HALO] for c in range(per_image)], axis=1
    ).reshape(chunks, 1, CHUNK + 2 * HALO)

    time_low = time_embedding(
        lax.dynamic_slice_in_dim(timesteps, me * own, own, 0), width
    ).astype(BF16)
    heads, entries = offset_bias.shape[1:]

    def make_rows(table):
        return bias_rows(table, index_table, grid_cols)

    biases, bias_pull = jax.vjp(make_rows, offset_bias.reshape(layers * heads, entries))
    biases = biases.reshape(layers, -1, QBLOCK)

    def rows_of(v):
        return v.reshape(layers, 1, -1)

    tp = jnp.einsum("it,ltc->lic", time_low, time_weight, preferred_element_type=F32)
    tproj = jnp.concatenate([tp[..., :width], jnp.zeros_like(tp[..., :width]), tp[..., width:]], -1)
    gain1, shift1, gain2, shift2 = map(
        rows_of, (first_gain, first_shift, second_gain, second_shift)
    )
    weights = (
        gain1,
        shift1,
        attend_weight,
        output_weight,
        rows_of(output_bias),
        gain2,
        shift2,
        expand_weight,
        rows_of(expand_bias),
        reduce_weight,
        rows_of(reduce_bias),
    )
    x, x_lead = tokens.reshape(images * part, width), 0
    kept = []
    for layer in range(layers):
        last = layer == layers - 1
        jobs = []
        if last:
            shard = cotangent.reshape(images * part, width)
            jobs = [("images", shard, (own, part), [0, chunks // 2, chunks + 2])]
        qkv, p, o, mid, act, slope, nxt, *more = forward_layer(
            x,
            x_lead,
            chunks,
            per_image,
            tproj[layer][:, None, :],
            mask,
            biases,
            layer,
            weights,
            BF16 if last else F32,
            Links(jobs),
            own,
            part,
            1 + layer,
        )
        if layer == 0:
            x = more[0]
        if last:
            gx = more[-1]
        kept.append((x, x_lead, qkv, p, o, mid, act, slope))
        x, x_lead = nxt, 2

    gx_lead = 0
    devices = bands * lax.axis_size("img")
    hidden = expand_weight.shape[2]
    fulls = [[None, None] for _ in range(layers)]
    extra = [time_low]
    attend_grads = None
    result = x
    for layer in reversed(range(layers)):
        x, x_lead, qkv, p, o, mid, act, slope = kept[layer]
        steps = own * patches // FEED
        if layer == layers - 1:
            jobs = [("bands", result, (2 * CHUNK, own, part), [0, steps // 2, steps])]
        else:
            jobs = [("sum", attend_grads, [spaced(9, steps + 1)])]
        gmid, go, feed_grads, sent = feed_back(
            gx,
            gx_lead,
            own * patches,
            mid,
            act,
            slope,
            o,
            layer,
            gain2,
            shift2,
            expand_weight,
            reduce_weight,
            output_weight,
            Links(jobs),
            1 + layers + 2 * layer,
        )
        if layer == layers - 1:
            output = sent.reshape(tokens.shape)
        else:
            fulls[layer + 1][1] = sent
        gx, gtime, attend_grads, fulls[layer][0] = attend_back(
            qkv,
            p,
            go,
            o,
            gmid,
            x,
            x_lead,
            chunks,
            per_image,
            layer,
            gain1,
            shift1,
            attend_weight,
            own,
            part,
            Links([("sum", feed_grads, [spaced(9, chunks + 1), [i + 1 for i in spaced(9, chunks + 1)]])]),
            2 + layers + 2 * layer,
        )
        gx_lead = 1
        extra.append(jnp.sum(gtime, axis=1).astype(BF16))
    input_grad = gx.reshape(tokens.shape)

    extra = jnp.concatenate(extra, axis=1).reshape(-1, 128)
    lead = extra.shape[0]
    extra = jnp.pad(extra, ((0, -lead % 16), (0, 0)))
    fulls[0][1], gathered = final_exchange(attend_grads, extra)
    gathered = gathered.reshape(devices, -1, 128)[:, :lead].reshape(devices * own, -1)
    grad_time = jnp.stack(
        [
            lax.dot_general(
                gathered[:, :width],
                gathered[:, width * (1 + 2 * turn) : width * (3 + 2 * turn)],
                (((0,), (0,)), ((), ())),
                preferred_element_type=F32,
            )
            for turn in reversed(range(layers))
        ]
    )
    (
        grad_reduce,
        grad_expand,
        grad_attend,
        grad_output,
        reduce_bias_grad,
        output_bias_grad,
        second_gain_grad,
        second_shift_grad,
        expand_bias_grad,
        first_gain_grad,
        first_shift_grad,
        grad_rows,
    ) = unpack(fulls, width, hidden)
    (grad_offset,) = bias_pull(grad_rows.reshape(layers * heads, 2, -1, QBLOCK))
    return (
        output,
        input_grad,
        first_gain_grad,
        first_shift_grad,
        grad_attend,
        grad_time,
        grad_offset.reshape(layers, heads, entries),
        grad_output,
        output_bias_grad,
        second_gain_grad,
        second_shift_grad,
        grad_expand,
        expand_bias_grad,
        grad_reduce,
        reduce_bias_grad,
    )


def solution(mesh):
    split = P("img", "band", None, None)
    placed = (split, split, P("img", None, None), P("img")) + (P(),) * 14
    return jax.shard_map(
        body,
        mesh=mesh,
        in_specs=placed,
        out_specs=(split, split) + (P(),) * 13,
        check_vma=False,
    )
```

```python
import functools
import math

import jax
import jax.numpy as jnp
from jax import lax
from jax.experimental import pallas as pl
from jax.experimental.pallas import tpu as pltpu
from jax.sharding import PartitionSpec as P

WIN = 4
CHUNK = 256
QBLOCK = 128
KWIN = 384
HALO = 128
FEED = 512

EXACT = lax.Precision.HIGHEST
NEG_FILL = -1000000000.0
EPSILON = 1e-06
GELU_A = math.sqrt(2.0 / math.pi)
GELU_B = 0.044715 * GELU_A
VMEM_BYTES = 58 * 1024 * 1024

F32 = jnp.float32
BF16 = jnp.bfloat16


def dot(a, b):
    return jnp.dot(a, b, preferred_element_type=F32)


def dot_nt(a, b):
    return lax.dot_general(a, b, (((1,), (1,)), ((), ())), preferred_element_type=F32)


def norm_stats(v):
    mean = jnp.mean(v, axis=-1, keepdims=True)
    centered = v - mean
    inverse = lax.rsqrt(jnp.mean(centered * centered, axis=-1, keepdims=True) + EPSILON)
    return centered * inverse, inverse


def norm_back(gy, xh, inverse, gain):
    gs = gy * gain
    return inverse * (
        gs - jnp.mean(gs, axis=-1, keepdims=True) - xh * jnp.mean(gs * xh, axis=-1, keepdims=True)
    )


def row_sums(v):
    rows, cols = v.shape
    return jnp.sum(v.reshape(rows // 8, 8, cols), axis=0)


def split_heads(block):
    lane = lax.broadcasted_iota(jnp.int32, block.shape, 1)
    zero = jnp.zeros_like(block)
    first = lane < block.shape[1] // 2
    return jnp.concatenate(
        [jnp.where(first, block, zero), jnp.where(first, zero, block)], axis=0
    )


def join_heads(product):
    half = product.shape[0] // 2
    width = product.shape[1] // 2
    return jnp.concatenate([product[:half, :width], product[half:, width:]], axis=0).T


def share_rows(rows):
    return max(n for n in range(16, 257, 16) if rows % n == 0)


def add_rows(total, at, others, rows):
    share = share_rows(rows)

    def one(i, carry):
        low = pl.multiple_of(i * share, 16)
        here = pl.ds(pl.multiple_of(at + low, 16), share)
        v = total[here, :].astype(F32)
        for ref, row in others:
            v = v + ref[pl.ds(pl.multiple_of(row + low, 16), share), :].astype(F32)
        total[here, :] = v.astype(total.dtype)
        return carry

    lax.fori_loop(0, rows // share, one, 0)


def cut(ref, at, rows):
    return ref.at[pl.ds(pl.multiple_of(at, 16), rows), :]


def both(first, second):
    first()
    second()


def dispatch(step, acts):
    whens = sorted(acts)
    if len(whens) <= 1:
        for when in whens:
            pl.when(step == when)(acts[when])
        return
    middle = whens[len(whens) // 2]
    low = {when: acts[when] for when in whens if when < middle}
    high = {when: acts[when] for when in whens if when >= middle}
    pl.when(step < middle)(lambda: dispatch(step, low))
    pl.when(step >= middle)(lambda: dispatch(step, high))


def mod(v, n):
    return jnp.bitwise_and(v, n - 1) if n & (n - 1) == 0 else lax.rem(v, n)


def halved(v, n):
    return jnp.right_shift(v, n.bit_length() - 1) if n & (n - 1) == 0 else v // n


class Places:
    def __init__(self, plan):
        self.xs, self.bs, self.zs = plan
        self.img = lax.axis_index("img")
        self.b = lax.axis_index("band")
        self.c = mod(self.img, 2)
        self.x = mod(halved(self.img, 2), self.xs)
        self.z = halved(self.img, 2 * self.xs)

    def core(self, by):
        return (self.img + 1 - 2 * self.c, self.b)

    def along_x(self, by):
        return ((self.z * self.xs + mod(self.x + by, self.xs)) * 2 + self.c, self.b)

    def along_b(self, by):
        return (self.img, mod(self.b + by, self.bs))

    def along_z(self, by):
        return ((mod(self.z + by, self.zs) * self.xs + self.x) * 2 + self.c, self.b)

    def greet(self):
        barrier = pltpu.get_barrier_semaphore()
        peers = [self.core(1)]
        peers += [self.along_x(by) for by in range(1, self.xs)]
        peers += [self.along_b(by) for by in range(1, self.bs)]
        peers += [self.along_z(by) for by in range(1, self.zs)]
        for peer in peers:
            pl.semaphore_signal(barrier, inc=1, device_id=peer, device_id_type=pl.DeviceIdType.MESH)
        pl.semaphore_wait(barrier, len(peers))


class Lane:
    def __init__(self, plan, sems):
        self.plan, self.sems, self.steps = plan, sems, []

    def add(self, copies, then=None):
        count = [0, 0]
        here = Places(self.plan)
        for src, dst, peer in copies(here):
            count[peer is None] += 1
        base = (self.sems.sent, self.sems.kept)
        self.sems.sent += count[0]
        self.sems.kept += count[1]
        self.steps.append((copies, then, base))

    def described(self, step):
        copies, _, (sent, kept) = self.steps[step]
        made = []
        for src, dst, peer in copies(Places(self.plan)):
            if peer is None:
                made.append(pltpu.make_async_copy(src, dst, self.sems.own.at[kept]))
                kept += 1
            else:
                made.append(
                    pltpu.make_async_remote_copy(
                        src_ref=src,
                        dst_ref=dst,
                        send_sem=self.sems.send.at[sent],
                        recv_sem=self.sems.recv.at[sent],
                        device_id=peer,
                        device_id_type=pl.DeviceIdType.MESH,
                    )
                )
                sent += 1
        return made

    def part(self, i):
        if i > 0:
            for copy in self.described(i - 1):
                copy.wait()
            if self.steps[i - 1][1] is not None:
                self.steps[i - 1][1](Places(self.plan))
        if i < len(self.steps):
            for copy in self.described(i):
                copy.start()


class Sems:
    def __init__(self, send, recv, own):
        self.send, self.recv, self.own = send, recv, own
        self.sent = self.kept = 0


def scatter_lane(lane, grad, held, chunk=None):
    acc, r1, r2a, r2b, r3a, r3b, r4 = held
    xs, bs, zs = lane.plan
    half = grad.shape[0] // 2
    quarter = half // 2
    nx, nb, n2 = quarter // xs, quarter // bs, quarter // (xs * bs)
    n = n2 // zs

    def core_copies(at):
        return [
            (cut(grad, at.c * half, half), acc, None),
            (cut(grad, half - at.c * half, half), r1, at.core(1)),
        ]

    lane.add(core_copies, lambda at: add_rows(acc, 0, [(r1, 0)], half))

    def wide_copies(at):
        made = []
        for by in range(1, xs):
            there = mod(at.x + by, xs)
            made.append((cut(acc, there * nx, nx), cut(r2a, (by - 1) * nx, nx), at.along_x(by)))
        for by in range(1, bs):
            there = quarter + mod(at.b + by, bs) * nb
            made.append((cut(acc, there, nb), cut(r2b, (by - 1) * nb, nb), at.along_b(by)))
        return made

    def wide_add(at):
        add_rows(acc, at.x * nx, [(r2a, k * nx) for k in range(xs - 1)], nx)
        add_rows(acc, quarter + at.b * nb, [(r2b, k * nb) for k in range(bs - 1)], nb)

    lane.add(wide_copies, wide_add)

    def cross_copies(at):
        made = []
        for by in range(1, bs):
            there = at.x * nx + mod(at.b + by, bs) * n2
            made.append((cut(acc, there, n2), cut(r3a, (by - 1) * n2, n2), at.along_b(by)))
        for by in range(1, xs):
            there = quarter + at.b * nb + mod(at.x + by, xs) * n2
            made.append((cut(acc, there, n2), cut(r3b, (by - 1) * n2, n2), at.along_x(by)))
        return made

    def plane(at):
        return at.x * nx + at.b * n2, quarter + at.b * nb + at.x * n2

    def cross_add(at):
        first, second = plane(at)
        add_rows(acc, first, [(r3a, k * n2) for k in range(bs - 1)], n2)
        add_rows(acc, second, [(r3b, k * n2) for k in range(xs - 1)], n2)

    lane.add(cross_copies, cross_add)

    def deep_copies(at):
        made = []
        for by in range(1, zs):
            there = mod(at.z + by, zs) * n
            for k, low in enumerate(plane(at)):
                slot = (2 * (by - 1) + k) * n
                made.append((cut(acc, low + there, n), cut(r4, slot, n), at.along_z(by)))
        return made

    def deep_add(at):
        for k, low in enumerate(plane(at)):
            add_rows(acc, low + at.z * n, [(r4, (2 * i + k) * n) for i in range(zs - 1)], n)

    lane.add(deep_copies, deep_add)

    def ends(at):
        return [cut(acc, low + at.z * n, n) for low in plane(at)]

    if chunk is None:
        return ends
    lane.add(lambda at: [(ref, cut(chunk, k * n, n), None) for k, ref in enumerate(ends(at))])


def collect_lane(lane, ends, out):
    xs, bs, zs = lane.plan
    half = out.shape[0] // 2
    quarter = half // 2
    nx, nb, n2 = quarter // xs, quarter // bs, quarter // (xs * bs)
    n = n2 // zs

    def plane(at):
        base = at.c * half
        return base + at.x * nx + at.b * n2, base + quarter + at.b * nb + at.x * n2

    def deep(at):
        made = []
        for ref, low in zip(ends(at), plane(at)):
            there = cut(out, low + at.z * n, n)
            made.append((ref, there, None))
            made += [(ref, there, at.along_z(by)) for by in range(1, zs)]
        return made

    def cross(at):
        first, second = plane(at)
        a, b = cut(out, first, n2), cut(out, second, n2)
        made = [(a, a, at.along_b(by)) for by in range(1, bs)]
        return made + [(b, b, at.along_x(by)) for by in range(1, xs)]

    def wide(at):
        a = cut(out, at.c * half + at.x * nx, nx)
        b = cut(out, at.c * half + quarter + at.b * nb, nb)
        made = [(a, a, at.along_x(by)) for by in range(1, xs)]
        return made + [(b, b, at.along_b(by)) for by in range(1, bs)]

    def core(at):
        whole = cut(out, at.c * half, half)
        return [(whole, whole, at.core(1))]

    for copies in (deep, cross, wide, core):
        lane.add(copies)


def extra_lane(lane, extra, out):
    xs, bs, zs = lane.plan
    rows = extra.shape[0]

    def deep(at):
        there = cut(out, (((at.c * xs + at.x) * bs + at.b) * zs + at.z) * rows, rows)
        return [(extra, there, None)] + [(extra, there, at.along_z(by)) for by in range(1, zs)]

    def cross(at):
        there = cut(out, ((at.c * xs + at.x) * bs + at.b) * zs * rows, zs * rows)
        return [(there, there, at.along_b(by)) for by in range(1, bs)]

    def wide(at):
        there = cut(out, (at.c * xs + at.x) * bs * zs * rows, bs * zs * rows)
        return [(there, there, at.along_x(by)) for by in range(1, xs)]

    def core(at):
        there = cut(out, at.c * xs * bs * zs * rows, xs * bs * zs * rows)
        return [(there, there, at.core(1))]

    for copies in (deep, cross, wide, core):
        lane.add(copies)


def link_plan():
    pairs = lax.axis_size("img") // 2
    xs = 2 if pairs % 2 == 0 else 1
    return xs, lax.axis_size("band"), pairs // xs


def padded_rows(rows):
    xs, bs, zs = link_plan()
    return -(-rows // (64 * xs * bs * zs)) * (64 * xs * bs * zs)


def held_shapes(plan, rows):
    xs, bs, zs = plan
    quarter = rows // 4
    sizes = [
        rows // 2,
        rows // 2,
        (xs - 1) * quarter // xs,
        (bs - 1) * quarter // bs,
        (bs - 1) * quarter // (xs * bs),
        (xs - 1) * quarter // (xs * bs),
        (zs - 1) * 2 * quarter // (xs * bs * zs),
    ]
    return [pltpu.VMEM((max(n, 16), 128), BF16) for n in sizes]


def sems_shapes(plan, lanes, moved=0):
    xs, bs, zs = plan
    count = lanes * (1 + 2 * (xs - 1 + bs - 1) + 2 * (zs - 1)) + moved
    return [
        pltpu.SemaphoreType.DMA((count,)),
        pltpu.SemaphoreType.DMA((count,)),
        pltpu.SemaphoreType.DMA((2 * lanes + moved + 1,)),
    ]


def images_copies(shard, at, own, part, images):
    made = []
    for by in range(at.bs):
        there = mod(at.b + by, at.bs)
        for i in images:
            made.append(((there * own + i) * part, (i * at.bs + at.b) * part, by))
    return made


def runs_of(rows, lanes):
    unit = padded_rows(1)
    units = rows // unit
    lanes = min(lanes, units)
    ends = [units * i // lanes * unit for i in range(lanes + 1)]
    return [(low, high - low) for low, high in zip(ends, ends[1:])]


def chunk_ends(chunk, low, rows, devices):
    low, half = low // devices, rows // devices // 2
    return lambda at: [cut(chunk, low + k * half, half) for k in range(2)]


def load_lane(lane, chunk, here, low, rows, devices):
    part = pl.ds(low // devices, rows // devices)
    lane.add(lambda at: [(chunk.at[part, :], here.at[part, :], None)])


class Links:
    def __init__(self, jobs):
        self.jobs = jobs
        self.plan = link_plan()
        xs, bs, zs = self.plan
        self.devices = 2 * xs * bs * zs
        self.arrays = [job[1] for job in jobs]
        self.shapes, self.scratch = [], []
        remote = local = 0
        for job in jobs:
            if job[0] in ("sum", "scatter", "collect"):
                rows_all = job[1].shape[0] * (self.devices if job[0] == "collect" else 1)
                for _, rows in runs_of(rows_all, len(job[-1])):
                    if job[0] != "collect":
                        self.scratch += held_shapes(self.plan, rows)
                    remote += 2 * (1 + 2 * (xs - 1 + bs - 1) + 2 * (zs - 1))
                    local += 4
                if job[0] == "collect":
                    self.scratch.append(pltpu.VMEM(job[1].shape, BF16))
                if job[0] == "scatter":
                    rows_all //= self.devices
                self.shapes.append(jax.ShapeDtypeStruct((rows_all, 128), BF16))
                continue
            width = job[1].shape[1]
            own, part = job[2][-2:]
            shape = (bs, own, part, width) if job[0] == "bands" else (own * bs * part, width)
            self.shapes.append(jax.ShapeDtypeStruct(shape, BF16))
            self.scratch.append(pltpu.VMEM((own, part, width), BF16))
            remote += (bs - 1) * own
            local += 2 * own
        if jobs:
            self.scratch += [
                pltpu.SemaphoreType.DMA((max(remote, 1),)),
                pltpu.SemaphoreType.DMA((max(remote, 1),)),
                pltpu.SemaphoreType.DMA((local,)),
            ]
        self.specs = [pl.BlockSpec(memory_space=pl.ANY)] * len(jobs)

    def host(self, kernel, ins, outs, scratch):
        def run(*refs):
            count = len(self.jobs)
            a, b, c = ins, ins + count, ins + count + outs
            d, e = c + count, c + count + scratch
            step = pl.program_id(0)
            acts = kernel(*refs[:a], *refs[b:c], *refs[d:e]) or {}
            if self.jobs:
                parts = self.parts(refs[a:b], refs[c:d], refs[e:])
                parts.setdefault(0, [])
                for when in sorted(parts):

                    def act(when=when):
                        if when == 0:
                            Places(self.plan).greet()
                        for lane, part in parts[when]:
                            lane.part(part)

                    at = min(when, pl.num_programs(0) - 1)
                    before = acts.get(at)
                    acts[at] = act if before is None else functools.partial(both, before, act)
            dispatch(step, acts)

        return run

    def parts(self, given, made, scratch):
        sems = Sems(*scratch[-3:])
        held = list(scratch[:-3])
        parts = {}
        lanes = []
        for job, ref, out in zip(self.jobs, given, made):
            if job[0] == "sum":
                for (low, rows), whens in zip(runs_of(ref.shape[0], len(job[-1])), job[-1]):
                    lane = Lane(self.plan, sems)
                    part_in, part_out = ref.at[pl.ds(low, rows), :], out.at[pl.ds(low, rows), :]
                    collect_lane(lane, scatter_lane(lane, part_in, held[:7]), part_out)
                    held = held[7:]
                    lanes.append((lane, whens))
                continue
            if job[0] == "scatter":
                for (low, rows), whens in zip(runs_of(ref.shape[0], len(job[-1])), job[-1]):
                    lane = Lane(self.plan, sems)
                    few = rows // self.devices
                    chunk = out.at[pl.ds(low // self.devices, few), :]
                    scatter_lane(lane, ref.at[pl.ds(low, rows), :], held[:7], chunk)
                    held = held[7:]
                    lanes.append((lane, whens))
                continue
            if job[0] == "collect":
                here = held[0]
                held = held[1:]
                for (low, rows), whens in zip(runs_of(out.shape[0], len(job[-1])), job[-1]):
                    lane = Lane(self.plan, sems)
                    load_lane(lane, ref, here, low, rows, self.devices)
                    ends = chunk_ends(here, low, rows, self.devices)
                    collect_lane(lane, ends, out.at[pl.ds(low, rows), :])
                    lanes.append((lane, whens))
                continue
            own, part = job[2][-2:]
            lead = job[2][0] if job[0] == "bands" else 0

            def copies(at, kind=job[0], ref=ref, out=out, own=own, part=part, lead=lead):
                made = []
                for i in range(own):
                    for by in range(self.plan[1]):
                        there = mod(at.b + by, self.plan[1])
                        if kind == "bands":
                            src = cut(ref, lead + (i * self.plan[1] + there) * part, part)
                            dst = out.at[at.b, i]
                        else:
                            src = cut(ref, (there * own + i) * part, part)
                            dst = cut(out, (i * self.plan[1] + at.b) * part, part)
                        made.append((i, src, dst, at.along_b(by) if by else None))
                return made

            lane = Lane(self.plan, sems)
            lane.add(lambda at, f=copies: [c[1:] for c in f(at) if c[3] is not None])
            lanes.append((lane, [job[-1][0], job[-1][-1]]))
            lane = Lane(self.plan, sems)
            here = held[0]
            held = held[1:]
            lane.add(lambda at, f=copies, h=here: [(c[1], h.at[c[0]], None) for c in f(at) if c[3] is None])
            lane.add(lambda at, f=copies, h=here: [(h.at[c[0]], c[2], None) for c in f(at) if c[3] is None])
            lanes.append((lane, job[-1]))
        for lane, whens in lanes:
            assert len(whens) == len(lane.steps) + 1
            for part, when in enumerate(whens):
                parts.setdefault(when, []).append((lane, part))
        return parts

    def params(self, number):
        if not self.jobs:
            return pltpu.CompilerParams(vmem_limit_bytes=VMEM_BYTES)
        return pltpu.CompilerParams(
            vmem_limit_bytes=VMEM_BYTES, collective_id=number, has_side_effects=True
        )


def fold(v, op):
    return op(v.reshape(v.shape[0] // 8, 8, v.shape[1]), axis=0)


def unroll_bias(rows, bias):
    pairs, keys, lanes = bias.shape
    grid_cols = QBLOCK // 4
    key_rows = keys // grid_cols
    lane = lax.broadcasted_iota(jnp.int32, (grid_cols, QBLOCK), 1)
    even = lax.rem(lane // grid_cols, 2) == 0
    for pair in range(pairs):
        for head in range(2):
            for key_row in range(key_rows):
                turned = [
                    pltpu.roll(
                        jnp.broadcast_to(
                            rows[pl.ds(((pair * 2 + head) * 2 + odd) * key_rows + key_row, 1), :],
                            (grid_cols, QBLOCK),
                        ),
                        0,
                        1,
                        stride=1,
                        stride_axis=0,
                    )
                    for odd in range(2)
                ]
                bias[
                    pair,
                    key_row * grid_cols : (key_row + 1) * grid_cols,
                    head * QBLOCK : (head + 1) * QBLOCK,
                ] = jnp.where(even, turned[0], turned[1])


def gather_bias(grads):
    pairs, keys, lanes = grads.shape
    grid_cols = QBLOCK // 4
    lane = lax.broadcasted_iota(jnp.int32, (keys, QBLOCK), 1)
    column = lax.rem(lax.broadcasted_iota(jnp.int32, (keys, QBLOCK), 0), grid_cols)
    parity = lax.rem(lane // grid_cols, 2)
    sums = []
    for pair in range(pairs):
        for head in range(2):
            for odd in range(2):
                v = grads[pair, :, head * QBLOCK : (head + 1) * QBLOCK]
                v = jnp.where(parity == odd, v, 0.0)
                for bit in (1, 2, 4, 8, 16):
                    turned = pltpu.roll(v, QBLOCK - bit, 1)
                    v = jnp.where(lax.rem(column // bit, 2) == 1, turned, v)
                sums.append(jnp.sum(v.reshape(keys // grid_cols, grid_cols, QBLOCK), axis=1))
    return jnp.concatenate(sums, axis=0)


def forward_kernel(
    pairs,
    layer,
    x_new,
    x_old,
    tproj,
    mask,
    bias_rows,
    gain1,
    shift1,
    wqkv,
    wo,
    bo,
    gain2,
    shift2,
    w1,
    b1,
    w2,
    b2,
    qkv_out,
    p_out,
    inverse_out,
    o_out,
    mid_out,
    acts_out,
    x_out,
    bias,
    q_ring,
    k_ring,
    vt_ring,
    o_ring,
    s_scr,
):
    step = pl.program_id(0)
    width = x_new.shape[1]
    gain1, shift1, bo, gain2, shift2, b1, b2 = [
        ref.at[pl.ds(layer, 1), :] for ref in (gain1, shift1, bo, gain2, shift2, b1, b2)
    ]

    @pl.when(step == 0)
    def _():
        unroll_bias(bias_rows, bias)
        q_ring[...] = jnp.zeros_like(q_ring)
        k_ring[...] = jnp.zeros_like(k_ring)
        vt_ring[...] = jnp.zeros_like(vt_ring)
        o_ring[...] = jnp.zeros_like(o_ring)

    act_out, slope_out = acts_out.at[0], acts_out.at[1]
    attended = o_ring[...]
    mid = x_old[...].astype(F32) + (dot(attended, wo[...]) + bo[...])
    mid_out[...] = mid
    xh2, _ = norm_stats(mid)
    c = (xh2 * gain2[...] + shift2[...]).astype(BF16)
    parts = 2 * pairs
    tile = w1.shape[1] // parts

    def feed(part):
        cols = slice(part * tile, (part + 1) * tile)
        whole = dot(c, w1[:, cols])
        for low in range(0, CHUNK, 64):
            u = whole[low : low + 64] + b1[:, cols]
            u2 = u * u
            t = jnp.tanh(u * (GELU_A + GELU_B * u2))
            h = 0.5 + 0.5 * t
            e = u * h
            act_out[low : low + 64, cols] = e.astype(BF16)
            slope_out[low : low + 64, cols] = (
                h + (e * (1.0 - t)) * (GELU_A + (3.0 * GELU_B) * u2)
            ).astype(BF16)

    queries = q_ring[...]
    xh1, _ = norm_stats(x_new[...].astype(F32))
    a = (xh1 * gain1[...] + shift1[...]).astype(BF16)
    qkv = (dot(a, wqkv[...]) + tproj[0]).astype(BF16)
    qkv_out[...] = qkv
    q_ring[...] = qkv[:, :width] * jnp.asarray(0.125, BF16)
    k_ring[:HALO, :] = k_ring[CHUNK : CHUNK + HALO, :]
    k_ring[HALO : HALO + CHUNK, :] = k_ring[HALO + CHUNK :, :]
    k_ring[HALO + CHUNK :, :] = qkv[:, width : 2 * width]
    vt_ring[:, :HALO] = vt_ring[:, CHUNK : CHUNK + HALO]
    vt_ring[:, HALO : HALO + CHUNK] = vt_ring[:, HALO + CHUNK :]
    vt_ring[:, HALO + CHUNK :] = qkv[:, 2 * width :].T

    key_index = lax.broadcasted_iota(jnp.int32, (KWIN, QBLOCK), 0)
    query_index = lax.broadcasted_iota(jnp.int32, (KWIN, QBLOCK), 1)
    diagonal = key_index == query_index + HALO
    extras = []
    for blk in range(CHUNK // QBLOCK):
        line = mask[0, :, blk * QBLOCK : blk * QBLOCK + KWIN]
        column = jnp.broadcast_to(line, (QBLOCK, KWIN)).T
        extras.append(jnp.where(diagonal, 0.0, column))
    todo = [(blk, pair) for blk in range(CHUNK // QBLOCK) for pair in range(pairs)]
    cells = [(k * 128, h * 128) for k in range(KWIN // 128) for h in range(2)]
    tops = {}

    def score(blk, pair):
        low = blk * QBLOCK
        feat = slice(pair * 128, (pair + 1) * 128)
        split_q = split_heads(queries[low : low + QBLOCK, feat])
        best = [None, None]
        for k in range(0, KWIN, 128):
            s = dot_nt(k_ring[low + k : low + k + 128, feat], split_q)
            for h in range(2):
                lane = slice(h * 128, h * 128 + 128)
                v = s[:, lane] + bias[pair, k : k + 128, lane] + extras[blk][k : k + 128]
                s_scr[blk, pair, k : k + 128, lane] = v
                top = fold(v, jnp.max)
                best[h] = top if best[h] is None else jnp.maximum(best[h], top)
        tops[blk, pair] = [jnp.max(v, axis=0, keepdims=True) for v in best]

    def soften(blk, pair):
        for k, lane in cells:
            at = (blk, pair, slice(k, k + 128), slice(lane, lane + 128))
            p_out[at] = jnp.exp(s_scr[at] - tops[blk, pair][lane // 128]).astype(BF16)

    ones = jnp.ones((16, KWIN), BF16)

    def attend(blk, pair):
        low = blk * QBLOCK
        feat = slice(pair * 128, (pair + 1) * 128)
        left = jnp.concatenate([vt_ring[feat, low : low + KWIN], ones], axis=0)
        sums = dot(left, p_out[blk, pair])
        inverse = 1.0 / sums[128:129]
        inverse_out[blk, pair : pair + 1, :] = inverse
        o_t = jnp.concatenate(
            [sums[:64, :128] * inverse[:, :128], sums[64:128, 128:] * inverse[:, 128:]], axis=0
        ).astype(BF16)
        o_out[feat, low : low + QBLOCK] = o_t
        o_ring[low : low + QBLOCK, feat] = o_t.T

    for i in range(len(todo) + 2):
        if i < len(todo):
            score(*todo[i])
            feed(i)
        if 1 <= i <= len(todo):
            soften(*todo[i - 1])
        if i >= 2:
            attend(*todo[i - 2])
    x_out[...] = (mid_out[...] + (dot(act_out[...], w2[...]) + b2[...])).astype(x_out.dtype)


def const_spec(shape):
    zeros = (0,) * len(shape)
    return pl.BlockSpec(shape, lambda g: zeros, pipeline_mode=pl.Buffered(1))


def layer_spec(shape, layer):
    if len(shape) == 2:
        return const_spec(shape)
    index = (layer,) + (0,) * (len(shape) - 1)
    return pl.BlockSpec((None,) + shape[1:], lambda g: index, pipeline_mode=pl.Buffered(1))


def first_forward_kernel(pairs, plan, chunks, own, part, shard, *refs):
    ins, outs, scratch = refs[:14], refs[14:22], refs[22:]
    x_all, send_sems, recv_sems, own_sems = scratch[-4:]
    step = pl.program_id(0)
    sems = Sems(send_sems, recv_sems, own_sems)
    lanes = []
    for i in range(own):
        lane = Lane(plan, sems)

        def copies(at, i=i):
            return [
                (cut(shard, src, part), cut(x_all, dst, part), at.along_b(by) if by else None)
                for src, dst, by in images_copies(shard, at, own, part, (i,))
            ]

        lane.add(copies)
        lanes.append(lane)
    for i in range(own):

        @pl.when(step == i * (chunks // own))
        def _(i=i):
            if i == 0:
                Places(plan).greet()
                for lane in lanes:
                    lane.part(0)
            lanes[i].part(1)

    def chunk(lead):
        at = jnp.clip(step - lead, 0, chunks - 1) * CHUNK
        return x_all.at[pl.ds(pl.multiple_of(at, CHUNK), CHUNK), :]

    x_copy = outs[-1]
    x_copy[...] = chunk(0)[...]
    forward_kernel(pairs, 0, chunk(0), chunk(2), *ins, *outs[:-1], *scratch[:-4])


def forward_layer(
    x, x_lead, chunks, chunks_per_image, tproj, mask, bias_rows, layer, weights, out_dtype, links, own, part, number
):
    width = x.shape[1]
    hidden = weights[7].shape[2]
    pairs = width // 128
    steps = chunks + 2
    first = layer == 0

    def at(lead, least=0):
        def index(g):
            return jnp.clip(g - lead, least, chunks - 1)

        return index

    new_at, attn_at, old_at = at(0), at(1), at(2)
    row = pl.BlockSpec((CHUNK, width), lambda g: (g, 0))
    rows = steps * CHUNK
    if first:
        x_specs, x_args = [pl.BlockSpec(memory_space=pl.ANY)], [x]
    else:
        x_specs = [
            pl.BlockSpec((CHUNK, width), lambda g: (new_at(g) + x_lead, 0)),
            pl.BlockSpec((CHUNK, width), lambda g: (old_at(g) + x_lead, 0)),
        ]
        x_args = [x, x]
    in_specs = x_specs + [
        pl.BlockSpec((1, 1, 3 * width), lambda g: (new_at(g) // chunks_per_image, 0, 0)),
        pl.BlockSpec((1, 1, CHUNK + 2 * HALO), lambda g: (attn_at(g), 0, 0)),
        layer_spec(bias_rows.shape, layer),
    ]
    in_specs += [layer_spec(w.shape, layer) for w in weights]
    out_specs = [
        pl.BlockSpec((CHUNK, 3 * width), lambda g: (new_at(g), 0)),
        pl.BlockSpec((CHUNK // QBLOCK, pairs, KWIN, 2 * QBLOCK), lambda g: (g, 0, 0, 0)),
        pl.BlockSpec((CHUNK // QBLOCK, 8, 2 * QBLOCK), lambda g: (g, 0, 0)),
        pl.BlockSpec((None, width, CHUNK), lambda g: (g + 1, 0, 0)),
        row,
        pl.BlockSpec((None, 2, CHUNK, hidden), lambda g: (g, 0, 0, 0)),
        row,
    ]
    out_shape = [
        jax.ShapeDtypeStruct((chunks * CHUNK, 3 * width), BF16),
        jax.ShapeDtypeStruct((steps * (CHUNK // QBLOCK), pairs, KWIN, 2 * QBLOCK), BF16),
        jax.ShapeDtypeStruct((steps * (CHUNK // QBLOCK), 8, 2 * QBLOCK), F32),
        jax.ShapeDtypeStruct((steps + 2, width, CHUNK), BF16),
        jax.ShapeDtypeStruct((rows, width), F32),
        jax.ShapeDtypeStruct((steps, 2, CHUNK, hidden), BF16),
        jax.ShapeDtypeStruct((rows, width), out_dtype),
    ]
    scratch = [
        pltpu.VMEM((pairs, KWIN, 2 * QBLOCK), F32),
        pltpu.VMEM((CHUNK, width), BF16),
        pltpu.VMEM((HALO + 2 * CHUNK, width), BF16),
        pltpu.VMEM((width, HALO + 2 * CHUNK), BF16),
        pltpu.VMEM((CHUNK, width), BF16),
        pltpu.VMEM((CHUNK // QBLOCK, pairs, KWIN, 2 * QBLOCK), F32),
    ]
    params = links.params(number)
    if first:
        plan = link_plan()
        remote = max((plan[1] - 1) * own, 1)
        kernel = functools.partial(first_forward_kernel, pairs, plan, chunks, own, part)
        out_specs.append(pl.BlockSpec((CHUNK, width), lambda g: (new_at(g), 0)))
        out_shape.append(jax.ShapeDtypeStruct((chunks * CHUNK, width), BF16))
        scratch += [
            pltpu.VMEM((chunks * CHUNK, width), BF16),
            pltpu.SemaphoreType.DMA((remote,)),
            pltpu.SemaphoreType.DMA((remote,)),
            pltpu.SemaphoreType.DMA((own,)),
        ]
        params = pltpu.CompilerParams(
            vmem_limit_bytes=VMEM_BYTES, collective_id=number, has_side_effects=True
        )
    else:
        kernel = links.host(
            functools.partial(forward_kernel, pairs, layer), len(in_specs), len(out_specs), len(scratch)
        )
    return pl.pallas_call(
        kernel,
        grid=(steps,),
        in_specs=in_specs + links.specs,
        out_specs=out_specs + links.specs,
        out_shape=out_shape + links.shapes,
        scratch_shapes=scratch + links.scratch,
        compiler_params=params,
        name="block_forward",
    )(*x_args, tproj, mask, bias_rows, *weights, *links.arrays)


def put_tiles(out, first, acc):
    width = acc.shape[0]
    for j in range(acc.shape[1] // 128):
        at = (first + j) * width
        out[at : at + width, :] = acc[:, j * 128 : (j + 1) * 128].astype(out.dtype)


def put_rows(out, at, vectors):
    lines = [v[:, j : j + 128] for v in vectors for j in range(0, v.shape[1], 128)]
    lines += [jnp.zeros((1, 128), F32)] * (-len(lines) % 16)
    out[at : at + len(lines), :] = jnp.concatenate(lines, axis=0).astype(out.dtype)


def feed_back_kernel(
    layer,
    gx,
    mid,
    acts,
    o,
    gain2,
    shift2,
    w1,
    w2,
    wo,
    gmid_out,
    go_out,
    grads_out,
    gw2t,
    gw1,
    gwo,
    sums,
    gb1,
    gu_scr,
):
    step = pl.program_id(0)
    gain2, shift2 = [ref.at[pl.ds(layer, 1), :] for ref in (gain2, shift2)]

    @pl.when(step == 0)
    def _():
        for ref in (gw2t, gw1, gwo, sums, gb1):
            ref[...] = jnp.zeros_like(ref)

    grad = gx[...].astype(F32)
    gr = grad.astype(BF16)
    gr_t = gr.T
    xh, inverse = norm_stats(mid[...])
    c_t = (xh * gain2[...] + shift2[...]).astype(BF16).T
    hidden = acts.shape[3]
    halves = acts.shape[0]
    tile = 256
    for low in range(0, hidden, tile):
        cols = slice(low, low + tile)
        ge = dot_nt(gr, w2[cols, :])
        slope = jnp.concatenate([acts[i, 1, :, cols] for i in range(halves)], axis=0)
        act = jnp.concatenate([acts[i, 0, :, cols] for i in range(halves)], axis=0)
        gu = (ge * slope.astype(F32)).astype(BF16)
        gu_scr[:, cols] = gu
        gb1[:, cols] += row_sums(gu.astype(F32))
        gw2t[:, cols] += dot(gr_t, act)
        gw1[:, cols] += dot(c_t, gu)
    gc = dot_nt(gu_scr[...], w1[...])
    gmid = grad + norm_back(gc, xh, inverse, gain2[...])
    gmid_out[...] = gmid
    gb = gmid.astype(BF16)
    gwo[...] += dot(jnp.concatenate([o[i] for i in range(o.shape[0])], axis=1), gb)
    go_t = dot_nt(wo[...], gb).astype(BF16)
    for i in range(o.shape[0]):
        go_out[i] = go_t[:, i * CHUNK : (i + 1) * CHUNK]
    sums[0] += row_sums(gr.astype(F32))
    sums[1] += row_sums(gb.astype(F32))
    sums[2] += row_sums(gc * xh)
    sums[3] += row_sums(gc)

    @pl.when(step == pl.num_programs(0) - 1)
    def _():
        tiles = hidden // 128
        put_tiles(grads_out, 0, gw2t)
        put_tiles(grads_out, tiles, gw1)
        put_tiles(grads_out, 2 * tiles, gwo)
        whole = [jnp.sum(sums[i], axis=0, keepdims=True) for i in range(4)]
        whole.append(jnp.sum(gb1[...], axis=0, keepdims=True))
        at = (2 * tiles + gwo.shape[1] // 128) * gwo.shape[0]
        put_rows(grads_out, at, whole)
        used = sum(feed_rows(gwo.shape[0], hidden))
        spare = grads_out.shape[0] - used
        if spare:
            grads_out[used:, :] = jnp.zeros((spare, 128), grads_out.dtype)


def feed_rows(width, hidden):
    tiles = (2 * hidden + width) // 128
    return tiles * width, -(-(4 * width + hidden) // 128 // 16) * 16


def feed_back(
    gx, gx_lead, patches, mid, acts, o, layer, gain2, shift2, w1, w2, wo, links, number
):
    width = mid.shape[1]
    hidden = acts.shape[3]

    def rows(cols, lead):
        return pl.BlockSpec((FEED, cols), lambda g: (g + lead, 0))

    grad_rows = padded_rows(sum(feed_rows(width, hidden)))
    return pl.pallas_call(
        links.host(functools.partial(feed_back_kernel, layer), 9, 3, 6),
        grid=(patches // FEED,),
        in_specs=[
            rows(width, gx_lead),
            rows(width, 1),
            pl.BlockSpec((FEED // CHUNK, 2, CHUNK, hidden), lambda g: (g + 1, 0, 0, 0)),
            pl.BlockSpec((FEED // CHUNK, width, CHUNK), lambda g: (g + 1, 0, 0)),
        ]
        + [layer_spec(w.shape, layer) for w in (gain2, shift2, w1, w2, wo)]
        + links.specs,
        out_specs=[
            rows(width, 0),
            pl.BlockSpec((FEED // CHUNK, width, CHUNK), lambda g: (g, 0, 0)),
            const_spec((grad_rows, 128)),
        ]
        + links.specs,
        out_shape=[
            jax.ShapeDtypeStruct((patches, width), F32),
            jax.ShapeDtypeStruct((patches // CHUNK, width, CHUNK), BF16),
            jax.ShapeDtypeStruct((grad_rows, 128), BF16),
        ]
        + links.shapes,
        scratch_shapes=[
            pltpu.VMEM((width, hidden), F32),
            pltpu.VMEM((width, hidden), F32),
            pltpu.VMEM((width, width), F32),
            pltpu.VMEM((4, 8, width), F32),
            pltpu.VMEM((8, hidden), F32),
            pltpu.VMEM((FEED, hidden), BF16),
        ]
        + links.scratch,
        compiler_params=links.params(number),
        name="feed_back",
    )(gx, mid, acts, o, gain2, shift2, w1, w2, wo, *links.arrays)


class Pusher:
    SLOTS = 8

    def __init__(self, plan, own, part, refs):
        self.plan, self.own, self.part = plan, own, part
        self.out, self.slots, self.send, self.recv, self.local = refs
        self.piece = min(part, CHUNK)
        self.subs = part // self.piece
        self.at = Places(plan)

    def each(self, chunk, act):
        at, bs = self.at, self.plan[1]
        whole = bs * self.part
        slot = chunk % self.SLOTS
        for k in range(CHUNK // self.piece):
            row = chunk * CHUNK + k * self.piece
            image, within = divmod(row, whole)
            target, sub = within // self.part, within % self.part // self.piece
            src = self.slots.at[slot, pl.ds(k * self.piece, self.piece), :]
            dst = self.out.at[at.b, image, pl.ds(sub * self.piece, self.piece), :]
            sem = slot * (CHUNK // self.piece) + k

            @pl.when(at.b == target)
            def _():
                act(pltpu.make_async_copy(src, dst, self.local.at[sem]), False)

            @pl.when(at.b != target)
            def _():
                by = mod(target - at.b + bs, bs)
                copy = pltpu.make_async_remote_copy(
                    src_ref=src,
                    dst_ref=dst,
                    send_sem=self.send.at[sem],
                    recv_sem=self.recv.at[((by - 1) * self.own + image) * self.subs + sub],
                    device_id=(at.img, target),
                    device_id_type=pl.DeviceIdType.MESH,
                )
                act(copy, True)

    def start(self, chunk):
        self.each(chunk, lambda copy, remote: copy.start())

    def sent(self, chunk):
        self.each(chunk, lambda copy, remote: copy.wait_send() if remote else copy.wait())

    def received(self):
        at, bs = self.at, self.plan[1]
        for by in range(1, bs):
            sender = mod(at.b - by + bs, bs)
            for image in range(self.own):
                for sub in range(self.subs):
                    pltpu.make_async_remote_copy(
                        src_ref=self.slots.at[0, pl.ds(0, self.piece), :],
                        dst_ref=self.out.at[sender, image, pl.ds(sub * self.piece, self.piece), :],
                        send_sem=self.send.at[0],
                        recv_sem=self.recv.at[((by - 1) * self.own + image) * self.subs + sub],
                        device_id=(at.img, sender),
                        device_id_type=pl.DeviceIdType.MESH,
                    ).wait_recv()


def last_attend_back_kernel(pairs, chunks, chunks_per_image, plan, own, part, *refs):
    ins, outs, scratch = refs[:12], refs[12:15], refs[15:]
    out, slots = outs[0], scratch[9]
    step = pl.program_id(0)
    pusher = Pusher(plan, own, part, (out, slots, *scratch[10:]))

    slot = slots.at[mod(step + Pusher.SLOTS - 1, Pusher.SLOTS)]
    attend_back_kernel(pairs, 0, chunks, chunks_per_image, *ins, slot, *outs[1:], *scratch[:9])
    acts = {}
    for chunk in range(chunks):

        def act(chunk=chunk):
            pusher.start(chunk)
            if 0 <= chunk + 1 - Pusher.SLOTS and chunk < chunks - 1:
                pusher.sent(chunk + 1 - Pusher.SLOTS)
            if chunk == chunks - 1:
                for old in range(max(chunks - Pusher.SLOTS, 0), chunks):
                    pusher.sent(old)
                pusher.received()

        acts[chunk + 1] = act
    return acts


def attend_back_kernel(
    pairs,
    layer,
    chunks,
    chunks_per_image,
    prev,
    cur,
    nxt,
    p_in,
    inverse_in,
    go_in,
    o_in,
    gmid,
    x,
    gain1,
    shift1,
    wqkv,
    gx_out,
    gtime,
    grads_out,
    gwqkv,
    gbias,
    sums,
    gq_ring,
    whole_ring,
    half_ring,
    next_ring,
    done,
    gs_scr,
):
    step = pl.program_id(0)
    width = x.shape[1]
    gain1, shift1 = [ref.at[pl.ds(layer, 1), :] for ref in (gain1, shift1)]

    @pl.when(step == 0)
    def _():
        for ref in (gwqkv, gbias, gtime, sums, gq_ring, whole_ring, half_ring, next_ring):
            ref[...] = jnp.zeros_like(ref)

    gq_old = gq_ring[...]
    live = (step < chunks).astype(F32)
    qkv = cur[...]
    queries = qkv[:, :width] * jnp.asarray(0.125, BF16)
    keys = jnp.concatenate(
        [prev[:, width : 2 * width], qkv[:, width : 2 * width], nxt[:, width : 2 * width]], axis=0
    )
    keys_t = keys.T
    values = jnp.concatenate([prev[:, 2 * width :], qkv[:, 2 * width :], nxt[:, 2 * width :]], axis=0)
    blocks = CHUNK // QBLOCK
    todo = [(blk, pair) for pair in range(pairs) for blk in range(blocks)]

    split_gos = {}

    def spread(blk, pair):
        low = blk * QBLOCK
        feat = slice(pair * 128, (pair + 1) * 128)
        inverse = inverse_in[blk, pair : pair + 1, :] * live
        go = go_in[feat, low : low + QBLOCK].astype(F32)
        go = [go[h * 64 : h * 64 + 64] * inverse[:, h * 128 : h * 128 + 128] for h in range(2)]
        o = o_in[feat, low : low + QBLOCK].astype(F32)
        row_dot = [
            jnp.sum(go[h] * o[h * 64 : h * 64 + 64], axis=0, keepdims=True) for h in range(2)
        ]
        split_go = split_heads(jnp.concatenate(go, axis=0).astype(BF16).T)
        split_gos[blk, pair] = split_go
        for k in range(0, KWIN, 128):
            gp = dot_nt(values[low + k : low + k + 128, feat], split_go)
            for h in range(2):
                lane = slice(h * 128, h * 128 + 128)
                gs = p_in[blk, pair, k : k + 128, lane].astype(F32) * (gp[:, lane] - row_dot[h])
                gbias[pair, k : k + 128, lane] += gs
                gs_scr[blk, pair, k : k + 128, lane] = gs.astype(BF16)

    late = []

    def pull(blk, pair):
        low = blk * QBLOCK
        feat = slice(pair * 128, (pair + 1) * 128)
        vfeat = slice(width + pair * 128, width + (pair + 1) * 128)
        gs = gs_scr[blk, pair]
        gk = dot(gs, split_heads(queries[low : low + QBLOCK, feat]))
        gv = dot(p_in[blk, pair], split_gos[blk, pair])
        gq = join_heads(dot(keys_t[feat, low : low + KWIN], gs)) * 0.125
        gq_ring[low : low + QBLOCK, feat] = gq.astype(BF16)
        late.append((gk, gv))
        if blk == blocks - 1:
            for cols, first, second in zip((feat, vfeat), late[-2], late[-1]):
                done[HALO:, cols] = (half_ring[:, cols] + first[:HALO]).astype(BF16)
                done[:HALO, cols] = whole_ring[:, cols]
                whole_ring[:, cols] = (
                    next_ring[:, cols] + first[HALO : 2 * HALO] + second[:HALO]
                ).astype(BF16)
                half_ring[:, cols] = first[2 * HALO :] + second[HALO : 2 * HALO]
                next_ring[:, cols] = second[2 * HALO :]

    for i in range(len(todo) + 1):
        if i < len(todo):
            spread(*todo[i])
        if i >= 1:
            pull(*todo[i - 1])

    done = jnp.concatenate([gq_old, done[...]], axis=1)
    xh, inverse = norm_stats(x[...].astype(F32))
    a = (xh * gain1[...] + shift1[...]).astype(BF16)
    gwqkv[...] += dot(a.T, done)
    ga = dot_nt(done, wqkv[...])
    gx_out[...] = (gmid[...] + norm_back(ga, xh, inverse, gain1[...])).astype(gx_out.dtype)
    sums[0] += row_sums(ga * xh)
    sums[1] += row_sums(ga)
    first = lax.rem(step + chunks_per_image - 1, chunks_per_image) == 0
    before = jnp.where(first, jnp.zeros(gtime.shape[1:], F32), gtime[0])
    summed = row_sums(done.astype(F32))
    gtime[0] = before + jnp.concatenate([summed[:, :width], summed[:, 2 * width :]], axis=1)

    @pl.when(step == chunks)
    def _():
        put_tiles(grads_out, 0, gwqkv)
        tiles = gwqkv.shape[1] // 128
        lines = attend_rows(width)[2]
        grads_out[tiles * width : tiles * width + lines, :] = gather_bias(gbias).astype(BF16)
        put_rows(
            grads_out,
            tiles * width + lines,
            [jnp.sum(sums[i], axis=0, keepdims=True) for i in range(2)],
        )
        used = attend_rows(width)[1]
        spare = grads_out.shape[0] - used
        if spare:
            grads_out[used:, :] = jnp.zeros((spare, 128), grads_out.dtype)


def attend_rows(width):
    lines = 2 * (width // 128) * (KWIN * 4 // QBLOCK) * 2
    small = -(-2 * width // 128 // 16) * 16
    return 3 * width // 128 * width, 3 * width // 128 * width + lines + small, lines


def attend_back(
    qkv,
    p,
    go,
    o,
    gmid,
    x,
    x_lead,
    chunks,
    chunks_per_image,
    layer,
    gain1,
    shift1,
    wqkv,
    own,
    part,
    links,
    number,
):
    width = x.shape[1]
    pairs = width // 128
    steps = chunks + 1
    halves = CHUNK // HALO

    def now(g):
        return jnp.minimum(g, chunks - 1)

    def late(g):
        return jnp.maximum(g - 1, 0)

    def rows(cols, lead, index):
        return pl.BlockSpec((CHUNK, cols), lambda g: (index(g) + lead, 0))

    images = chunks // chunks_per_image
    grad_rows = padded_rows(attend_rows(width)[1])
    in_specs = [
        pl.BlockSpec((HALO, 3 * width), lambda g: (jnp.maximum(halves * now(g) - 1, 0), 0)),
        rows(3 * width, 0, now),
        pl.BlockSpec(
            (HALO, 3 * width),
            lambda g: (jnp.minimum(halves * (now(g) + 1), halves * chunks - 1), 0),
        ),
        pl.BlockSpec((CHUNK // QBLOCK, pairs, KWIN, 2 * QBLOCK), lambda g: (now(g) + 1, 0, 0, 0)),
        pl.BlockSpec((CHUNK // QBLOCK, 8, 2 * QBLOCK), lambda g: (now(g) + 1, 0, 0)),
        pl.BlockSpec((None, width, CHUNK), lambda g: (now(g), 0, 0)),
        pl.BlockSpec((None, width, CHUNK), lambda g: (now(g) + 2, 0, 0)),
        rows(width, 0, late),
        rows(width, x_lead, late),
    ]
    in_specs += [layer_spec(w.shape, layer) for w in (gain1, shift1, wqkv)]
    out_specs = [
        rows(width, 1, lambda g: g),
        pl.BlockSpec((1, 8, 2 * width), lambda g: (late(g) // chunks_per_image, 0, 0)),
        const_spec((grad_rows, 128)),
    ]
    out_shape = [
        jax.ShapeDtypeStruct(((steps + 1) * CHUNK, width), F32),
        jax.ShapeDtypeStruct((images, 8, 2 * width), F32),
        jax.ShapeDtypeStruct((grad_rows, 128), BF16),
    ]
    scratch = [
        pltpu.VMEM((width, 3 * width), F32),
        pltpu.VMEM((pairs, KWIN, 2 * QBLOCK), F32),
        pltpu.VMEM((2, 8, width), F32),
        pltpu.VMEM((CHUNK, width), BF16),
        pltpu.VMEM((HALO, 2 * width), BF16),
        pltpu.VMEM((HALO, 2 * width), F32),
        pltpu.VMEM((HALO, 2 * width), F32),
        pltpu.VMEM((CHUNK, 2 * width), BF16),
        pltpu.VMEM((CHUNK // QBLOCK, pairs, KWIN, 2 * QBLOCK), BF16),
    ]
    kernel = functools.partial(attend_back_kernel, pairs, layer, chunks, chunks_per_image)
    if layer == 0:
        plan = link_plan()
        bs = plan[1]
        piece = min(part, CHUNK)
        pieces = CHUNK // piece
        kernel = functools.partial(
            last_attend_back_kernel, pairs, chunks, chunks_per_image, plan, own, part
        )
        out_specs[0] = pl.BlockSpec(memory_space=pl.ANY)
        out_shape[0] = jax.ShapeDtypeStruct((bs, own, part, width), BF16)
        scratch += [
            pltpu.VMEM((Pusher.SLOTS, CHUNK, width), BF16),
            pltpu.SemaphoreType.DMA((Pusher.SLOTS * pieces,)),
            pltpu.SemaphoreType.DMA((max((bs - 1) * own * (part // piece), 1),)),
            pltpu.SemaphoreType.DMA((Pusher.SLOTS * pieces,)),
        ]
    return pl.pallas_call(
        links.host(kernel, len(in_specs), len(out_specs), len(scratch)),
        grid=(steps,),
        in_specs=in_specs + links.specs,
        out_specs=out_specs + links.specs,
        out_shape=out_shape + links.shapes,
        scratch_shapes=scratch + links.scratch,
        compiler_params=links.params(number),
        name="attend_back",
    )(qkv, qkv, qkv, *p, go, o, gmid, x, gain1, shift1, wqkv, *links.arrays)


def final_kernel(plan, lanes_of_chunk, *refs):
    chunk, grad, extra = refs[:3]
    feed_out, attend_out, extra_out = refs[3:6]
    scratch = refs[6:]
    sems = Sems(*scratch[-3:])
    Places(plan).greet()
    lanes = [Lane(plan, sems) for _ in range(2)]
    collect_lane(lanes[0], scatter_lane(lanes[0], grad, scratch[:-3]), attend_out)
    extra_lane(lanes[1], extra, extra_out)
    for low, rows in runs_of(feed_out.shape[0], lanes_of_chunk):
        lane = Lane(plan, sems)
        devices = 2 * plan[0] * plan[1] * plan[2]
        collect_lane(lane, chunk_ends(chunk, low, rows, devices), feed_out.at[pl.ds(low, rows), :])
        lanes.append(lane)
    for i in range(max(len(lane.steps) for lane in lanes) + 1):
        for lane in lanes:
            if i <= len(lane.steps):
                lane.part(i)


def final_exchange(chunk, lanes_of_chunk, grad, extra):
    plan = link_plan()
    xs, bs, zs = plan
    devices = 2 * xs * bs * zs
    anywhere = pl.BlockSpec(memory_space=pl.ANY)
    here = pl.BlockSpec(memory_space=pltpu.VMEM)
    return pl.pallas_call(
        functools.partial(final_kernel, plan, lanes_of_chunk),
        in_specs=[here, anywhere, here],
        out_specs=[anywhere] * 3,
        out_shape=[
            jax.ShapeDtypeStruct((chunk.shape[0] * devices, 128), BF16),
            jax.ShapeDtypeStruct(grad.shape, BF16),
            jax.ShapeDtypeStruct((devices * extra.shape[0], 128), BF16),
        ],
        scratch_shapes=held_shapes(plan, grad.shape[0]) + sems_shapes(plan, 3 + lanes_of_chunk),
        compiler_params=pltpu.CompilerParams(
            vmem_limit_bytes=VMEM_BYTES, collective_id=0, has_side_effects=True
        ),
        name="final_exchange",
    )(chunk, grad, extra)


def unpack_kernel(layers, lines, *refs):
    ins = [refs[6 * i : 6 * i + 6] for i in range(layers)]
    w2_out, w1_out, attend_out, wo_out = refs[6 * layers : 6 * layers + 4]
    small_outs = refs[6 * layers + 4 : 6 * layers + 11]
    rows_out = refs[6 * layers + 11]
    width = w1_out.shape[1]
    for layer, (w2t, w1, attend, wo, feed_small, attend_small) in enumerate(ins):
        for j in range(w1.shape[0] // width):
            rows = slice(j * width, (j + 1) * width)
            cols = slice(j * 128, (j + 1) * 128)
            w2_out[layer, cols, :] = w2t[rows, :].astype(F32).T
            w1_out[layer, :, cols] = w1[rows, :].astype(F32)
            attend_out[layer, :, cols] = attend[rows, :].astype(F32)
            wo_out[layer, :, cols] = wo[rows, :].astype(F32)
        feed = feed_small[...].astype(F32)
        tail = attend_small[...].astype(F32)
        rows_out[layer] = tail[:lines]
        at = 0
        for out in small_outs[:5]:
            for j in range(out.shape[1] // 128):
                out[layer : layer + 1, j * 128 : (j + 1) * 128] = feed[at : at + 1]
                at += 1
        at = lines
        for out in small_outs[5:]:
            for j in range(out.shape[1] // 128):
                out[layer : layer + 1, j * 128 : (j + 1) * 128] = tail[at : at + 1]
                at += 1


def unpack(fulls, width, hidden):
    layers = len(fulls)
    wide = width // 128
    steps = hidden // width
    rows = wide * width
    last = 3 * width // width - 1
    block = (rows, 128)
    feed_big, feed_small = feed_rows(width, hidden)
    attend_big, attend_all, lines = attend_rows(width)
    attend_small = attend_all - attend_big
    while attend_big % attend_small:
        attend_small += 16
    assert feed_big % feed_small == 0

    def spec(first, top):
        return pl.BlockSpec(block, lambda g: (first + jnp.minimum(g, top), 0))

    ins = [
        spec(0, steps),
        spec(steps, steps),
        spec(0, last),
        spec(2 * steps, 0),
        pl.BlockSpec((feed_small, 128), lambda g: (feed_big // feed_small, 0)),
        pl.BlockSpec((attend_small, 128), lambda g: (attend_big // attend_small, 0)),
    ]
    vectors = [width] * 4 + [hidden] + [width] * 2
    return pl.pallas_call(
        functools.partial(unpack_kernel, layers, lines),
        grid=(steps,),
        in_specs=ins * layers,
        out_specs=[
            pl.BlockSpec((layers, width, width), lambda g: (0, g, 0)),
            pl.BlockSpec((layers, width, width), lambda g: (0, 0, g)),
            pl.BlockSpec((layers, width, width), lambda g: (0, 0, jnp.minimum(g, last))),
            pl.BlockSpec((layers, width, width), lambda g: (0, 0, 0)),
        ]
        + [pl.BlockSpec((layers, n), lambda g: (0, 0)) for n in vectors]
        + [pl.BlockSpec((layers, lines, 128), lambda g: (0, 0, 0))],
        out_shape=[
            jax.ShapeDtypeStruct((layers, hidden, width), F32),
            jax.ShapeDtypeStruct((layers, width, hidden), F32),
            jax.ShapeDtypeStruct((layers, width, 3 * width), F32),
            jax.ShapeDtypeStruct((layers, width, width), F32),
        ]
        + [jax.ShapeDtypeStruct((layers, n), F32) for n in vectors]
        + [jax.ShapeDtypeStruct((layers, lines, 128), F32)],
        compiler_params=pltpu.CompilerParams(vmem_limit_bytes=VMEM_BYTES),
        name="unpack",
    )(
        *[
            ref
            for feed, attend in fulls
            for ref in (
                feed,
                feed,
                attend,
                feed,
                feed,
                attend,
            )
        ]
    )


def time_embedding(timesteps, width):
    half_width = width // 2
    frequency = jnp.exp(
        jnp.arange(half_width, dtype=jnp.int32).astype(F32) * (-math.log(10000.0) / half_width)
    )
    angles = timesteps.astype(F32)[:, None] * frequency[None, :]
    return jnp.concatenate([jnp.sin(angles), jnp.cos(angles)], axis=-1)


def bias_rows(table, index_table, grid_cols):
    heads, entries = table.shape
    span = 2 * WIN + 1
    offsets = 2 * grid_cols - 1
    turned = index_table.reshape(span, offsets)[:, ::-1].reshape(entries)
    select = (turned[None, :] == jnp.arange(entries, dtype=jnp.int32)[:, None]).astype(F32)
    rows = jnp.dot(table, select, precision=EXACT).reshape(heads, span, offsets)
    key_rows = KWIN // grid_cols
    a0, a1, a2, a3 = [
        jnp.pad(
            rows, ((0, 0), (q, key_rows - span - q), (0, 0)), constant_values=NEG_FILL
        )
        for q in range(QBLOCK // grid_cols)
    ]
    gap = jnp.full((heads, key_rows, 1), NEG_FILL, F32)
    even = jnp.concatenate(
        [a0[..., grid_cols - 1 :], gap, a2, gap, a0[..., : grid_cols - 1]], axis=-1
    )
    odd = jnp.concatenate([gap, a1, gap, a3], axis=-1)
    return jnp.stack([even, odd], axis=1)


def spaced(parts, steps):
    return [i * (steps - 1) // (parts - 1) for i in range(parts)]


def body(
    tokens,
    cotangent,
    valid_mask,
    timesteps,
    index_table,
    first_gain,
    first_shift,
    attend_weight,
    time_weight,
    offset_bias,
    output_weight,
    output_bias,
    second_gain,
    second_shift,
    expand_weight,
    expand_bias,
    reduce_weight,
    reduce_bias,
):
    images, band_rows, grid_cols, width = tokens.shape
    layers = attend_weight.shape[0]
    bands = lax.axis_size("band")
    me = lax.axis_index("band")
    own = images // bands
    part = band_rows * grid_cols
    patches = bands * part
    per_image = patches // CHUNK
    chunks = own * per_image

    mine = lax.dynamic_slice_in_dim(valid_mask, me * own, own, 0).reshape(own, patches)
    fill = jnp.where(mine == 1, 0.0, NEG_FILL).astype(F32)
    fill = jnp.pad(fill, ((0, 0), (HALO, HALO)), constant_values=NEG_FILL)
    mask = jnp.stack(
        [fill[:, c * CHUNK : (c + 1) * CHUNK + 2 * HALO] for c in range(per_image)], axis=1
    ).reshape(chunks, 1, CHUNK + 2 * HALO)

    time_low = time_embedding(
        lax.dynamic_slice_in_dim(timesteps, me * own, own, 0), width
    ).astype(BF16)
    heads, entries = offset_bias.shape[1:]

    def make_rows(table):
        return bias_rows(table, index_table, grid_cols)

    biases, bias_pull = jax.vjp(make_rows, offset_bias.reshape(layers * heads, entries))
    biases = biases.reshape(layers, -1, QBLOCK)

    tp = jnp.einsum("it,ltc->lic", time_low, time_weight, preferred_element_type=F32)
    tproj = jnp.concatenate([tp[..., :width], jnp.zeros_like(tp[..., :width]), tp[..., width:]], -1)
    weights = (
        first_gain,
        first_shift,
        attend_weight,
        output_weight,
        output_bias,
        second_gain,
        second_shift,
        expand_weight,
        expand_bias,
        reduce_weight,
        reduce_bias,
    )
    x, x_lead = tokens.reshape(images * part, width), 0
    kept = []
    for layer in range(layers):
        last = layer == layers - 1
        jobs = []
        if last:
            shard = cotangent.reshape(images * part, width)
            jobs = [("images", shard, (own, part), [0, chunks // 2, chunks + 2])]
        qkv, p, inverse, o, mid, acts, nxt, *more = forward_layer(
            x,
            x_lead,
            chunks,
            per_image,
            tproj[layer][:, None, :],
            mask,
            biases,
            layer,
            weights,
            BF16 if last else F32,
            Links(jobs),
            own,
            part,
            1 + layer,
        )
        if layer == 0:
            x = more[0]
        if last:
            gx = more[-1]
        kept.append((x, x_lead, qkv, (p, inverse), o, mid, acts))
        x, x_lead = nxt, 2

    gx_lead = 0
    devices = bands * lax.axis_size("img")
    hidden = expand_weight.shape[2]
    fulls = [[None, None] for _ in range(layers)]
    extra = [time_low]
    attend_grads = feed_part = None
    result = x
    for layer in reversed(range(layers)):
        x, x_lead, qkv, p, o, mid, acts = kept[layer]
        steps = own * patches // FEED
        if layer == layers - 1:
            jobs = [("bands", result, (2 * CHUNK, own, part), [0, steps // 2, steps])]
        else:
            jobs = [("sum", attend_grads, [spaced(9, steps)])]
        gmid, go, feed_grads, *sent = feed_back(
            gx,
            gx_lead,
            own * patches,
            mid,
            acts,
            o,
            layer,
            second_gain,
            second_shift,
            expand_weight,
            reduce_weight,
            output_weight,
            Links(jobs),
            1 + layers + 2 * layer,
        )
        if layer == layers - 1:
            output = sent[0].reshape(tokens.shape)
        else:
            fulls[layer + 1] = [feed_part, sent[0]]
        gx, gtime, attend_grads, feed_part = attend_back(
            qkv,
            p,
            go,
            o,
            gmid,
            x,
            x_lead,
            chunks,
            per_image,
            layer,
            first_gain,
            first_shift,
            attend_weight,
            own,
            part,
            Links(
                [
                    ("sum", feed_grads, [spaced(9, chunks), [i + 1 for i in spaced(9, chunks)]])
                    if layer
                    else ("scatter", feed_grads, [spaced(6, chunks), [i + 1 for i in spaced(6, chunks)]])
                ]
            ),
            2 + layers + 2 * layer,
        )
        gx_lead = 1
        extra.append(jnp.sum(gtime, axis=1).astype(BF16))
    input_grad = gx.reshape(tokens.shape)

    extra = jnp.concatenate(extra, axis=1).reshape(-1, 128)
    lead = extra.shape[0]
    extra = jnp.pad(extra, ((0, -lead % 16), (0, 0)))
    *fulls[0], gathered = final_exchange(feed_part, 2, attend_grads, extra)
    gathered = gathered.reshape(devices, -1, 128)[:, :lead].reshape(devices * own, -1)
    grad_time = jnp.stack(
        [
            lax.dot_general(
                gathered[:, :width],
                gathered[:, width * (1 + 2 * turn) : width * (3 + 2 * turn)],
                (((0,), (0,)), ((), ())),
                preferred_element_type=F32,
            )
            for turn in reversed(range(layers))
        ]
    )
    (
        grad_reduce,
        grad_expand,
        grad_attend,
        grad_output,
        reduce_bias_grad,
        output_bias_grad,
        second_gain_grad,
        second_shift_grad,
        expand_bias_grad,
        first_gain_grad,
        first_shift_grad,
        grad_rows,
    ) = unpack(fulls, width, hidden)
    (grad_offset,) = bias_pull(grad_rows.reshape(layers * heads, 2, -1, QBLOCK))
    return (
        output,
        input_grad,
        first_gain_grad,
        first_shift_grad,
        grad_attend,
        grad_time,
        grad_offset.reshape(layers, heads, entries),
        grad_output,
        output_bias_grad,
        second_gain_grad,
        second_shift_grad,
        grad_expand,
        expand_bias_grad,
        grad_reduce,
        reduce_bias_grad,
    )


def solution(mesh):
    split = P("img", "band", None, None)
    placed = (split, split, P("img", None, None), P("img")) + (P(),) * 14
    return jax.shard_map(
        body,
        mesh=mesh,
        in_specs=placed,
        out_specs=(split, split) + (P(),) * 13,
        check_vma=False,
    )
```

```python
import functools
import math

import jax
import jax.numpy as jnp
from jax import lax
from jax.experimental import pallas as pl
from jax.experimental.pallas import tpu as pltpu
from jax.sharding import PartitionSpec as P

WIN = 4
CHUNK = 256
QBLOCK = 128
KWIN = 384
HALO = 128
FEED = 512

EXACT = lax.Precision.HIGHEST
NEG_FILL = -1000000000.0
EPSILON = 1e-06
LOG2E = math.log2(math.e)
GELU_A = math.sqrt(2.0 / math.pi)
GELU_B = 0.044715 * GELU_A
VMEM_BYTES = 58 * 1024 * 1024

F32 = jnp.float32
BF16 = jnp.bfloat16


def dot(a, b):
    return jnp.dot(a, b, preferred_element_type=F32)


def dot_nt(a, b):
    return lax.dot_general(a, b, (((1,), (1,)), ((), ())), preferred_element_type=F32)


def norm_stats(v):
    mean = jnp.mean(v, axis=-1, keepdims=True)
    centered = v - mean
    inverse = lax.rsqrt(jnp.mean(centered * centered, axis=-1, keepdims=True) + EPSILON)
    return centered * inverse, inverse


def norm_back(gy, xh, inverse, gain):
    gs = gy * gain
    return inverse * (
        gs - jnp.mean(gs, axis=-1, keepdims=True) - xh * jnp.mean(gs * xh, axis=-1, keepdims=True)
    )


def row_sums(v):
    rows, cols = v.shape
    return jnp.sum(v.reshape(rows // 8, 8, cols), axis=0)


def split_heads(block):
    lane = lax.broadcasted_iota(jnp.int32, block.shape, 1)
    zero = jnp.zeros_like(block)
    first = lane < block.shape[1] // 2
    return jnp.concatenate(
        [jnp.where(first, block, zero), jnp.where(first, zero, block)], axis=0
    )


def join_heads(product):
    half = product.shape[0] // 2
    width = product.shape[1] // 2
    return jnp.concatenate([product[:half, :width], product[half:, width:]], axis=0).T


def share_rows(rows):
    return max(n for n in range(16, 257, 16) if rows % n == 0)


def add_rows(total, at, others, rows):
    share = share_rows(rows)

    def one(i, carry):
        low = pl.multiple_of(i * share, 16)
        here = pl.ds(pl.multiple_of(at + low, 16), share)
        v = total[here, :].astype(F32)
        for ref, row in others:
            v = v + ref[pl.ds(pl.multiple_of(row + low, 16), share), :].astype(F32)
        total[here, :] = v.astype(total.dtype)
        return carry

    lax.fori_loop(0, rows // share, one, 0)


def cut(ref, at, rows):
    return ref.at[pl.ds(pl.multiple_of(at, 16), rows), :]


def both(first, second):
    first()
    second()


def dispatch(step, acts):
    whens = sorted(acts)
    if len(whens) <= 1:
        for when in whens:
            pl.when(step == when)(acts[when])
        return
    middle = whens[len(whens) // 2]
    low = {when: acts[when] for when in whens if when < middle}
    high = {when: acts[when] for when in whens if when >= middle}
    pl.when(step < middle)(lambda: dispatch(step, low))
    pl.when(step >= middle)(lambda: dispatch(step, high))


def mod(v, n):
    return jnp.bitwise_and(v, n - 1) if n & (n - 1) == 0 else lax.rem(v, n)


def halved(v, n):
    return jnp.right_shift(v, n.bit_length() - 1) if n & (n - 1) == 0 else v // n


class Places:
    def __init__(self, plan):
        self.xs, self.bs, self.zs = plan
        self.img = lax.axis_index("img")
        self.b = lax.axis_index("band")
        self.c = mod(self.img, 2)
        self.x = mod(halved(self.img, 2), self.xs)
        self.z = halved(self.img, 2 * self.xs)

    def core(self, by):
        return (self.img + 1 - 2 * self.c, self.b)

    def along_x(self, by):
        return ((self.z * self.xs + mod(self.x + by, self.xs)) * 2 + self.c, self.b)

    def along_b(self, by):
        return (self.img, mod(self.b + by, self.bs))

    def along_z(self, by):
        return ((mod(self.z + by, self.zs) * self.xs + self.x) * 2 + self.c, self.b)

    def greet(self):
        barrier = pltpu.get_barrier_semaphore()
        peers = [self.core(1)]
        peers += [self.along_x(by) for by in range(1, self.xs)]
        peers += [self.along_b(by) for by in range(1, self.bs)]
        peers += [self.along_z(by) for by in range(1, self.zs)]
        for peer in peers:
            pl.semaphore_signal(barrier, inc=1, device_id=peer, device_id_type=pl.DeviceIdType.MESH)
        pl.semaphore_wait(barrier, len(peers))


class Lane:
    def __init__(self, plan, sems):
        self.plan, self.sems, self.steps = plan, sems, []

    def add(self, copies, then=None):
        count = [0, 0]
        here = Places(self.plan)
        for src, dst, peer in copies(here):
            count[peer is None] += 1
        base = (self.sems.sent, self.sems.kept)
        self.sems.sent += count[0]
        self.sems.kept += count[1]
        self.steps.append((copies, then, base))

    def described(self, step):
        copies, _, (sent, kept) = self.steps[step]
        made = []
        for src, dst, peer in copies(Places(self.plan)):
            if peer is None:
                made.append(pltpu.make_async_copy(src, dst, self.sems.own.at[kept]))
                kept += 1
            else:
                made.append(
                    pltpu.make_async_remote_copy(
                        src_ref=src,
                        dst_ref=dst,
                        send_sem=self.sems.send.at[sent],
                        recv_sem=self.sems.recv.at[sent],
                        device_id=peer,
                        device_id_type=pl.DeviceIdType.MESH,
                    )
                )
                sent += 1
        return made

    def part(self, i):
        if i > 0:
            for copy in self.described(i - 1):
                copy.wait()
            if self.steps[i - 1][1] is not None:
                self.steps[i - 1][1](Places(self.plan))
        if i < len(self.steps):
            for copy in self.described(i):
                copy.start()


class Sems:
    def __init__(self, send, recv, own):
        self.send, self.recv, self.own = send, recv, own
        self.sent = self.kept = 0


def scatter_lane(lane, grad, held, chunk=None):
    acc, r1, r2a, r2b, r3a, r3b, r4 = held
    xs, bs, zs = lane.plan
    half = grad.shape[0] // 2
    quarter = half // 2
    nx, nb, n2 = quarter // xs, quarter // bs, quarter // (xs * bs)
    n = n2 // zs

    def core_copies(at):
        return [
            (cut(grad, at.c * half, half), acc, None),
            (cut(grad, half - at.c * half, half), r1, at.core(1)),
        ]

    lane.add(core_copies, lambda at: add_rows(acc, 0, [(r1, 0)], half))

    def wide_copies(at):
        made = []
        for by in range(1, xs):
            there = mod(at.x + by, xs)
            made.append((cut(acc, there * nx, nx), cut(r2a, (by - 1) * nx, nx), at.along_x(by)))
        for by in range(1, bs):
            there = quarter + mod(at.b + by, bs) * nb
            made.append((cut(acc, there, nb), cut(r2b, (by - 1) * nb, nb), at.along_b(by)))
        return made

    def wide_add(at):
        add_rows(acc, at.x * nx, [(r2a, k * nx) for k in range(xs - 1)], nx)
        add_rows(acc, quarter + at.b * nb, [(r2b, k * nb) for k in range(bs - 1)], nb)

    lane.add(wide_copies, wide_add)

    def cross_copies(at):
        made = []
        for by in range(1, bs):
            there = at.x * nx + mod(at.b + by, bs) * n2
            made.append((cut(acc, there, n2), cut(r3a, (by - 1) * n2, n2), at.along_b(by)))
        for by in range(1, xs):
            there = quarter + at.b * nb + mod(at.x + by, xs) * n2
            made.append((cut(acc, there, n2), cut(r3b, (by - 1) * n2, n2), at.along_x(by)))
        return made

    def plane(at):
        return at.x * nx + at.b * n2, quarter + at.b * nb + at.x * n2

    def cross_add(at):
        first, second = plane(at)
        add_rows(acc, first, [(r3a, k * n2) for k in range(bs - 1)], n2)
        add_rows(acc, second, [(r3b, k * n2) for k in range(xs - 1)], n2)

    lane.add(cross_copies, cross_add)

    def deep_copies(at):
        made = []
        for by in range(1, zs):
            there = mod(at.z + by, zs) * n
            for k, low in enumerate(plane(at)):
                slot = (2 * (by - 1) + k) * n
                made.append((cut(acc, low + there, n), cut(r4, slot, n), at.along_z(by)))
        return made

    def deep_add(at):
        for k, low in enumerate(plane(at)):
            add_rows(acc, low + at.z * n, [(r4, (2 * i + k) * n) for i in range(zs - 1)], n)

    lane.add(deep_copies, deep_add)

    def ends(at):
        return [cut(acc, low + at.z * n, n) for low in plane(at)]

    if chunk is None:
        return ends
    lane.add(lambda at: [(ref, cut(chunk, k * n, n), None) for k, ref in enumerate(ends(at))])


def collect_lane(lane, ends, out):
    xs, bs, zs = lane.plan
    half = out.shape[0] // 2
    quarter = half // 2
    nx, nb, n2 = quarter // xs, quarter // bs, quarter // (xs * bs)
    n = n2 // zs

    def plane(at):
        base = at.c * half
        return base + at.x * nx + at.b * n2, base + quarter + at.b * nb + at.x * n2

    def deep(at):
        made = []
        for ref, low in zip(ends(at), plane(at)):
            there = cut(out, low + at.z * n, n)
            made.append((ref, there, None))
            made += [(ref, there, at.along_z(by)) for by in range(1, zs)]
        return made

    def cross(at):
        first, second = plane(at)
        a, b = cut(out, first, n2), cut(out, second, n2)
        made = [(a, a, at.along_b(by)) for by in range(1, bs)]
        return made + [(b, b, at.along_x(by)) for by in range(1, xs)]

    def wide(at):
        a = cut(out, at.c * half + at.x * nx, nx)
        b = cut(out, at.c * half + quarter + at.b * nb, nb)
        made = [(a, a, at.along_x(by)) for by in range(1, xs)]
        return made + [(b, b, at.along_b(by)) for by in range(1, bs)]

    def core(at):
        whole = cut(out, at.c * half, half)
        return [(whole, whole, at.core(1))]

    for copies in (deep, cross, wide, core):
        lane.add(copies)


def extra_lane(lane, extra, out):
    xs, bs, zs = lane.plan
    rows = extra.shape[0]

    def deep(at):
        there = cut(out, (((at.c * xs + at.x) * bs + at.b) * zs + at.z) * rows, rows)
        return [(extra, there, None)] + [(extra, there, at.along_z(by)) for by in range(1, zs)]

    def cross(at):
        there = cut(out, ((at.c * xs + at.x) * bs + at.b) * zs * rows, zs * rows)
        return [(there, there, at.along_b(by)) for by in range(1, bs)]

    def wide(at):
        there = cut(out, (at.c * xs + at.x) * bs * zs * rows, bs * zs * rows)
        return [(there, there, at.along_x(by)) for by in range(1, xs)]

    def core(at):
        there = cut(out, at.c * xs * bs * zs * rows, xs * bs * zs * rows)
        return [(there, there, at.core(1))]

    for copies in (deep, cross, wide, core):
        lane.add(copies)


def link_plan():
    pairs = lax.axis_size("img") // 2
    xs = 2 if pairs % 2 == 0 else 1
    return xs, lax.axis_size("band"), pairs // xs


def padded_rows(rows):
    xs, bs, zs = link_plan()
    return -(-rows // (64 * xs * bs * zs)) * (64 * xs * bs * zs)


def held_shapes(plan, rows):
    xs, bs, zs = plan
    quarter = rows // 4
    sizes = [
        rows // 2,
        rows // 2,
        (xs - 1) * quarter // xs,
        (bs - 1) * quarter // bs,
        (bs - 1) * quarter // (xs * bs),
        (xs - 1) * quarter // (xs * bs),
        (zs - 1) * 2 * quarter // (xs * bs * zs),
    ]
    return [pltpu.VMEM((max(n, 16), 128), BF16) for n in sizes]


def sems_shapes(plan, lanes, moved=0):
    xs, bs, zs = plan
    count = lanes * (1 + 2 * (xs - 1 + bs - 1) + 2 * (zs - 1)) + moved
    return [
        pltpu.SemaphoreType.DMA((count,)),
        pltpu.SemaphoreType.DMA((count,)),
        pltpu.SemaphoreType.DMA((2 * lanes + moved + 1,)),
    ]


def images_copies(shard, at, own, part, images):
    made = []
    for by in range(at.bs):
        there = mod(at.b + by, at.bs)
        for i in images:
            made.append(((there * own + i) * part, (i * at.bs + at.b) * part, by))
    return made


def runs_of(rows, lanes):
    unit = padded_rows(1)
    units = rows // unit
    lanes = min(lanes, units)
    ends = [units * i // lanes * unit for i in range(lanes + 1)]
    return [(low, high - low) for low, high in zip(ends, ends[1:])]


def chunk_ends(chunk, low, rows, devices):
    low, half = low // devices, rows // devices // 2
    return lambda at: [cut(chunk, low + k * half, half) for k in range(2)]


def load_lane(lane, chunk, here, low, rows, devices):
    part = pl.ds(low // devices, rows // devices)
    lane.add(lambda at: [(chunk.at[part, :], here.at[part, :], None)])


class Links:
    def __init__(self, jobs):
        self.jobs = jobs
        self.plan = link_plan()
        xs, bs, zs = self.plan
        self.devices = 2 * xs * bs * zs
        self.arrays = [job[1] for job in jobs]
        self.shapes, self.scratch = [], []
        remote = local = 0
        for job in jobs:
            if job[0] in ("sum", "scatter", "collect"):
                rows_all = job[1].shape[0] * (self.devices if job[0] == "collect" else 1)
                for _, rows in runs_of(rows_all, len(job[-1])):
                    if job[0] != "collect":
                        self.scratch += held_shapes(self.plan, rows)
                    remote += 2 * (1 + 2 * (xs - 1 + bs - 1) + 2 * (zs - 1))
                    local += 4
                if job[0] == "collect":
                    self.scratch.append(pltpu.VMEM(job[1].shape, BF16))
                if job[0] == "scatter":
                    rows_all //= self.devices
                self.shapes.append(jax.ShapeDtypeStruct((rows_all, 128), BF16))
                continue
            width = job[1].shape[1]
            own, part = job[2][-2:]
            shape = (bs, own, part, width) if job[0] == "bands" else (own * bs * part, width)
            self.shapes.append(jax.ShapeDtypeStruct(shape, BF16))
            self.scratch.append(pltpu.VMEM((own, part, width), BF16))
            remote += (bs - 1) * own
            local += 2 * own
        if jobs:
            self.scratch += [
                pltpu.SemaphoreType.DMA((max(remote, 1),)),
                pltpu.SemaphoreType.DMA((max(remote, 1),)),
                pltpu.SemaphoreType.DMA((local,)),
            ]
        self.specs = [pl.BlockSpec(memory_space=pl.ANY)] * len(jobs)

    def host(self, kernel, ins, outs, scratch):
        def run(*refs):
            count = len(self.jobs)
            a, b, c = ins, ins + count, ins + count + outs
            d, e = c + count, c + count + scratch
            step = pl.program_id(0)
            acts = kernel(*refs[:a], *refs[b:c], *refs[d:e]) or {}
            if self.jobs:
                parts = self.parts(refs[a:b], refs[c:d], refs[e:])
                parts.setdefault(0, [])
                for when in sorted(parts):

                    def act(when=when):
                        if when == 0:
                            Places(self.plan).greet()
                        for lane, part in parts[when]:
                            lane.part(part)

                    at = min(when, pl.num_programs(0) - 1)
                    before = acts.get(at)
                    acts[at] = act if before is None else functools.partial(both, before, act)
            dispatch(step, acts)

        return run

    def parts(self, given, made, scratch):
        sems = Sems(*scratch[-3:])
        held = list(scratch[:-3])
        parts = {}
        lanes = []
        for job, ref, out in zip(self.jobs, given, made):
            if job[0] == "sum":
                for (low, rows), whens in zip(runs_of(ref.shape[0], len(job[-1])), job[-1]):
                    lane = Lane(self.plan, sems)
                    part_in, part_out = ref.at[pl.ds(low, rows), :], out.at[pl.ds(low, rows), :]
                    collect_lane(lane, scatter_lane(lane, part_in, held[:7]), part_out)
                    held = held[7:]
                    lanes.append((lane, whens))
                continue
            if job[0] == "scatter":
                for (low, rows), whens in zip(runs_of(ref.shape[0], len(job[-1])), job[-1]):
                    lane = Lane(self.plan, sems)
                    few = rows // self.devices
                    chunk = out.at[pl.ds(low // self.devices, few), :]
                    scatter_lane(lane, ref.at[pl.ds(low, rows), :], held[:7], chunk)
                    held = held[7:]
                    lanes.append((lane, whens))
                continue
            if job[0] == "collect":
                here = held[0]
                held = held[1:]
                for (low, rows), whens in zip(runs_of(out.shape[0], len(job[-1])), job[-1]):
                    lane = Lane(self.plan, sems)
                    load_lane(lane, ref, here, low, rows, self.devices)
                    ends = chunk_ends(here, low, rows, self.devices)
                    collect_lane(lane, ends, out.at[pl.ds(low, rows), :])
                    lanes.append((lane, whens))
                continue
            own, part = job[2][-2:]
            lead = job[2][0] if job[0] == "bands" else 0

            def copies(at, kind=job[0], ref=ref, out=out, own=own, part=part, lead=lead):
                made = []
                for i in range(own):
                    for by in range(self.plan[1]):
                        there = mod(at.b + by, self.plan[1])
                        if kind == "bands":
                            src = cut(ref, lead + (i * self.plan[1] + there) * part, part)
                            dst = out.at[at.b, i]
                        else:
                            src = cut(ref, (there * own + i) * part, part)
                            dst = cut(out, (i * self.plan[1] + at.b) * part, part)
                        made.append((i, src, dst, at.along_b(by) if by else None))
                return made

            lane = Lane(self.plan, sems)
            lane.add(lambda at, f=copies: [c[1:] for c in f(at) if c[3] is not None])
            lanes.append((lane, [job[-1][0], job[-1][-1]]))
            lane = Lane(self.plan, sems)
            here = held[0]
            held = held[1:]
            lane.add(lambda at, f=copies, h=here: [(c[1], h.at[c[0]], None) for c in f(at) if c[3] is None])
            lane.add(lambda at, f=copies, h=here: [(h.at[c[0]], c[2], None) for c in f(at) if c[3] is None])
            lanes.append((lane, job[-1]))
        for lane, whens in lanes:
            assert len(whens) == len(lane.steps) + 1
            for part, when in enumerate(whens):
                parts.setdefault(when, []).append((lane, part))
        return parts

    def params(self, number):
        if not self.jobs:
            return pltpu.CompilerParams(vmem_limit_bytes=VMEM_BYTES)
        return pltpu.CompilerParams(
            vmem_limit_bytes=VMEM_BYTES, collective_id=number, has_side_effects=True
        )


def fold(v, op):
    return op(v.reshape(v.shape[0] // 8, 8, v.shape[1]), axis=0)


def unroll_bias(rows, bias):
    pairs, keys, lanes = bias.shape
    grid_cols = QBLOCK // 4
    key_rows = keys // grid_cols
    lane = lax.broadcasted_iota(jnp.int32, (grid_cols, QBLOCK), 1)
    even = lax.rem(lane // grid_cols, 2) == 0
    for pair in range(pairs):
        for head in range(2):
            for key_row in range(key_rows):
                turned = [
                    pltpu.roll(
                        jnp.broadcast_to(
                            rows[pl.ds(((pair * 2 + head) * 2 + odd) * key_rows + key_row, 1), :],
                            (grid_cols, QBLOCK),
                        ),
                        0,
                        1,
                        stride=1,
                        stride_axis=0,
                    )
                    for odd in range(2)
                ]
                bias[
                    pair,
                    key_row * grid_cols : (key_row + 1) * grid_cols,
                    head * QBLOCK : (head + 1) * QBLOCK,
                ] = jnp.where(even, turned[0], turned[1])


def gather_bias(grads):
    pairs, keys, lanes = grads.shape
    grid_cols = QBLOCK // 4
    lane = lax.broadcasted_iota(jnp.int32, (keys, QBLOCK), 1)
    column = lax.rem(lax.broadcasted_iota(jnp.int32, (keys, QBLOCK), 0), grid_cols)
    parity = lax.rem(lane // grid_cols, 2)
    sums = []
    for pair in range(pairs):
        for head in range(2):
            for odd in range(2):
                v = grads[pair, :, head * QBLOCK : (head + 1) * QBLOCK]
                v = jnp.where(parity == odd, v, 0.0)
                for bit in (1, 2, 4, 8, 16):
                    turned = pltpu.roll(v, QBLOCK - bit, 1)
                    v = jnp.where(lax.rem(column // bit, 2) == 1, turned, v)
                sums.append(jnp.sum(v.reshape(keys // grid_cols, grid_cols, QBLOCK), axis=1))
    return jnp.concatenate(sums, axis=0)


def low_of(value):
    return jnp.asarray(value, BF16)


def forward_kernel(
    pairs,
    layer,
    x_new,
    x_old,
    tproj,
    mask,
    bias_rows,
    gain1,
    shift1,
    wqkv,
    wo,
    bo,
    gain2,
    shift2,
    w1,
    b1,
    w2,
    b2,
    qkv_out,
    p_out,
    inverse_out,
    o_out,
    mid_out,
    acts_out,
    x_out,
    bias,
    q_ring,
    k_ring,
    vt_ring,
    o_ring,
    s_scr,
):
    step = pl.program_id(0)
    width = x_new.shape[1]
    gain1, shift1, bo, gain2, shift2, b1, b2 = [
        ref.at[pl.ds(layer, 1), :] for ref in (gain1, shift1, bo, gain2, shift2, b1, b2)
    ]

    @pl.when(step == 0)
    def _():
        unroll_bias(bias_rows, bias)
        q_ring[...] = jnp.zeros_like(q_ring)
        k_ring[...] = jnp.zeros_like(k_ring)
        vt_ring[...] = jnp.zeros_like(vt_ring)
        o_ring[...] = jnp.zeros_like(o_ring)

    act_out, slope_out = acts_out.at[0], acts_out.at[1]
    attended = o_ring[...]
    mid = x_old[...].astype(F32) + (dot(attended, wo[...]) + bo[...])
    mid_out[...] = mid
    xh2, _ = norm_stats(mid)
    c = (xh2 * gain2[...] + shift2[...]).astype(BF16)
    parts = 2 * pairs
    tile = w1.shape[1] // parts

    def feed(part):
        cols = slice(part * tile, (part + 1) * tile)
        whole = dot(c, w1[:, cols])
        for low in range(0, CHUNK, 64):
            u = (whole[low : low + 64] + b1[:, cols]).astype(BF16)
            u2 = u * u
            t = jnp.tanh(u * (low_of(GELU_A) + low_of(GELU_B) * u2))
            h = low_of(0.5) + low_of(0.5) * t
            e = u * h
            act_out[low : low + 64, cols] = e
            slope_out[low : low + 64, cols] = h + (e * (low_of(1.0) - t)) * (
                low_of(GELU_A) + low_of(3.0 * GELU_B) * u2
            )

    queries = q_ring[...]
    xh1, _ = norm_stats(x_new[...].astype(F32))
    a = (xh1 * gain1[...] + shift1[...]).astype(BF16)
    projected = dot(a, wqkv[...]) + tproj[0]
    qkv = projected.astype(BF16)
    qkv_out[...] = qkv
    q_ring[...] = (projected[:, :width] * (0.125 * LOG2E)).astype(BF16)
    k_ring[:HALO, :] = k_ring[CHUNK : CHUNK + HALO, :]
    k_ring[HALO : HALO + CHUNK, :] = k_ring[HALO + CHUNK :, :]
    k_ring[HALO + CHUNK :, :] = qkv[:, width : 2 * width]
    vt_ring[:, :HALO] = vt_ring[:, CHUNK : CHUNK + HALO]
    vt_ring[:, HALO : HALO + CHUNK] = vt_ring[:, HALO + CHUNK :]
    vt_ring[:, HALO + CHUNK :] = qkv[:, 2 * width :].T

    key_index = lax.broadcasted_iota(jnp.int32, (KWIN, QBLOCK), 0)
    query_index = lax.broadcasted_iota(jnp.int32, (KWIN, QBLOCK), 1)
    diagonal = key_index == query_index + HALO
    extras = []
    for blk in range(CHUNK // QBLOCK):
        line = mask[0, :, blk * QBLOCK : blk * QBLOCK + KWIN]
        column = jnp.broadcast_to(line, (QBLOCK, KWIN)).T
        extras.append(jnp.where(diagonal, 0.0, column))
    todo = [(blk, pair) for blk in range(CHUNK // QBLOCK) for pair in range(pairs)]
    cells = [(k * 128, h * 128) for k in range(KWIN // 128) for h in range(2)]
    tops = {}

    def score(blk, pair):
        low = blk * QBLOCK
        feat = slice(pair * 128, (pair + 1) * 128)
        split_q = split_heads(queries[low : low + QBLOCK, feat])
        best = [None, None]
        for k in range(0, KWIN, 128):
            s = dot_nt(k_ring[low + k : low + k + 128, feat], split_q)
            for h in range(2):
                lane = slice(h * 128, h * 128 + 128)
                v = s[:, lane] + bias[pair, k : k + 128, lane] + extras[blk][k : k + 128]
                s_scr[blk, pair, k : k + 128, lane] = v
                top = fold(v, jnp.max)
                best[h] = top if best[h] is None else jnp.maximum(best[h], top)
        tops[blk, pair] = [jnp.max(v, axis=0, keepdims=True) for v in best]

    def soften(blk, pair):
        for k, lane in cells:
            at = (blk, pair, slice(k, k + 128), slice(lane, lane + 128))
            p_out[at] = jnp.exp2(s_scr[at] - tops[blk, pair][lane // 128]).astype(BF16)

    ones = jnp.ones((16, KWIN), BF16)

    def attend(blk, pair):
        low = blk * QBLOCK
        feat = slice(pair * 128, (pair + 1) * 128)
        left = jnp.concatenate([vt_ring[feat, low : low + KWIN], ones], axis=0)
        sums = dot(left, p_out[blk, pair])
        inverse = 1.0 / sums[128:129]
        inverse_out[blk, pair : pair + 1, :] = inverse
        o_t = jnp.concatenate(
            [sums[:64, :128] * inverse[:, :128], sums[64:128, 128:] * inverse[:, 128:]], axis=0
        ).astype(BF16)
        o_out[feat, low : low + QBLOCK] = o_t
        o_ring[low : low + QBLOCK, feat] = o_t.T

    for i in range(len(todo) + 2):
        if i < len(todo):
            score(*todo[i])
            feed(i)
        if 1 <= i <= len(todo):
            soften(*todo[i - 1])
        if i >= 2:
            attend(*todo[i - 2])
    x_out[...] = (mid_out[...] + (dot(act_out[...], w2[...]) + b2[...])).astype(x_out.dtype)


def const_spec(shape):
    zeros = (0,) * len(shape)
    return pl.BlockSpec(shape, lambda g: zeros, pipeline_mode=pl.Buffered(1))


def layer_spec(shape, layer):
    if len(shape) == 2:
        return const_spec(shape)
    index = (layer,) + (0,) * (len(shape) - 1)
    return pl.BlockSpec((None,) + shape[1:], lambda g: index, pipeline_mode=pl.Buffered(1))


def first_forward_kernel(pairs, plan, chunks, own, part, shard, *refs):
    ins, outs, scratch = refs[:14], refs[14:22], refs[22:]
    x_all, send_sems, recv_sems, own_sems = scratch[-4:]
    step = pl.program_id(0)
    sems = Sems(send_sems, recv_sems, own_sems)
    lanes = []
    for i in range(own):
        lane = Lane(plan, sems)

        def copies(at, i=i):
            return [
                (cut(shard, src, part), cut(x_all, dst, part), at.along_b(by) if by else None)
                for src, dst, by in images_copies(shard, at, own, part, (i,))
            ]

        lane.add(copies)
        lanes.append(lane)
    for i in range(own):

        @pl.when(step == i * (chunks // own))
        def _(i=i):
            if i == 0:
                Places(plan).greet()
                for lane in lanes:
                    lane.part(0)
            lanes[i].part(1)

    def chunk(lead):
        at = jnp.clip(step - lead, 0, chunks - 1) * CHUNK
        return x_all.at[pl.ds(pl.multiple_of(at, CHUNK), CHUNK), :]

    x_copy = outs[-1]
    x_copy[...] = chunk(0)[...]
    forward_kernel(pairs, 0, chunk(0), chunk(2), *ins, *outs[:-1], *scratch[:-4])


def forward_layer(
    x, x_lead, chunks, chunks_per_image, tproj, mask, bias_rows, layer, weights, out_dtype, links, own, part, number
):
    width = x.shape[1]
    hidden = weights[7].shape[2]
    pairs = width // 128
    steps = chunks + 2
    first = layer == 0

    def at(lead, least=0):
        def index(g):
            return jnp.clip(g - lead, least, chunks - 1)

        return index

    new_at, attn_at, old_at = at(0), at(1), at(2)
    row = pl.BlockSpec((CHUNK, width), lambda g: (g, 0))
    rows = steps * CHUNK
    if first:
        x_specs, x_args = [pl.BlockSpec(memory_space=pl.ANY)], [x]
    else:
        x_specs = [
            pl.BlockSpec((CHUNK, width), lambda g: (new_at(g) + x_lead, 0)),
            pl.BlockSpec((CHUNK, width), lambda g: (old_at(g) + x_lead, 0)),
        ]
        x_args = [x, x]
    in_specs = x_specs + [
        pl.BlockSpec((1, 1, 3 * width), lambda g: (new_at(g) // chunks_per_image, 0, 0)),
        pl.BlockSpec((1, 1, CHUNK + 2 * HALO), lambda g: (attn_at(g), 0, 0)),
        layer_spec(bias_rows.shape, layer),
    ]
    in_specs += [layer_spec(w.shape, layer) for w in weights]
    out_specs = [
        pl.BlockSpec((CHUNK, 3 * width), lambda g: (new_at(g), 0)),
        pl.BlockSpec((CHUNK // QBLOCK, pairs, KWIN, 2 * QBLOCK), lambda g: (g, 0, 0, 0)),
        pl.BlockSpec((CHUNK // QBLOCK, 8, 2 * QBLOCK), lambda g: (g, 0, 0)),
        pl.BlockSpec((None, width, CHUNK), lambda g: (g + 1, 0, 0)),
        row,
        pl.BlockSpec((None, 2, CHUNK, hidden), lambda g: (g, 0, 0, 0)),
        row,
    ]
    out_shape = [
        jax.ShapeDtypeStruct((chunks * CHUNK, 3 * width), BF16),
        jax.ShapeDtypeStruct((steps * (CHUNK // QBLOCK), pairs, KWIN, 2 * QBLOCK), BF16),
        jax.ShapeDtypeStruct((steps * (CHUNK // QBLOCK), 8, 2 * QBLOCK), F32),
        jax.ShapeDtypeStruct((steps + 2, width, CHUNK), BF16),
        jax.ShapeDtypeStruct((rows, width), F32),
        jax.ShapeDtypeStruct((steps, 2, CHUNK, hidden), BF16),
        jax.ShapeDtypeStruct((rows, width), out_dtype),
    ]
    scratch = [
        pltpu.VMEM((pairs, KWIN, 2 * QBLOCK), F32),
        pltpu.VMEM((CHUNK, width), BF16),
        pltpu.VMEM((HALO + 2 * CHUNK, width), BF16),
        pltpu.VMEM((width, HALO + 2 * CHUNK), BF16),
        pltpu.VMEM((CHUNK, width), BF16),
        pltpu.VMEM((CHUNK // QBLOCK, pairs, KWIN, 2 * QBLOCK), F32),
    ]
    params = links.params(number)
    if first:
        plan = link_plan()
        remote = max((plan[1] - 1) * own, 1)
        kernel = functools.partial(first_forward_kernel, pairs, plan, chunks, own, part)
        out_specs.append(pl.BlockSpec((CHUNK, width), lambda g: (new_at(g), 0)))
        out_shape.append(jax.ShapeDtypeStruct((chunks * CHUNK, width), BF16))
        scratch += [
            pltpu.VMEM((chunks * CHUNK, width), BF16),
            pltpu.SemaphoreType.DMA((remote,)),
            pltpu.SemaphoreType.DMA((remote,)),
            pltpu.SemaphoreType.DMA((own,)),
        ]
        params = pltpu.CompilerParams(
            vmem_limit_bytes=VMEM_BYTES, collective_id=number, has_side_effects=True
        )
    else:
        kernel = links.host(
            functools.partial(forward_kernel, pairs, layer), len(in_specs), len(out_specs), len(scratch)
        )
    return pl.pallas_call(
        kernel,
        grid=(steps,),
        in_specs=in_specs + links.specs,
        out_specs=out_specs + links.specs,
        out_shape=out_shape + links.shapes,
        scratch_shapes=scratch + links.scratch,
        compiler_params=params,
        name="block_forward",
    )(*x_args, tproj, mask, bias_rows, *weights, *links.arrays)


def put_tiles(out, first, acc):
    width = acc.shape[0]
    for j in range(acc.shape[1] // 128):
        at = (first + j) * width
        out[at : at + width, :] = acc[:, j * 128 : (j + 1) * 128].astype(out.dtype)


def put_rows(out, at, vectors):
    lines = [v[:, j : j + 128] for v in vectors for j in range(0, v.shape[1], 128)]
    lines += [jnp.zeros((1, 128), F32)] * (-len(lines) % 16)
    out[at : at + len(lines), :] = jnp.concatenate(lines, axis=0).astype(out.dtype)


def feed_back_kernel(
    layer,
    gx,
    mid,
    acts,
    o,
    gain2,
    shift2,
    w1,
    w2,
    wo,
    gmid_out,
    go_out,
    grads_out,
    gw2t,
    gw1,
    gwo,
    sums,
    gb1,
    gu_scr,
):
    step = pl.program_id(0)
    gain2, shift2 = [ref.at[pl.ds(layer, 1), :] for ref in (gain2, shift2)]

    @pl.when(step == 0)
    def _():
        for ref in (gw2t, gw1, gwo, sums, gb1):
            ref[...] = jnp.zeros_like(ref)

    grad = gx[...].astype(F32)
    gr = grad.astype(BF16)
    gr_t = gr.T
    xh, inverse = norm_stats(mid[...])
    c_t = (xh * gain2[...] + shift2[...]).astype(BF16).T
    hidden = acts.shape[3]
    halves = acts.shape[0]
    tile = 256
    for low in range(0, hidden, tile):
        cols = slice(low, low + tile)
        ge = dot_nt(gr, w2[cols, :])
        slope = jnp.concatenate([acts[i, 1, :, cols] for i in range(halves)], axis=0)
        act = jnp.concatenate([acts[i, 0, :, cols] for i in range(halves)], axis=0)
        gu = (ge * slope.astype(F32)).astype(BF16)
        gu_scr[:, cols] = gu
        gb1[:, cols] += row_sums(gu.astype(F32))
        gw2t[:, cols] += dot(gr_t, act)
        gw1[:, cols] += dot(c_t, gu)
    gc = dot_nt(gu_scr[...], w1[...])
    gmid = grad + norm_back(gc, xh, inverse, gain2[...])
    gmid_out[...] = gmid
    gb = gmid.astype(BF16)
    gwo[...] += dot(jnp.concatenate([o[i] for i in range(o.shape[0])], axis=1), gb)
    go_t = dot_nt(wo[...], gb).astype(BF16)
    for i in range(o.shape[0]):
        go_out[i] = go_t[:, i * CHUNK : (i + 1) * CHUNK]
    sums[0] += row_sums(gr.astype(F32))
    sums[1] += row_sums(gb.astype(F32))
    sums[2] += row_sums(gc * xh)
    sums[3] += row_sums(gc)

    @pl.when(step == pl.num_programs(0) - 1)
    def _():
        tiles = hidden // 128
        put_tiles(grads_out, 0, gw2t)
        put_tiles(grads_out, tiles, gw1)
        put_tiles(grads_out, 2 * tiles, gwo)
        whole = [jnp.sum(sums[i], axis=0, keepdims=True) for i in range(4)]
        whole.append(jnp.sum(gb1[...], axis=0, keepdims=True))
        at = (2 * tiles + gwo.shape[1] // 128) * gwo.shape[0]
        put_rows(grads_out, at, whole)
        used = sum(feed_rows(gwo.shape[0], hidden))
        spare = grads_out.shape[0] - used
        if spare:
            grads_out[used:, :] = jnp.zeros((spare, 128), grads_out.dtype)


def feed_rows(width, hidden):
    tiles = (2 * hidden + width) // 128
    return tiles * width, -(-(4 * width + hidden) // 128 // 16) * 16


def feed_back(
    gx, gx_lead, patches, mid, acts, o, layer, gain2, shift2, w1, w2, wo, links, number
):
    width = mid.shape[1]
    hidden = acts.shape[3]

    def rows(cols, lead):
        return pl.BlockSpec((FEED, cols), lambda g: (g + lead, 0))

    grad_rows = padded_rows(sum(feed_rows(width, hidden)))
    return pl.pallas_call(
        links.host(functools.partial(feed_back_kernel, layer), 9, 3, 6),
        grid=(patches // FEED,),
        in_specs=[
            rows(width, gx_lead),
            rows(width, 1),
            pl.BlockSpec((FEED // CHUNK, 2, CHUNK, hidden), lambda g: (g + 1, 0, 0, 0)),
            pl.BlockSpec((FEED // CHUNK, width, CHUNK), lambda g: (g + 1, 0, 0)),
        ]
        + [layer_spec(w.shape, layer) for w in (gain2, shift2, w1, w2, wo)]
        + links.specs,
        out_specs=[
            rows(width, 0),
            pl.BlockSpec((FEED // CHUNK, width, CHUNK), lambda g: (g, 0, 0)),
            const_spec((grad_rows, 128)),
        ]
        + links.specs,
        out_shape=[
            jax.ShapeDtypeStruct((patches, width), F32),
            jax.ShapeDtypeStruct((patches // CHUNK, width, CHUNK), BF16),
            jax.ShapeDtypeStruct((grad_rows, 128), BF16),
        ]
        + links.shapes,
        scratch_shapes=[
            pltpu.VMEM((width, hidden), F32),
            pltpu.VMEM((width, hidden), F32),
            pltpu.VMEM((width, width), F32),
            pltpu.VMEM((4, 8, width), F32),
            pltpu.VMEM((8, hidden), F32),
            pltpu.VMEM((FEED, hidden), BF16),
        ]
        + links.scratch,
        compiler_params=links.params(number),
        name="feed_back",
    )(gx, mid, acts, o, gain2, shift2, w1, w2, wo, *links.arrays)


class Pusher:
    SLOTS = 8

    def __init__(self, plan, own, part, refs):
        self.plan, self.own, self.part = plan, own, part
        self.out, self.slots, self.send, self.recv, self.local = refs
        self.piece = min(part, CHUNK)
        self.subs = part // self.piece
        self.at = Places(plan)

    def each(self, chunk, act):
        at, bs = self.at, self.plan[1]
        whole = bs * self.part
        slot = chunk % self.SLOTS
        for k in range(CHUNK // self.piece):
            row = chunk * CHUNK + k * self.piece
            image, within = divmod(row, whole)
            target, sub = within // self.part, within % self.part // self.piece
            src = self.slots.at[slot, pl.ds(k * self.piece, self.piece), :]
            dst = self.out.at[at.b, image, pl.ds(sub * self.piece, self.piece), :]
            sem = slot * (CHUNK // self.piece) + k

            @pl.when(at.b == target)
            def _():
                act(pltpu.make_async_copy(src, dst, self.local.at[sem]), False)

            @pl.when(at.b != target)
            def _():
                by = mod(target - at.b + bs, bs)
                copy = pltpu.make_async_remote_copy(
                    src_ref=src,
                    dst_ref=dst,
                    send_sem=self.send.at[sem],
                    recv_sem=self.recv.at[((by - 1) * self.own + image) * self.subs + sub],
                    device_id=(at.img, target),
                    device_id_type=pl.DeviceIdType.MESH,
                )
                act(copy, True)

    def start(self, chunk):
        self.each(chunk, lambda copy, remote: copy.start())

    def sent(self, chunk):
        self.each(chunk, lambda copy, remote: copy.wait_send() if remote else copy.wait())

    def received(self):
        at, bs = self.at, self.plan[1]
        for by in range(1, bs):
            sender = mod(at.b - by + bs, bs)
            for image in range(self.own):
                for sub in range(self.subs):
                    pltpu.make_async_remote_copy(
                        src_ref=self.slots.at[0, pl.ds(0, self.piece), :],
                        dst_ref=self.out.at[sender, image, pl.ds(sub * self.piece, self.piece), :],
                        send_sem=self.send.at[0],
                        recv_sem=self.recv.at[((by - 1) * self.own + image) * self.subs + sub],
                        device_id=(at.img, sender),
                        device_id_type=pl.DeviceIdType.MESH,
                    ).wait_recv()


def last_attend_back_kernel(pairs, chunks, chunks_per_image, plan, own, part, *refs):
    ins, outs, scratch = refs[:12], refs[12:15], refs[15:]
    out, slots = outs[0], scratch[9]
    step = pl.program_id(0)
    pusher = Pusher(plan, own, part, (out, slots, *scratch[10:]))

    slot = slots.at[mod(step + Pusher.SLOTS - 1, Pusher.SLOTS)]
    attend_back_kernel(pairs, 0, chunks, chunks_per_image, *ins, slot, *outs[1:], *scratch[:9])
    acts = {}
    for chunk in range(chunks):

        def act(chunk=chunk):
            pusher.start(chunk)
            if 0 <= chunk + 1 - Pusher.SLOTS and chunk < chunks - 1:
                pusher.sent(chunk + 1 - Pusher.SLOTS)
            if chunk == chunks - 1:
                for old in range(max(chunks - Pusher.SLOTS, 0), chunks):
                    pusher.sent(old)
                pusher.received()

        acts[chunk + 1] = act
    return acts


def attend_back_kernel(
    pairs,
    layer,
    chunks,
    chunks_per_image,
    prev,
    cur,
    nxt,
    p_in,
    inverse_in,
    go_in,
    o_in,
    gmid,
    x,
    gain1,
    shift1,
    wqkv,
    gx_out,
    gtime,
    grads_out,
    gwqkv,
    gbias,
    sums,
    gq_ring,
    whole_ring,
    half_ring,
    next_ring,
    done,
    gs_scr,
):
    step = pl.program_id(0)
    width = x.shape[1]
    gain1, shift1 = [ref.at[pl.ds(layer, 1), :] for ref in (gain1, shift1)]

    @pl.when(step == 0)
    def _():
        for ref in (gwqkv, gbias, gtime, sums, gq_ring, whole_ring, half_ring, next_ring):
            ref[...] = jnp.zeros_like(ref)

    gq_old = gq_ring[...]
    live = (step < chunks).astype(F32)
    qkv = cur[...]
    queries = qkv[:, :width] * jnp.asarray(0.125, BF16)
    keys = jnp.concatenate(
        [prev[:, width : 2 * width], qkv[:, width : 2 * width], nxt[:, width : 2 * width]], axis=0
    )
    keys_t = keys.T
    values = jnp.concatenate([prev[:, 2 * width :], qkv[:, 2 * width :], nxt[:, 2 * width :]], axis=0)
    blocks = CHUNK // QBLOCK
    todo = [(blk, pair) for pair in range(pairs) for blk in range(blocks)]

    split_gos = {}

    def spread(blk, pair):
        low = blk * QBLOCK
        feat = slice(pair * 128, (pair + 1) * 128)
        inverse = inverse_in[blk, pair : pair + 1, :] * live
        go = go_in[feat, low : low + QBLOCK].astype(F32)
        go = [go[h * 64 : h * 64 + 64] * inverse[:, h * 128 : h * 128 + 128] for h in range(2)]
        o = o_in[feat, low : low + QBLOCK].astype(F32)
        row_dot = [
            jnp.sum(go[h] * o[h * 64 : h * 64 + 64], axis=0, keepdims=True) for h in range(2)
        ]
        split_go = split_heads(jnp.concatenate(go, axis=0).astype(BF16).T)
        split_gos[blk, pair] = split_go
        for k in range(0, KWIN, 128):
            gp = dot_nt(values[low + k : low + k + 128, feat], split_go)
            for h in range(2):
                lane = slice(h * 128, h * 128 + 128)
                gs = p_in[blk, pair, k : k + 128, lane].astype(F32) * (gp[:, lane] - row_dot[h])
                gbias[pair, k : k + 128, lane] += gs
                gs_scr[blk, pair, k : k + 128, lane] = gs.astype(BF16)

    late = []

    def pull(blk, pair):
        low = blk * QBLOCK
        feat = slice(pair * 128, (pair + 1) * 128)
        vfeat = slice(width + pair * 128, width + (pair + 1) * 128)
        gs = gs_scr[blk, pair]
        gk = dot(gs, split_heads(queries[low : low + QBLOCK, feat]))
        gv = dot(p_in[blk, pair], split_gos[blk, pair])
        gq = join_heads(dot(keys_t[feat, low : low + KWIN], gs)) * 0.125
        gq_ring[low : low + QBLOCK, feat] = gq.astype(BF16)
        late.append((gk, gv))
        if blk == blocks - 1:
            for cols, first, second in zip((feat, vfeat), late[-2], late[-1]):
                done[HALO:, cols] = (half_ring[:, cols] + first[:HALO]).astype(BF16)
                done[:HALO, cols] = whole_ring[:, cols]
                whole_ring[:, cols] = (
                    next_ring[:, cols] + first[HALO : 2 * HALO] + second[:HALO]
                ).astype(BF16)
                half_ring[:, cols] = first[2 * HALO :] + second[HALO : 2 * HALO]
                next_ring[:, cols] = second[2 * HALO :]

    for i in range(len(todo) + 1):
        if i < len(todo):
            spread(*todo[i])
        if i >= 1:
            pull(*todo[i - 1])

    done = jnp.concatenate([gq_old, done[...]], axis=1)
    xh, inverse = norm_stats(x[...].astype(F32))
    a = (xh * gain1[...] + shift1[...]).astype(BF16)
    gwqkv[...] += dot(a.T, done)
    ga = dot_nt(done, wqkv[...])
    gx_out[...] = (gmid[...] + norm_back(ga, xh, inverse, gain1[...])).astype(gx_out.dtype)
    sums[0] += row_sums(ga * xh)
    sums[1] += row_sums(ga)
    first = lax.rem(step + chunks_per_image - 1, chunks_per_image) == 0
    before = jnp.where(first, jnp.zeros(gtime.shape[1:], F32), gtime[0])
    summed = row_sums(done.astype(F32))
    gtime[0] = before + jnp.concatenate([summed[:, :width], summed[:, 2 * width :]], axis=1)

    @pl.when(step == chunks)
    def _():
        put_tiles(grads_out, 0, gwqkv)
        tiles = gwqkv.shape[1] // 128
        lines = attend_rows(width)[2]
        grads_out[tiles * width : tiles * width + lines, :] = gather_bias(gbias).astype(BF16)
        put_rows(
            grads_out,
            tiles * width + lines,
            [jnp.sum(sums[i], axis=0, keepdims=True) for i in range(2)],
        )
        used = attend_rows(width)[1]
        spare = grads_out.shape[0] - used
        if spare:
            grads_out[used:, :] = jnp.zeros((spare, 128), grads_out.dtype)


def attend_rows(width):
    lines = 2 * (width // 128) * (KWIN * 4 // QBLOCK) * 2
    small = -(-2 * width // 128 // 16) * 16
    return 3 * width // 128 * width, 3 * width // 128 * width + lines + small, lines


def attend_back(
    qkv,
    p,
    go,
    o,
    gmid,
    x,
    x_lead,
    chunks,
    chunks_per_image,
    layer,
    gain1,
    shift1,
    wqkv,
    own,
    part,
    links,
    number,
):
    width = x.shape[1]
    pairs = width // 128
    steps = chunks + 1
    halves = CHUNK // HALO

    def now(g):
        return jnp.minimum(g, chunks - 1)

    def late(g):
        return jnp.maximum(g - 1, 0)

    def rows(cols, lead, index):
        return pl.BlockSpec((CHUNK, cols), lambda g: (index(g) + lead, 0))

    images = chunks // chunks_per_image
    grad_rows = padded_rows(attend_rows(width)[1])
    in_specs = [
        pl.BlockSpec((HALO, 3 * width), lambda g: (jnp.maximum(halves * now(g) - 1, 0), 0)),
        rows(3 * width, 0, now),
        pl.BlockSpec(
            (HALO, 3 * width),
            lambda g: (jnp.minimum(halves * (now(g) + 1), halves * chunks - 1), 0),
        ),
        pl.BlockSpec((CHUNK // QBLOCK, pairs, KWIN, 2 * QBLOCK), lambda g: (now(g) + 1, 0, 0, 0)),
        pl.BlockSpec((CHUNK // QBLOCK, 8, 2 * QBLOCK), lambda g: (now(g) + 1, 0, 0)),
        pl.BlockSpec((None, width, CHUNK), lambda g: (now(g), 0, 0)),
        pl.BlockSpec((None, width, CHUNK), lambda g: (now(g) + 2, 0, 0)),
        rows(width, 0, late),
        rows(width, x_lead, late),
    ]
    in_specs += [layer_spec(w.shape, layer) for w in (gain1, shift1, wqkv)]
    out_specs = [
        rows(width, 1, lambda g: g),
        pl.BlockSpec((1, 8, 2 * width), lambda g: (late(g) // chunks_per_image, 0, 0)),
        const_spec((grad_rows, 128)),
    ]
    out_shape = [
        jax.ShapeDtypeStruct(((steps + 1) * CHUNK, width), F32),
        jax.ShapeDtypeStruct((images, 8, 2 * width), F32),
        jax.ShapeDtypeStruct((grad_rows, 128), BF16),
    ]
    scratch = [
        pltpu.VMEM((width, 3 * width), F32),
        pltpu.VMEM((pairs, KWIN, 2 * QBLOCK), F32),
        pltpu.VMEM((2, 8, width), F32),
        pltpu.VMEM((CHUNK, width), BF16),
        pltpu.VMEM((HALO, 2 * width), BF16),
        pltpu.VMEM((HALO, 2 * width), F32),
        pltpu.VMEM((HALO, 2 * width), F32),
        pltpu.VMEM((CHUNK, 2 * width), BF16),
        pltpu.VMEM((CHUNK // QBLOCK, pairs, KWIN, 2 * QBLOCK), BF16),
    ]
    kernel = functools.partial(attend_back_kernel, pairs, layer, chunks, chunks_per_image)
    if layer == 0:
        plan = link_plan()
        bs = plan[1]
        piece = min(part, CHUNK)
        pieces = CHUNK // piece
        kernel = functools.partial(
            last_attend_back_kernel, pairs, chunks, chunks_per_image, plan, own, part
        )
        out_specs[0] = pl.BlockSpec(memory_space=pl.ANY)
        out_shape[0] = jax.ShapeDtypeStruct((bs, own, part, width), BF16)
        scratch += [
            pltpu.VMEM((Pusher.SLOTS, CHUNK, width), BF16),
            pltpu.SemaphoreType.DMA((Pusher.SLOTS * pieces,)),
            pltpu.SemaphoreType.DMA((max((bs - 1) * own * (part // piece), 1),)),
            pltpu.SemaphoreType.DMA((Pusher.SLOTS * pieces,)),
        ]
    return pl.pallas_call(
        links.host(kernel, len(in_specs), len(out_specs), len(scratch)),
        grid=(steps,),
        in_specs=in_specs + links.specs,
        out_specs=out_specs + links.specs,
        out_shape=out_shape + links.shapes,
        scratch_shapes=scratch + links.scratch,
        compiler_params=links.params(number),
        name="attend_back",
    )(qkv, qkv, qkv, *p, go, o, gmid, x, gain1, shift1, wqkv, *links.arrays)


def final_kernel(plan, lanes_of_chunk, *refs):
    chunk, grad, extra = refs[:3]
    feed_out, attend_out, extra_out = refs[3:6]
    scratch = refs[6:]
    sems = Sems(*scratch[-3:])
    Places(plan).greet()
    parts = {}

    def planned(lane, whens):
        assert len(whens) == len(lane.steps) + 1
        for part, when in enumerate(whens):
            parts.setdefault(when, []).append((lane, part))

    lane = Lane(plan, sems)
    collect_lane(lane, scatter_lane(lane, grad, scratch[:-3]), attend_out)
    planned(lane, range(9))
    devices = 2 * plan[0] * plan[1] * plan[2]
    for low, rows in runs_of(feed_out.shape[0], lanes_of_chunk):
        lane = Lane(plan, sems)
        collect_lane(lane, chunk_ends(chunk, low, rows, devices), feed_out.at[pl.ds(low, rows), :])
        planned(lane, [0, 2, 4, 6, 8])
    lane = Lane(plan, sems)
    extra_lane(lane, extra, extra_out)
    planned(lane, [0, 1, 3, 5, 7])
    for when in sorted(parts):
        for lane, part in parts[when]:
            lane.part(part)


def final_exchange(chunk, lanes_of_chunk, grad, extra):
    plan = link_plan()
    xs, bs, zs = plan
    devices = 2 * xs * bs * zs
    anywhere = pl.BlockSpec(memory_space=pl.ANY)
    here = pl.BlockSpec(memory_space=pltpu.VMEM)
    return pl.pallas_call(
        functools.partial(final_kernel, plan, lanes_of_chunk),
        in_specs=[here, anywhere, here],
        out_specs=[anywhere] * 3,
        out_shape=[
            jax.ShapeDtypeStruct((chunk.shape[0] * devices, 128), BF16),
            jax.ShapeDtypeStruct(grad.shape, BF16),
            jax.ShapeDtypeStruct((devices * extra.shape[0], 128), BF16),
        ],
        scratch_shapes=held_shapes(plan, grad.shape[0]) + sems_shapes(plan, 3 + lanes_of_chunk),
        compiler_params=pltpu.CompilerParams(
            vmem_limit_bytes=VMEM_BYTES, collective_id=0, has_side_effects=True
        ),
        name="final_exchange",
    )(chunk, grad, extra)


def unpack_kernel(layers, lines, *refs):
    ins = [refs[6 * i : 6 * i + 6] for i in range(layers)]
    w2_out, w1_out, attend_out, wo_out = refs[6 * layers : 6 * layers + 4]
    small_outs = refs[6 * layers + 4 : 6 * layers + 11]
    rows_out = refs[6 * layers + 11]
    width = w1_out.shape[1]
    for layer, (w2t, w1, attend, wo, feed_small, attend_small) in enumerate(ins):
        for j in range(w1.shape[0] // width):
            rows = slice(j * width, (j + 1) * width)
            cols = slice(j * 128, (j + 1) * 128)
            w2_out[layer, cols, :] = w2t[rows, :].astype(F32).T
            w1_out[layer, :, cols] = w1[rows, :].astype(F32)
            attend_out[layer, :, cols] = attend[rows, :].astype(F32)
            wo_out[layer, :, cols] = wo[rows, :].astype(F32)
        feed = feed_small[...].astype(F32)
        tail = attend_small[...].astype(F32)
        rows_out[layer] = tail[:lines]
        at = 0
        for out in small_outs[:5]:
            for j in range(out.shape[1] // 128):
                out[layer : layer + 1, j * 128 : (j + 1) * 128] = feed[at : at + 1]
                at += 1
        at = lines
        for out in small_outs[5:]:
            for j in range(out.shape[1] // 128):
                out[layer : layer + 1, j * 128 : (j + 1) * 128] = tail[at : at + 1]
                at += 1


def unpack(fulls, width, hidden):
    layers = len(fulls)
    wide = width // 128
    steps = hidden // width
    rows = wide * width
    last = 3 * width // width - 1
    block = (rows, 128)
    feed_big, feed_small = feed_rows(width, hidden)
    attend_big, attend_all, lines = attend_rows(width)
    attend_small = attend_all - attend_big
    while attend_big % attend_small:
        attend_small += 16
    assert feed_big % feed_small == 0

    def spec(first, top):
        return pl.BlockSpec(block, lambda g: (first + jnp.minimum(g, top), 0))

    ins = [
        spec(0, steps),
        spec(steps, steps),
        spec(0, last),
        spec(2 * steps, 0),
        pl.BlockSpec((feed_small, 128), lambda g: (feed_big // feed_small, 0)),
        pl.BlockSpec((attend_small, 128), lambda g: (attend_big // attend_small, 0)),
    ]
    vectors = [width] * 4 + [hidden] + [width] * 2
    return pl.pallas_call(
        functools.partial(unpack_kernel, layers, lines),
        grid=(steps,),
        in_specs=ins * layers,
        out_specs=[
            pl.BlockSpec((layers, width, width), lambda g: (0, g, 0)),
            pl.BlockSpec((layers, width, width), lambda g: (0, 0, g)),
            pl.BlockSpec((layers, width, width), lambda g: (0, 0, jnp.minimum(g, last))),
            pl.BlockSpec((layers, width, width), lambda g: (0, 0, 0)),
        ]
        + [pl.BlockSpec((layers, n), lambda g: (0, 0)) for n in vectors]
        + [pl.BlockSpec((layers, lines, 128), lambda g: (0, 0, 0))],
        out_shape=[
            jax.ShapeDtypeStruct((layers, hidden, width), F32),
            jax.ShapeDtypeStruct((layers, width, hidden), F32),
            jax.ShapeDtypeStruct((layers, width, 3 * width), F32),
            jax.ShapeDtypeStruct((layers, width, width), F32),
        ]
        + [jax.ShapeDtypeStruct((layers, n), F32) for n in vectors]
        + [jax.ShapeDtypeStruct((layers, lines, 128), F32)],
        compiler_params=pltpu.CompilerParams(vmem_limit_bytes=VMEM_BYTES),
        name="unpack",
    )(
        *[
            ref
            for feed, attend in fulls
            for ref in (
                feed,
                feed,
                attend,
                feed,
                feed,
                attend,
            )
        ]
    )


def time_embedding(timesteps, width):
    half_width = width // 2
    frequency = jnp.exp(
        jnp.arange(half_width, dtype=jnp.int32).astype(F32) * (-math.log(10000.0) / half_width)
    )
    angles = timesteps.astype(F32)[:, None] * frequency[None, :]
    return jnp.concatenate([jnp.sin(angles), jnp.cos(angles)], axis=-1)


def bias_rows(table, index_table, grid_cols):
    heads, entries = table.shape
    span = 2 * WIN + 1
    offsets = 2 * grid_cols - 1
    turned = index_table.reshape(span, offsets)[:, ::-1].reshape(entries)
    select = (turned[None, :] == jnp.arange(entries, dtype=jnp.int32)[:, None]).astype(F32)
    rows = jnp.dot(table, select, precision=EXACT).reshape(heads, span, offsets)
    key_rows = KWIN // grid_cols
    a0, a1, a2, a3 = [
        jnp.pad(
            rows, ((0, 0), (q, key_rows - span - q), (0, 0)), constant_values=NEG_FILL
        )
        for q in range(QBLOCK // grid_cols)
    ]
    gap = jnp.full((heads, key_rows, 1), NEG_FILL, F32)
    even = jnp.concatenate(
        [a0[..., grid_cols - 1 :], gap, a2, gap, a0[..., : grid_cols - 1]], axis=-1
    )
    odd = jnp.concatenate([gap, a1, gap, a3], axis=-1)
    return jnp.stack([even, odd], axis=1)


def spaced(parts, steps):
    return [i * (steps - 1) // (parts - 1) for i in range(parts)]


def body(
    tokens,
    cotangent,
    valid_mask,
    timesteps,
    index_table,
    first_gain,
    first_shift,
    attend_weight,
    time_weight,
    offset_bias,
    output_weight,
    output_bias,
    second_gain,
    second_shift,
    expand_weight,
    expand_bias,
    reduce_weight,
    reduce_bias,
):
    images, band_rows, grid_cols, width = tokens.shape
    layers = attend_weight.shape[0]
    bands = lax.axis_size("band")
    me = lax.axis_index("band")
    own = images // bands
    part = band_rows * grid_cols
    patches = bands * part
    per_image = patches // CHUNK
    chunks = own * per_image

    mine = lax.dynamic_slice_in_dim(valid_mask, me * own, own, 0).reshape(own, patches)
    fill = jnp.where(mine == 1, 0.0, NEG_FILL).astype(F32)
    fill = jnp.pad(fill, ((0, 0), (HALO, HALO)), constant_values=NEG_FILL)
    mask = jnp.stack(
        [fill[:, c * CHUNK : (c + 1) * CHUNK + 2 * HALO] for c in range(per_image)], axis=1
    ).reshape(chunks, 1, CHUNK + 2 * HALO)

    time_low = time_embedding(
        lax.dynamic_slice_in_dim(timesteps, me * own, own, 0), width
    ).astype(BF16)
    heads, entries = offset_bias.shape[1:]

    def make_rows(table):
        return bias_rows(table, index_table, grid_cols)

    biases, bias_pull = jax.vjp(make_rows, offset_bias.reshape(layers * heads, entries))
    biases = biases.reshape(layers, -1, QBLOCK) * LOG2E

    tp = jnp.einsum("it,ltc->lic", time_low, time_weight, preferred_element_type=F32)
    tproj = jnp.concatenate([tp[..., :width], jnp.zeros_like(tp[..., :width]), tp[..., width:]], -1)
    weights = (
        first_gain,
        first_shift,
        attend_weight,
        output_weight,
        output_bias,
        second_gain,
        second_shift,
        expand_weight,
        expand_bias,
        reduce_weight,
        reduce_bias,
    )
    x, x_lead = tokens.reshape(images * part, width), 0
    kept = []
    for layer in range(layers):
        last = layer == layers - 1
        jobs = []
        if last:
            shard = cotangent.reshape(images * part, width)
            jobs = [("images", shard, (own, part), [0, chunks // 2, chunks + 2])]
        qkv, p, inverse, o, mid, acts, nxt, *more = forward_layer(
            x,
            x_lead,
            chunks,
            per_image,
            tproj[layer][:, None, :],
            mask,
            biases,
            layer,
            weights,
            BF16 if last else F32,
            Links(jobs),
            own,
            part,
            1 + layer,
        )
        if layer == 0:
            x = more[0]
        if last:
            gx = more[-1]
        kept.append((x, x_lead, qkv, (p, inverse), o, mid, acts))
        x, x_lead = nxt, 2

    gx_lead = 0
    devices = bands * lax.axis_size("img")
    hidden = expand_weight.shape[2]
    fulls = [[None, None] for _ in range(layers)]
    extra = [time_low]
    attend_grads = feed_part = None
    result = x
    for layer in reversed(range(layers)):
        x, x_lead, qkv, p, o, mid, acts = kept[layer]
        steps = own * patches // FEED
        if layer == layers - 1:
            jobs = [("bands", result, (2 * CHUNK, own, part), [0, steps // 2, steps])]
        else:
            jobs = [("sum", attend_grads, [spaced(9, steps)])]
        gmid, go, feed_grads, *sent = feed_back(
            gx,
            gx_lead,
            own * patches,
            mid,
            acts,
            o,
            layer,
            second_gain,
            second_shift,
            expand_weight,
            reduce_weight,
            output_weight,
            Links(jobs),
            1 + layers + 2 * layer,
        )
        if layer == layers - 1:
            output = sent[0].reshape(tokens.shape)
        else:
            fulls[layer + 1] = [feed_part, sent[0]]
        gx, gtime, attend_grads, feed_part = attend_back(
            qkv,
            p,
            go,
            o,
            gmid,
            x,
            x_lead,
            chunks,
            per_image,
            layer,
            first_gain,
            first_shift,
            attend_weight,
            own,
            part,
            Links(
                [
                    ("sum", feed_grads, [spaced(9, chunks), [i + 1 for i in spaced(9, chunks)]])
                    if layer
                    else ("scatter", feed_grads, [spaced(6, chunks), [i + 1 for i in spaced(6, chunks)]])
                ]
            ),
            2 + layers + 2 * layer,
        )
        gx_lead = 1
        extra.append(jnp.sum(gtime, axis=1).astype(BF16))
    input_grad = gx.reshape(tokens.shape)

    extra = jnp.concatenate(extra, axis=1).reshape(-1, 128)
    lead = extra.shape[0]
    extra = jnp.pad(extra, ((0, -lead % 16), (0, 0)))
    *fulls[0], gathered = final_exchange(feed_part, 2, attend_grads, extra)
    gathered = gathered.reshape(devices, -1, 128)[:, :lead].reshape(devices * own, -1)
    grad_time = jnp.stack(
        [
            lax.dot_general(
                gathered[:, :width],
                gathered[:, width * (1 + 2 * turn) : width * (3 + 2 * turn)],
                (((0,), (0,)), ((), ())),
                preferred_element_type=F32,
            )
            for turn in reversed(range(layers))
        ]
    )
    (
        grad_reduce,
        grad_expand,
        grad_attend,
        grad_output,
        reduce_bias_grad,
        output_bias_grad,
        second_gain_grad,
        second_shift_grad,
        expand_bias_grad,
        first_gain_grad,
        first_shift_grad,
        grad_rows,
    ) = unpack(fulls, width, hidden)
    (grad_offset,) = bias_pull(grad_rows.reshape(layers * heads, 2, -1, QBLOCK))
    return (
        output,
        input_grad,
        first_gain_grad,
        first_shift_grad,
        grad_attend,
        grad_time,
        grad_offset.reshape(layers, heads, entries),
        grad_output,
        output_bias_grad,
        second_gain_grad,
        second_shift_grad,
        grad_expand,
        expand_bias_grad,
        grad_reduce,
        reduce_bias_grad,
    )


def solution(mesh):
    split = P("img", "band", None, None)
    placed = (split, split, P("img", None, None), P("img")) + (P(),) * 14
    return jax.shard_map(
        body,
        mesh=mesh,
        in_specs=placed,
        out_specs=(split, split) + (P(),) * 13,
        check_vma=False,
    )
```

```python
import functools
import math

import jax
import jax.numpy as jnp
from jax import lax
from jax.experimental import pallas as pl
from jax.experimental.pallas import tpu as pltpu
from jax.sharding import PartitionSpec as P

WIN = 4
CHUNK = 256
QBLOCK = 128
KWIN = 384
HALO = 128
FEED = 512

EXACT = lax.Precision.HIGHEST
NEG_FILL = -1000000000.0
EPSILON = 1e-06
LOG2E = math.log2(math.e)
GELU_A = math.sqrt(2.0 / math.pi)
GELU_B = 0.044715 * GELU_A
VMEM_BYTES = 58 * 1024 * 1024

F32 = jnp.float32
BF16 = jnp.bfloat16


def dot(a, b):
    return jnp.dot(a, b, preferred_element_type=F32)


def dot_nt(a, b):
    return lax.dot_general(a, b, (((1,), (1,)), ((), ())), preferred_element_type=F32)


def norm_stats(v):
    mean = jnp.mean(v, axis=-1, keepdims=True)
    centered = v - mean
    inverse = lax.rsqrt(jnp.mean(centered * centered, axis=-1, keepdims=True) + EPSILON)
    return centered * inverse, inverse


def norm_back(gy, xh, inverse, gain):
    gs = gy * gain
    return inverse * (
        gs - jnp.mean(gs, axis=-1, keepdims=True) - xh * jnp.mean(gs * xh, axis=-1, keepdims=True)
    )


def row_sums(v):
    rows, cols = v.shape
    return jnp.sum(v.reshape(rows // 8, 8, cols), axis=0)


def split_heads(block):
    lane = lax.broadcasted_iota(jnp.int32, block.shape, 1)
    zero = jnp.zeros_like(block)
    first = lane < block.shape[1] // 2
    return jnp.concatenate(
        [jnp.where(first, block, zero), jnp.where(first, zero, block)], axis=0
    )


def join_heads(product):
    half = product.shape[0] // 2
    width = product.shape[1] // 2
    return jnp.concatenate([product[:half, :width], product[half:, width:]], axis=0).T


def share_rows(rows):
    return max(n for n in range(16, 257, 16) if rows % n == 0)


def add_rows(total, at, others, rows):
    share = share_rows(rows)

    def one(i, carry):
        low = pl.multiple_of(i * share, 16)
        here = pl.ds(pl.multiple_of(at + low, 16), share)
        v = total[here, :].astype(F32)
        for ref, row in others:
            v = v + ref[pl.ds(pl.multiple_of(row + low, 16), share), :].astype(F32)
        total[here, :] = v.astype(total.dtype)
        return carry

    lax.fori_loop(0, rows // share, one, 0)


def cut(ref, at, rows):
    return ref.at[pl.ds(pl.multiple_of(at, 16), rows), :]


def both(first, second):
    first()
    second()


def dispatch(step, acts):
    whens = sorted(acts)
    if len(whens) <= 1:
        for when in whens:
            pl.when(step == when)(acts[when])
        return
    middle = whens[len(whens) // 2]
    low = {when: acts[when] for when in whens if when < middle}
    high = {when: acts[when] for when in whens if when >= middle}
    pl.when(step < middle)(lambda: dispatch(step, low))
    pl.when(step >= middle)(lambda: dispatch(step, high))


def mod(v, n):
    return jnp.bitwise_and(v, n - 1) if n & (n - 1) == 0 else lax.rem(v, n)


def halved(v, n):
    return jnp.right_shift(v, n.bit_length() - 1) if n & (n - 1) == 0 else v // n


class Places:
    def __init__(self, plan):
        self.xs, self.bs, self.zs = plan
        self.img = lax.axis_index("img")
        self.b = lax.axis_index("band")
        self.c = mod(self.img, 2)
        self.x = mod(halved(self.img, 2), self.xs)
        self.z = halved(self.img, 2 * self.xs)

    def core(self, by):
        return (self.img + 1 - 2 * self.c, self.b)

    def along_x(self, by):
        return ((self.z * self.xs + mod(self.x + by, self.xs)) * 2 + self.c, self.b)

    def along_b(self, by):
        return (self.img, mod(self.b + by, self.bs))

    def along_z(self, by):
        return ((mod(self.z + by, self.zs) * self.xs + self.x) * 2 + self.c, self.b)

    def greet(self):
        barrier = pltpu.get_barrier_semaphore()
        peers = [self.core(1)]
        peers += [self.along_x(by) for by in range(1, self.xs)]
        peers += [self.along_b(by) for by in range(1, self.bs)]
        peers += [self.along_z(by) for by in range(1, self.zs)]
        for peer in peers:
            pl.semaphore_signal(barrier, inc=1, device_id=peer, device_id_type=pl.DeviceIdType.MESH)
        pl.semaphore_wait(barrier, len(peers))


class Lane:
    def __init__(self, plan, sems):
        self.plan, self.sems, self.steps = plan, sems, []

    def add(self, copies, then=None):
        count = [0, 0]
        here = Places(self.plan)
        for src, dst, peer in copies(here):
            count[peer is None] += 1
        base = (self.sems.sent, self.sems.kept)
        self.sems.sent += count[0]
        self.sems.kept += count[1]
        self.steps.append((copies, then, base))

    def described(self, step):
        copies, _, (sent, kept) = self.steps[step]
        made = []
        for src, dst, peer in copies(Places(self.plan)):
            if peer is None:
                made.append(pltpu.make_async_copy(src, dst, self.sems.own.at[kept]))
                kept += 1
            else:
                made.append(
                    pltpu.make_async_remote_copy(
                        src_ref=src,
                        dst_ref=dst,
                        send_sem=self.sems.send.at[sent],
                        recv_sem=self.sems.recv.at[sent],
                        device_id=peer,
                        device_id_type=pl.DeviceIdType.MESH,
                    )
                )
                sent += 1
        return made

    def part(self, i):
        if i > 0:
            for copy in self.described(i - 1):
                copy.wait()
            if self.steps[i - 1][1] is not None:
                self.steps[i - 1][1](Places(self.plan))
        if i < len(self.steps):
            for copy in self.described(i):
                copy.start()


class Sems:
    def __init__(self, send, recv, own):
        self.send, self.recv, self.own = send, recv, own
        self.sent = self.kept = 0


def scatter_lane(lane, grad, held, chunk=None):
    acc, r1, r2a, r2b, r3a, r3b, r4 = held
    xs, bs, zs = lane.plan
    half = grad.shape[0] // 2
    quarter = half // 2
    nx, nb, n2 = quarter // xs, quarter // bs, quarter // (xs * bs)
    n = n2 // zs

    def core_copies(at):
        return [
            (cut(grad, at.c * half, half), acc, None),
            (cut(grad, half - at.c * half, half), r1, at.core(1)),
        ]

    lane.add(core_copies, lambda at: add_rows(acc, 0, [(r1, 0)], half))

    def wide_copies(at):
        made = []
        for by in range(1, xs):
            there = mod(at.x + by, xs)
            made.append((cut(acc, there * nx, nx), cut(r2a, (by - 1) * nx, nx), at.along_x(by)))
        for by in range(1, bs):
            there = quarter + mod(at.b + by, bs) * nb
            made.append((cut(acc, there, nb), cut(r2b, (by - 1) * nb, nb), at.along_b(by)))
        return made

    def wide_add(at):
        add_rows(acc, at.x * nx, [(r2a, k * nx) for k in range(xs - 1)], nx)
        add_rows(acc, quarter + at.b * nb, [(r2b, k * nb) for k in range(bs - 1)], nb)

    lane.add(wide_copies, wide_add)

    def cross_copies(at):
        made = []
        for by in range(1, bs):
            there = at.x * nx + mod(at.b + by, bs) * n2
            made.append((cut(acc, there, n2), cut(r3a, (by - 1) * n2, n2), at.along_b(by)))
        for by in range(1, xs):
            there = quarter + at.b * nb + mod(at.x + by, xs) * n2
            made.append((cut(acc, there, n2), cut(r3b, (by - 1) * n2, n2), at.along_x(by)))
        return made

    def plane(at):
        return at.x * nx + at.b * n2, quarter + at.b * nb + at.x * n2

    def cross_add(at):
        first, second = plane(at)
        add_rows(acc, first, [(r3a, k * n2) for k in range(bs - 1)], n2)
        add_rows(acc, second, [(r3b, k * n2) for k in range(xs - 1)], n2)

    lane.add(cross_copies, cross_add)

    def deep_copies(at):
        made = []
        for by in range(1, zs):
            there = mod(at.z + by, zs) * n
            for k, low in enumerate(plane(at)):
                slot = (2 * (by - 1) + k) * n
                made.append((cut(acc, low + there, n), cut(r4, slot, n), at.along_z(by)))
        return made

    def deep_add(at):
        for k, low in enumerate(plane(at)):
            add_rows(acc, low + at.z * n, [(r4, (2 * i + k) * n) for i in range(zs - 1)], n)

    lane.add(deep_copies, deep_add)

    def ends(at):
        return [cut(acc, low + at.z * n, n) for low in plane(at)]

    if chunk is None:
        return ends
    lane.add(lambda at: [(ref, cut(chunk, k * n, n), None) for k, ref in enumerate(ends(at))])


def collect_lane(lane, ends, out):
    xs, bs, zs = lane.plan
    half = out.shape[0] // 2
    quarter = half // 2
    nx, nb, n2 = quarter // xs, quarter // bs, quarter // (xs * bs)
    n = n2 // zs

    def plane(at):
        base = at.c * half
        return base + at.x * nx + at.b * n2, base + quarter + at.b * nb + at.x * n2

    def deep(at):
        made = []
        for ref, low in zip(ends(at), plane(at)):
            there = cut(out, low + at.z * n, n)
            made.append((ref, there, None))
            made += [(ref, there, at.along_z(by)) for by in range(1, zs)]
        return made

    def cross(at):
        first, second = plane(at)
        a, b = cut(out, first, n2), cut(out, second, n2)
        made = [(a, a, at.along_b(by)) for by in range(1, bs)]
        return made + [(b, b, at.along_x(by)) for by in range(1, xs)]

    def wide(at):
        a = cut(out, at.c * half + at.x * nx, nx)
        b = cut(out, at.c * half + quarter + at.b * nb, nb)
        made = [(a, a, at.along_x(by)) for by in range(1, xs)]
        return made + [(b, b, at.along_b(by)) for by in range(1, bs)]

    def core(at):
        whole = cut(out, at.c * half, half)
        return [(whole, whole, at.core(1))]

    for copies in (deep, cross, wide, core):
        lane.add(copies)


def extra_lane(lane, extra, out):
    xs, bs, zs = lane.plan
    rows = extra.shape[0]

    def deep(at):
        there = cut(out, (((at.c * xs + at.x) * bs + at.b) * zs + at.z) * rows, rows)
        return [(extra, there, None)] + [(extra, there, at.along_z(by)) for by in range(1, zs)]

    def cross(at):
        there = cut(out, ((at.c * xs + at.x) * bs + at.b) * zs * rows, zs * rows)
        return [(there, there, at.along_b(by)) for by in range(1, bs)]

    def wide(at):
        there = cut(out, (at.c * xs + at.x) * bs * zs * rows, bs * zs * rows)
        return [(there, there, at.along_x(by)) for by in range(1, xs)]

    def core(at):
        there = cut(out, at.c * xs * bs * zs * rows, xs * bs * zs * rows)
        return [(there, there, at.core(1))]

    for copies in (deep, cross, wide, core):
        lane.add(copies)


def link_plan():
    pairs = lax.axis_size("img") // 2
    xs = 2 if pairs % 2 == 0 else 1
    return xs, lax.axis_size("band"), pairs // xs


def padded_rows(rows):
    xs, bs, zs = link_plan()
    return -(-rows // (64 * xs * bs * zs)) * (64 * xs * bs * zs)


def held_shapes(plan, rows):
    xs, bs, zs = plan
    quarter = rows // 4
    sizes = [
        rows // 2,
        rows // 2,
        (xs - 1) * quarter // xs,
        (bs - 1) * quarter // bs,
        (bs - 1) * quarter // (xs * bs),
        (xs - 1) * quarter // (xs * bs),
        (zs - 1) * 2 * quarter // (xs * bs * zs),
    ]
    return [pltpu.VMEM((max(n, 16), 128), BF16) for n in sizes]


def sems_shapes(plan, lanes, moved=0):
    xs, bs, zs = plan
    count = lanes * (1 + 2 * (xs - 1 + bs - 1) + 2 * (zs - 1)) + moved
    return [
        pltpu.SemaphoreType.DMA((count,)),
        pltpu.SemaphoreType.DMA((count,)),
        pltpu.SemaphoreType.DMA((2 * lanes + moved + 1,)),
    ]


def images_copies(shard, at, own, part, images):
    made = []
    for by in range(at.bs):
        there = mod(at.b + by, at.bs)
        for i in images:
            made.append(((there * own + i) * part, (i * at.bs + at.b) * part, by))
    return made


def runs_of(rows, lanes):
    unit = padded_rows(1)
    units = rows // unit
    lanes = min(lanes, units)
    ends = [units * i // lanes * unit for i in range(lanes + 1)]
    return [(low, high - low) for low, high in zip(ends, ends[1:])]


def chunk_ends(chunk, low, rows, devices):
    low, half = low // devices, rows // devices // 2
    return lambda at: [cut(chunk, low + k * half, half) for k in range(2)]


def load_lane(lane, chunk, here, low, rows, devices):
    part = pl.ds(low // devices, rows // devices)
    lane.add(lambda at: [(chunk.at[part, :], here.at[part, :], None)])


class Links:
    def __init__(self, jobs):
        self.jobs = jobs
        self.plan = link_plan()
        xs, bs, zs = self.plan
        self.devices = 2 * xs * bs * zs
        self.arrays = [job[1] for job in jobs]
        self.shapes, self.scratch = [], []
        remote = local = 0
        for job in jobs:
            if job[0] in ("sum", "scatter", "collect"):
                rows_all = job[1].shape[0] * (self.devices if job[0] == "collect" else 1)
                for _, rows in runs_of(rows_all, len(job[-1])):
                    if job[0] != "collect":
                        self.scratch += held_shapes(self.plan, rows)
                    remote += 2 * (1 + 2 * (xs - 1 + bs - 1) + 2 * (zs - 1))
                    local += 4
                if job[0] == "collect":
                    self.scratch.append(pltpu.VMEM(job[1].shape, BF16))
                if job[0] == "scatter":
                    rows_all //= self.devices
                self.shapes.append(jax.ShapeDtypeStruct((rows_all, 128), BF16))
                continue
            width = job[1].shape[1]
            own, part = job[2][-2:]
            shape = (bs, own, part, width) if job[0] == "bands" else (own * bs * part, width)
            self.shapes.append(jax.ShapeDtypeStruct(shape, BF16))
            self.scratch.append(pltpu.VMEM((own, part, width), BF16))
            remote += (bs - 1) * own
            local += 2 * own
        if jobs:
            self.scratch += [
                pltpu.SemaphoreType.DMA((max(remote, 1),)),
                pltpu.SemaphoreType.DMA((max(remote, 1),)),
                pltpu.SemaphoreType.DMA((local,)),
            ]
        self.specs = [pl.BlockSpec(memory_space=pl.ANY)] * len(jobs)

    def host(self, kernel, ins, outs, scratch):
        def run(*refs):
            count = len(self.jobs)
            a, b, c = ins, ins + count, ins + count + outs
            d, e = c + count, c + count + scratch
            step = pl.program_id(0)
            acts = kernel(*refs[:a], *refs[b:c], *refs[d:e]) or {}
            if self.jobs:
                parts = self.parts(refs[a:b], refs[c:d], refs[e:])
                parts.setdefault(0, [])
                for when in sorted(parts):

                    def act(when=when):
                        if when == 0:
                            Places(self.plan).greet()
                        for lane, part in parts[when]:
                            lane.part(part)

                    at = min(when, pl.num_programs(0) - 1)
                    before = acts.get(at)
                    acts[at] = act if before is None else functools.partial(both, before, act)
            dispatch(step, acts)

        return run

    def parts(self, given, made, scratch):
        sems = Sems(*scratch[-3:])
        held = list(scratch[:-3])
        parts = {}
        lanes = []
        for job, ref, out in zip(self.jobs, given, made):
            if job[0] == "sum":
                for (low, rows), whens in zip(runs_of(ref.shape[0], len(job[-1])), job[-1]):
                    lane = Lane(self.plan, sems)
                    part_in, part_out = ref.at[pl.ds(low, rows), :], out.at[pl.ds(low, rows), :]
                    collect_lane(lane, scatter_lane(lane, part_in, held[:7]), part_out)
                    held = held[7:]
                    lanes.append((lane, whens))
                continue
            if job[0] == "scatter":
                for (low, rows), whens in zip(runs_of(ref.shape[0], len(job[-1])), job[-1]):
                    lane = Lane(self.plan, sems)
                    few = rows // self.devices
                    chunk = out.at[pl.ds(low // self.devices, few), :]
                    scatter_lane(lane, ref.at[pl.ds(low, rows), :], held[:7], chunk)
                    held = held[7:]
                    lanes.append((lane, whens))
                continue
            if job[0] == "collect":
                here = held[0]
                held = held[1:]
                for (low, rows), whens in zip(runs_of(out.shape[0], len(job[-1])), job[-1]):
                    lane = Lane(self.plan, sems)
                    load_lane(lane, ref, here, low, rows, self.devices)
                    ends = chunk_ends(here, low, rows, self.devices)
                    collect_lane(lane, ends, out.at[pl.ds(low, rows), :])
                    lanes.append((lane, whens))
                continue
            own, part = job[2][-2:]
            lead = job[2][0] if job[0] == "bands" else 0

            def copies(at, kind=job[0], ref=ref, out=out, own=own, part=part, lead=lead):
                made = []
                for i in range(own):
                    for by in range(self.plan[1]):
                        there = mod(at.b + by, self.plan[1])
                        if kind == "bands":
                            src = cut(ref, lead + (i * self.plan[1] + there) * part, part)
                            dst = out.at[at.b, i]
                        else:
                            src = cut(ref, (there * own + i) * part, part)
                            dst = cut(out, (i * self.plan[1] + at.b) * part, part)
                        made.append((i, src, dst, at.along_b(by) if by else None))
                return made

            lane = Lane(self.plan, sems)
            lane.add(lambda at, f=copies: [c[1:] for c in f(at) if c[3] is not None])
            lanes.append((lane, [job[-1][0], job[-1][-1]]))
            lane = Lane(self.plan, sems)
            here = held[0]
            held = held[1:]
            lane.add(lambda at, f=copies, h=here: [(c[1], h.at[c[0]], None) for c in f(at) if c[3] is None])
            lane.add(lambda at, f=copies, h=here: [(h.at[c[0]], c[2], None) for c in f(at) if c[3] is None])
            lanes.append((lane, job[-1]))
        for lane, whens in lanes:
            assert len(whens) == len(lane.steps) + 1
            for part, when in enumerate(whens):
                parts.setdefault(when, []).append((lane, part))
        return parts

    def params(self, number):
        if not self.jobs:
            return pltpu.CompilerParams(vmem_limit_bytes=VMEM_BYTES)
        return pltpu.CompilerParams(
            vmem_limit_bytes=VMEM_BYTES, collective_id=number, has_side_effects=True
        )


def fold(v, op):
    return op(v.reshape(v.shape[0] // 8, 8, v.shape[1]), axis=0)


def unroll_bias(rows, bias):
    pairs, keys, lanes = bias.shape
    grid_cols = QBLOCK // 4
    key_rows = keys // grid_cols
    lane = lax.broadcasted_iota(jnp.int32, (grid_cols, QBLOCK), 1)
    even = lax.rem(lane // grid_cols, 2) == 0
    for pair in range(pairs):
        for head in range(2):
            for key_row in range(key_rows):
                turned = [
                    pltpu.roll(
                        jnp.broadcast_to(
                            rows[pl.ds(((pair * 2 + head) * 2 + odd) * key_rows + key_row, 1), :],
                            (grid_cols, QBLOCK),
                        ),
                        0,
                        1,
                        stride=1,
                        stride_axis=0,
                    )
                    for odd in range(2)
                ]
                bias[
                    pair,
                    key_row * grid_cols : (key_row + 1) * grid_cols,
                    head * QBLOCK : (head + 1) * QBLOCK,
                ] = jnp.where(even, turned[0], turned[1])


def gather_bias(grads):
    pairs, keys, lanes = grads.shape
    grid_cols = QBLOCK // 4
    lane = lax.broadcasted_iota(jnp.int32, (keys, QBLOCK), 1)
    column = lax.rem(lax.broadcasted_iota(jnp.int32, (keys, QBLOCK), 0), grid_cols)
    parity = lax.rem(lane // grid_cols, 2)
    sums = []
    for pair in range(pairs):
        for head in range(2):
            for odd in range(2):
                v = grads[pair, :, head * QBLOCK : (head + 1) * QBLOCK]
                v = jnp.where(parity == odd, v, 0.0)
                for bit in (1, 2, 4, 8, 16):
                    turned = pltpu.roll(v, QBLOCK - bit, 1)
                    v = jnp.where(lax.rem(column // bit, 2) == 1, turned, v)
                sums.append(jnp.sum(v.reshape(keys // grid_cols, grid_cols, QBLOCK), axis=1))
    return jnp.concatenate(sums, axis=0)


def low_of(value):
    return jnp.asarray(value, BF16)


def forward_kernel(
    pairs,
    layer,
    x_new,
    x_old,
    tproj,
    mask,
    bias_rows,
    gain1,
    shift1,
    wqkv,
    wo,
    bo,
    gain2,
    shift2,
    w1,
    b1,
    w2,
    b2,
    qkv_out,
    p_out,
    inverse_out,
    o_out,
    mid_out,
    acts_out,
    x_out,
    bias,
    q_ring,
    k_ring,
    vt_ring,
    o_ring,
    s_scr,
):
    step = pl.program_id(0)
    width = x_new.shape[1]
    gain1, shift1, bo, gain2, shift2, b1, b2 = [
        ref.at[pl.ds(layer, 1), :] for ref in (gain1, shift1, bo, gain2, shift2, b1, b2)
    ]

    @pl.when(step == 0)
    def _():
        unroll_bias(bias_rows, bias)
        q_ring[...] = jnp.zeros_like(q_ring)
        k_ring[...] = jnp.zeros_like(k_ring)
        vt_ring[...] = jnp.zeros_like(vt_ring)
        o_ring[...] = jnp.zeros_like(o_ring)

    act_out, slope_out = acts_out.at[0], acts_out.at[1]
    attended = o_ring[...]
    mid = x_old[...].astype(F32) + (dot(attended, wo[...]) + bo[...])
    mid_out[...] = mid
    xh2, _ = norm_stats(mid)
    c = (xh2 * gain2[...] + shift2[...]).astype(BF16)
    parts = 2 * pairs
    tile = w1.shape[1] // parts

    def feed(part):
        cols = slice(part * tile, (part + 1) * tile)
        whole = dot(c, w1[:, cols])
        for low in range(0, CHUNK, 64):
            u = (whole[low : low + 64] + b1[:, cols]).astype(BF16)
            u2 = u * u
            t = jnp.tanh(u * (low_of(GELU_A) + low_of(GELU_B) * u2))
            h = low_of(0.5) + low_of(0.5) * t
            e = u * h
            act_out[low : low + 64, cols] = e
            slope_out[low : low + 64, cols] = h + (e * (low_of(1.0) - t)) * (
                low_of(GELU_A) + low_of(3.0 * GELU_B) * u2
            )

    queries = q_ring[...]
    xh1, _ = norm_stats(x_new[...].astype(F32))
    a = (xh1 * gain1[...] + shift1[...]).astype(BF16)
    projected = dot(a, wqkv[...]) + tproj[0]
    qkv = projected.astype(BF16)
    qkv_out[...] = qkv
    q_ring[...] = (projected[:, :width] * (0.125 * LOG2E)).astype(BF16)
    k_ring[:HALO, :] = k_ring[CHUNK : CHUNK + HALO, :]
    k_ring[HALO : HALO + CHUNK, :] = k_ring[HALO + CHUNK :, :]
    k_ring[HALO + CHUNK :, :] = qkv[:, width : 2 * width]
    vt_ring[:, :HALO] = vt_ring[:, CHUNK : CHUNK + HALO]
    vt_ring[:, HALO : HALO + CHUNK] = vt_ring[:, HALO + CHUNK :]
    vt_ring[:, HALO + CHUNK :] = qkv[:, 2 * width :].T

    key_index = lax.broadcasted_iota(jnp.int32, (KWIN, QBLOCK), 0)
    query_index = lax.broadcasted_iota(jnp.int32, (KWIN, QBLOCK), 1)
    diagonal = key_index == query_index + HALO
    extras = []
    for blk in range(CHUNK // QBLOCK):
        line = mask[0, :, blk * QBLOCK : blk * QBLOCK + KWIN]
        column = jnp.broadcast_to(line, (QBLOCK, KWIN)).T
        extras.append(jnp.where(diagonal, 0.0, column))
    todo = [(blk, pair) for blk in range(CHUNK // QBLOCK) for pair in range(pairs)]
    cells = [(k * 128, h * 128) for k in range(KWIN // 128) for h in range(2)]
    tops = {}

    def score(blk, pair):
        low = blk * QBLOCK
        feat = slice(pair * 128, (pair + 1) * 128)
        split_q = split_heads(queries[low : low + QBLOCK, feat])
        best = [None, None]
        for k in range(0, KWIN, 128):
            s = dot_nt(k_ring[low + k : low + k + 128, feat], split_q)
            for h in range(2):
                lane = slice(h * 128, h * 128 + 128)
                v = s[:, lane] + bias[pair, k : k + 128, lane] + extras[blk][k : k + 128]
                s_scr[blk, pair, k : k + 128, lane] = v
                top = fold(v, jnp.max)
                best[h] = top if best[h] is None else jnp.maximum(best[h], top)
        tops[blk, pair] = [jnp.max(v, axis=0, keepdims=True) for v in best]

    def soften(blk, pair):
        for k, lane in cells:
            at = (blk, pair, slice(k, k + 128), slice(lane, lane + 128))
            p_out[at] = jnp.exp2(s_scr[at] - tops[blk, pair][lane // 128]).astype(BF16)

    ones = jnp.ones((16, KWIN), BF16)

    def attend(blk, pair):
        low = blk * QBLOCK
        feat = slice(pair * 128, (pair + 1) * 128)
        left = jnp.concatenate([vt_ring[feat, low : low + KWIN], ones], axis=0)
        sums = dot(left, p_out[blk, pair])
        inverse = 1.0 / sums[128:129]
        inverse_out[blk, pair : pair + 1, :] = inverse
        o_t = jnp.concatenate(
            [sums[:64, :128] * inverse[:, :128], sums[64:128, 128:] * inverse[:, 128:]], axis=0
        ).astype(BF16)
        o_out[feat, low : low + QBLOCK] = o_t
        o_ring[low : low + QBLOCK, feat] = o_t.T

    for i in range(len(todo) + 2):
        if i < len(todo):
            score(*todo[i])
            feed(i)
        if 1 <= i <= len(todo):
            soften(*todo[i - 1])
        if i >= 2:
            attend(*todo[i - 2])
    x_out[...] = (mid_out[...] + (dot(act_out[...], w2[...]) + b2[...])).astype(x_out.dtype)


def const_spec(shape):
    zeros = (0,) * len(shape)
    return pl.BlockSpec(shape, lambda g: zeros, pipeline_mode=pl.Buffered(1))


def layer_spec(shape, layer):
    if len(shape) == 2:
        return const_spec(shape)
    index = (layer,) + (0,) * (len(shape) - 1)
    return pl.BlockSpec((None,) + shape[1:], lambda g: index, pipeline_mode=pl.Buffered(1))


def first_forward_kernel(pairs, plan, chunks, own, part, shard, *refs):
    ins, outs, scratch = refs[:14], refs[14:22], refs[22:]
    x_all, send_sems, recv_sems, own_sems = scratch[-4:]
    step = pl.program_id(0)
    sems = Sems(send_sems, recv_sems, own_sems)
    lanes = []
    for i in range(own):
        lane = Lane(plan, sems)

        def copies(at, i=i):
            return [
                (cut(shard, src, part), cut(x_all, dst, part), at.along_b(by) if by else None)
                for src, dst, by in images_copies(shard, at, own, part, (i,))
            ]

        lane.add(copies)
        lanes.append(lane)
    for i in range(own):

        @pl.when(step == i * (chunks // own))
        def _(i=i):
            if i == 0:
                Places(plan).greet()
                for lane in lanes:
                    lane.part(0)
            lanes[i].part(1)

    def chunk(lead):
        at = jnp.clip(step - lead, 0, chunks - 1) * CHUNK
        return x_all.at[pl.ds(pl.multiple_of(at, CHUNK), CHUNK), :]

    x_copy = outs[-1]
    x_copy[...] = chunk(0)[...]
    forward_kernel(pairs, 0, chunk(0), chunk(2), *ins, *outs[:-1], *scratch[:-4])


def forward_layer(
    x, x_lead, chunks, chunks_per_image, tproj, mask, bias_rows, layer, weights, out_dtype, links, own, part, number
):
    width = x.shape[1]
    hidden = weights[7].shape[2]
    pairs = width // 128
    steps = chunks + 2
    first = layer == 0

    def at(lead, least=0):
        def index(g):
            return jnp.clip(g - lead, least, chunks - 1)

        return index

    new_at, attn_at, old_at = at(0), at(1), at(2)
    row = pl.BlockSpec((CHUNK, width), lambda g: (g, 0))
    rows = steps * CHUNK
    if first:
        x_specs, x_args = [pl.BlockSpec(memory_space=pl.ANY)], [x]
    else:
        x_specs = [
            pl.BlockSpec((CHUNK, width), lambda g: (new_at(g) + x_lead, 0)),
            pl.BlockSpec((CHUNK, width), lambda g: (old_at(g) + x_lead, 0)),
        ]
        x_args = [x, x]
    in_specs = x_specs + [
        pl.BlockSpec((1, 1, 3 * width), lambda g: (new_at(g) // chunks_per_image, 0, 0)),
        pl.BlockSpec((1, 1, CHUNK + 2 * HALO), lambda g: (attn_at(g), 0, 0)),
        layer_spec(bias_rows.shape, layer),
    ]
    in_specs += [layer_spec(w.shape, layer) for w in weights]
    out_specs = [
        pl.BlockSpec((CHUNK, 3 * width), lambda g: (new_at(g), 0)),
        pl.BlockSpec((CHUNK // QBLOCK, pairs, KWIN, 2 * QBLOCK), lambda g: (g, 0, 0, 0)),
        pl.BlockSpec((CHUNK // QBLOCK, 8, 2 * QBLOCK), lambda g: (g, 0, 0)),
        pl.BlockSpec((None, width, CHUNK), lambda g: (g + 1, 0, 0)),
        row,
        pl.BlockSpec((None, 2, CHUNK, hidden), lambda g: (g, 0, 0, 0)),
        row,
    ]
    out_shape = [
        jax.ShapeDtypeStruct((chunks * CHUNK, 3 * width), BF16),
        jax.ShapeDtypeStruct((steps * (CHUNK // QBLOCK), pairs, KWIN, 2 * QBLOCK), BF16),
        jax.ShapeDtypeStruct((steps * (CHUNK // QBLOCK), 8, 2 * QBLOCK), F32),
        jax.ShapeDtypeStruct((steps + 2, width, CHUNK), BF16),
        jax.ShapeDtypeStruct((rows, width), F32),
        jax.ShapeDtypeStruct((steps, 2, CHUNK, hidden), BF16),
        jax.ShapeDtypeStruct((rows, width), out_dtype),
    ]
    scratch = [
        pltpu.VMEM((pairs, KWIN, 2 * QBLOCK), F32),
        pltpu.VMEM((CHUNK, width), BF16),
        pltpu.VMEM((HALO + 2 * CHUNK, width), BF16),
        pltpu.VMEM((width, HALO + 2 * CHUNK), BF16),
        pltpu.VMEM((CHUNK, width), BF16),
        pltpu.VMEM((CHUNK // QBLOCK, pairs, KWIN, 2 * QBLOCK), F32),
    ]
    params = links.params(number)
    if first:
        plan = link_plan()
        remote = max((plan[1] - 1) * own, 1)
        kernel = functools.partial(first_forward_kernel, pairs, plan, chunks, own, part)
        out_specs.append(pl.BlockSpec((CHUNK, width), lambda g: (new_at(g), 0)))
        out_shape.append(jax.ShapeDtypeStruct((chunks * CHUNK, width), BF16))
        scratch += [
            pltpu.VMEM((chunks * CHUNK, width), BF16),
            pltpu.SemaphoreType.DMA((remote,)),
            pltpu.SemaphoreType.DMA((remote,)),
            pltpu.SemaphoreType.DMA((own,)),
        ]
        params = pltpu.CompilerParams(
            vmem_limit_bytes=VMEM_BYTES, collective_id=number, has_side_effects=True
        )
    else:
        kernel = links.host(
            functools.partial(forward_kernel, pairs, layer), len(in_specs), len(out_specs), len(scratch)
        )
    return pl.pallas_call(
        kernel,
        grid=(steps,),
        in_specs=in_specs + links.specs,
        out_specs=out_specs + links.specs,
        out_shape=out_shape + links.shapes,
        scratch_shapes=scratch + links.scratch,
        compiler_params=params,
        name="block_forward",
    )(*x_args, tproj, mask, bias_rows, *weights, *links.arrays)


def put_tiles(out, first, acc):
    width = acc.shape[0]
    for j in range(acc.shape[1] // 128):
        at = (first + j) * width
        out[at : at + width, :] = acc[:, j * 128 : (j + 1) * 128].astype(out.dtype)


def put_rows(out, at, vectors):
    lines = [v[:, j : j + 128] for v in vectors for j in range(0, v.shape[1], 128)]
    lines += [jnp.zeros((1, 128), F32)] * (-len(lines) % 16)
    out[at : at + len(lines), :] = jnp.concatenate(lines, axis=0).astype(out.dtype)


def feed_back_kernel(
    layer,
    gx,
    mid,
    acts,
    o,
    gain2,
    shift2,
    w1,
    w2,
    wo,
    gmid_out,
    go_out,
    grads_out,
    gw2t,
    gw1,
    gwo,
    sums,
    gb1,
    gu_scr,
):
    step = pl.program_id(0)
    gain2, shift2 = [ref.at[pl.ds(layer, 1), :] for ref in (gain2, shift2)]

    @pl.when(step == 0)
    def _():
        for ref in (gw2t, gw1, gwo, sums, gb1):
            ref[...] = jnp.zeros_like(ref)

    grad = gx[...].astype(F32)
    gr = grad.astype(BF16)
    gr_t = gr.T
    xh, inverse = norm_stats(mid[...])
    c_t = (xh * gain2[...] + shift2[...]).astype(BF16).T
    hidden = acts.shape[3]
    halves = acts.shape[0]
    tile = 256
    for low in range(0, hidden, tile):
        cols = slice(low, low + tile)
        ge = dot_nt(gr, w2[cols, :])
        slope = jnp.concatenate([acts[i, 1, :, cols] for i in range(halves)], axis=0)
        act = jnp.concatenate([acts[i, 0, :, cols] for i in range(halves)], axis=0)
        gu = (ge * slope.astype(F32)).astype(BF16)
        gu_scr[:, cols] = gu
        gb1[:, cols] += row_sums(gu.astype(F32))
        gw2t[:, cols] += dot(gr_t, act)
        gw1[:, cols] += dot(c_t, gu)
    gc = dot_nt(gu_scr[...], w1[...])
    gmid = grad + norm_back(gc, xh, inverse, gain2[...])
    gmid_out[...] = gmid
    gb = gmid.astype(BF16)
    gwo[...] += dot(jnp.concatenate([o[i] for i in range(o.shape[0])], axis=1), gb)
    go_t = dot_nt(wo[...], gb).astype(BF16)
    for i in range(o.shape[0]):
        go_out[i] = go_t[:, i * CHUNK : (i + 1) * CHUNK]
    sums[0] += row_sums(gr.astype(F32))
    sums[1] += row_sums(gb.astype(F32))
    sums[2] += row_sums(gc * xh)
    sums[3] += row_sums(gc)

    @pl.when(step == pl.num_programs(0) - 1)
    def _():
        tiles = hidden // 128
        put_tiles(grads_out, 0, gw2t)
        put_tiles(grads_out, tiles, gw1)
        put_tiles(grads_out, 2 * tiles, gwo)
        whole = [jnp.sum(sums[i], axis=0, keepdims=True) for i in range(4)]
        whole.append(jnp.sum(gb1[...], axis=0, keepdims=True))
        at = (2 * tiles + gwo.shape[1] // 128) * gwo.shape[0]
        put_rows(grads_out, at, whole)
        used = sum(feed_rows(gwo.shape[0], hidden))
        spare = grads_out.shape[0] - used
        if spare:
            grads_out[used:, :] = jnp.zeros((spare, 128), grads_out.dtype)


def feed_rows(width, hidden):
    tiles = (2 * hidden + width) // 128
    return tiles * width, -(-(4 * width + hidden) // 128 // 16) * 16


def feed_back(
    gx, gx_lead, patches, mid, acts, o, layer, gain2, shift2, w1, w2, wo, links, number
):
    width = mid.shape[1]
    hidden = acts.shape[3]

    def rows(cols, lead):
        return pl.BlockSpec((FEED, cols), lambda g: (g + lead, 0))

    grad_rows = padded_rows(sum(feed_rows(width, hidden)))
    return pl.pallas_call(
        links.host(functools.partial(feed_back_kernel, layer), 9, 3, 6),
        grid=(patches // FEED,),
        in_specs=[
            rows(width, gx_lead),
            rows(width, 1),
            pl.BlockSpec((FEED // CHUNK, 2, CHUNK, hidden), lambda g: (g + 1, 0, 0, 0)),
            pl.BlockSpec((FEED // CHUNK, width, CHUNK), lambda g: (g + 1, 0, 0)),
        ]
        + [layer_spec(w.shape, layer) for w in (gain2, shift2, w1, w2, wo)]
        + links.specs,
        out_specs=[
            rows(width, 0),
            pl.BlockSpec((FEED // CHUNK, width, CHUNK), lambda g: (g, 0, 0)),
            const_spec((grad_rows, 128)),
        ]
        + links.specs,
        out_shape=[
            jax.ShapeDtypeStruct((patches, width), F32),
            jax.ShapeDtypeStruct((patches // CHUNK, width, CHUNK), BF16),
            jax.ShapeDtypeStruct((grad_rows, 128), BF16),
        ]
        + links.shapes,
        scratch_shapes=[
            pltpu.VMEM((width, hidden), F32),
            pltpu.VMEM((width, hidden), F32),
            pltpu.VMEM((width, width), F32),
            pltpu.VMEM((4, 8, width), F32),
            pltpu.VMEM((8, hidden), F32),
            pltpu.VMEM((FEED, hidden), BF16),
        ]
        + links.scratch,
        compiler_params=links.params(number),
        name="feed_back",
    )(gx, mid, acts, o, gain2, shift2, w1, w2, wo, *links.arrays)


class Pusher:
    SLOTS = 8

    def __init__(self, plan, own, part, refs):
        self.plan, self.own, self.part = plan, own, part
        self.out, self.slots, self.send, self.recv, self.local = refs
        self.piece = min(part, CHUNK)
        self.subs = part // self.piece
        self.at = Places(plan)

    def each(self, chunk, act):
        at, bs = self.at, self.plan[1]
        whole = bs * self.part
        slot = chunk % self.SLOTS
        for k in range(CHUNK // self.piece):
            row = chunk * CHUNK + k * self.piece
            image, within = divmod(row, whole)
            target, sub = within // self.part, within % self.part // self.piece
            src = self.slots.at[slot, pl.ds(k * self.piece, self.piece), :]
            dst = self.out.at[at.b, image, pl.ds(sub * self.piece, self.piece), :]
            sem = slot * (CHUNK // self.piece) + k

            @pl.when(at.b == target)
            def _():
                act(pltpu.make_async_copy(src, dst, self.local.at[sem]), False)

            @pl.when(at.b != target)
            def _():
                by = mod(target - at.b + bs, bs)
                copy = pltpu.make_async_remote_copy(
                    src_ref=src,
                    dst_ref=dst,
                    send_sem=self.send.at[sem],
                    recv_sem=self.recv.at[((by - 1) * self.own + image) * self.subs + sub],
                    device_id=(at.img, target),
                    device_id_type=pl.DeviceIdType.MESH,
                )
                act(copy, True)

    def start(self, chunk):
        self.each(chunk, lambda copy, remote: copy.start())

    def sent(self, chunk):
        self.each(chunk, lambda copy, remote: copy.wait_send() if remote else copy.wait())

    def received(self):
        at, bs = self.at, self.plan[1]
        for by in range(1, bs):
            sender = mod(at.b - by + bs, bs)
            for image in range(self.own):
                for sub in range(self.subs):
                    pltpu.make_async_remote_copy(
                        src_ref=self.slots.at[0, pl.ds(0, self.piece), :],
                        dst_ref=self.out.at[sender, image, pl.ds(sub * self.piece, self.piece), :],
                        send_sem=self.send.at[0],
                        recv_sem=self.recv.at[((by - 1) * self.own + image) * self.subs + sub],
                        device_id=(at.img, sender),
                        device_id_type=pl.DeviceIdType.MESH,
                    ).wait_recv()


def last_attend_back_kernel(pairs, chunks, chunks_per_image, plan, own, part, *refs):
    ins, outs, scratch = refs[:12], refs[12:15], refs[15:]
    out, slots = outs[0], scratch[9]
    step = pl.program_id(0)
    pusher = Pusher(plan, own, part, (out, slots, *scratch[10:]))

    slot = slots.at[mod(step + Pusher.SLOTS - 1, Pusher.SLOTS)]
    attend_back_kernel(pairs, 0, chunks, chunks_per_image, *ins, slot, *outs[1:], *scratch[:9])
    acts = {}
    for chunk in range(chunks):

        def act(chunk=chunk):
            pusher.start(chunk)
            if 0 <= chunk + 1 - Pusher.SLOTS and chunk < chunks - 1:
                pusher.sent(chunk + 1 - Pusher.SLOTS)
            if chunk == chunks - 1:
                for old in range(max(chunks - Pusher.SLOTS, 0), chunks):
                    pusher.sent(old)
                pusher.received()

        acts[chunk + 1] = act
    return acts


def attend_back_kernel(
    pairs,
    layer,
    chunks,
    chunks_per_image,
    prev,
    cur,
    nxt,
    p_in,
    inverse_in,
    go_in,
    o_in,
    gmid,
    x,
    gain1,
    shift1,
    wqkv,
    gx_out,
    gtime,
    grads_out,
    gwqkv,
    gbias,
    sums,
    gq_ring,
    whole_ring,
    half_ring,
    next_ring,
    done,
    gs_scr,
):
    step = pl.program_id(0)
    width = x.shape[1]
    gain1, shift1 = [ref.at[pl.ds(layer, 1), :] for ref in (gain1, shift1)]

    @pl.when(step == 0)
    def _():
        for ref in (gwqkv, gbias, gtime, sums, gq_ring, whole_ring, half_ring, next_ring):
            ref[...] = jnp.zeros_like(ref)

    gq_old = gq_ring[...]
    live = (step < chunks).astype(F32)
    qkv = cur[...]
    queries = qkv[:, :width] * jnp.asarray(0.125, BF16)
    keys = jnp.concatenate(
        [prev[:, width : 2 * width], qkv[:, width : 2 * width], nxt[:, width : 2 * width]], axis=0
    )
    keys_t = keys.T
    values = jnp.concatenate([prev[:, 2 * width :], qkv[:, 2 * width :], nxt[:, 2 * width :]], axis=0)
    blocks = CHUNK // QBLOCK
    todo = [(blk, pair) for pair in range(pairs) for blk in range(blocks)]

    split_gos = {}

    def spread(blk, pair):
        low = blk * QBLOCK
        feat = slice(pair * 128, (pair + 1) * 128)
        inverse = inverse_in[blk, pair : pair + 1, :] * live
        go = go_in[feat, low : low + QBLOCK].astype(F32)
        go = [go[h * 64 : h * 64 + 64] * inverse[:, h * 128 : h * 128 + 128] for h in range(2)]
        o = o_in[feat, low : low + QBLOCK].astype(F32)
        row_dot = [
            jnp.sum(go[h] * o[h * 64 : h * 64 + 64], axis=0, keepdims=True) for h in range(2)
        ]
        split_go = split_heads(jnp.concatenate(go, axis=0).astype(BF16).T)
        split_gos[blk, pair] = split_go
        for k in range(0, KWIN, 128):
            gp = dot_nt(values[low + k : low + k + 128, feat], split_go)
            for h in range(2):
                lane = slice(h * 128, h * 128 + 128)
                gs = p_in[blk, pair, k : k + 128, lane].astype(F32) * (gp[:, lane] - row_dot[h])
                gbias[pair, k : k + 128, lane] += gs
                gs_scr[blk, pair, k : k + 128, lane] = gs.astype(BF16)

    late = []

    def pull(blk, pair):
        low = blk * QBLOCK
        feat = slice(pair * 128, (pair + 1) * 128)
        vfeat = slice(width + pair * 128, width + (pair + 1) * 128)
        gs = gs_scr[blk, pair]
        gk = dot(gs, split_heads(queries[low : low + QBLOCK, feat]))
        gv = dot(p_in[blk, pair], split_gos[blk, pair])
        gq = join_heads(dot(keys_t[feat, low : low + KWIN], gs)) * 0.125
        gq_ring[low : low + QBLOCK, feat] = gq.astype(BF16)
        late.append((gk, gv))
        if blk == blocks - 1:
            for cols, first, second in zip((feat, vfeat), late[-2], late[-1]):
                done[HALO:, cols] = (half_ring[:, cols] + first[:HALO]).astype(BF16)
                done[:HALO, cols] = whole_ring[:, cols]
                whole_ring[:, cols] = (
                    next_ring[:, cols] + first[HALO : 2 * HALO] + second[:HALO]
                ).astype(BF16)
                half_ring[:, cols] = first[2 * HALO :] + second[HALO : 2 * HALO]
                next_ring[:, cols] = second[2 * HALO :]

    for i in range(len(todo) + 1):
        if i < len(todo):
            spread(*todo[i])
        if i >= 1:
            pull(*todo[i - 1])

    done = jnp.concatenate([gq_old, done[...]], axis=1)
    xh, inverse = norm_stats(x[...].astype(F32))
    a = (xh * gain1[...] + shift1[...]).astype(BF16)
    gwqkv[...] += dot(a.T, done)
    ga = dot_nt(done, wqkv[...])
    gx_out[...] = (gmid[...] + norm_back(ga, xh, inverse, gain1[...])).astype(gx_out.dtype)
    sums[0] += row_sums(ga * xh)
    sums[1] += row_sums(ga)
    first = lax.rem(step + chunks_per_image - 1, chunks_per_image) == 0
    before = jnp.where(first, jnp.zeros(gtime.shape[1:], F32), gtime[0])
    summed = row_sums(done.astype(F32))
    gtime[0] = before + jnp.concatenate([summed[:, :width], summed[:, 2 * width :]], axis=1)

    @pl.when(step == chunks)
    def _():
        put_tiles(grads_out, 0, gwqkv)
        tiles = gwqkv.shape[1] // 128
        lines = attend_rows(width)[2]
        grads_out[tiles * width : tiles * width + lines, :] = gather_bias(gbias).astype(BF16)
        put_rows(
            grads_out,
            tiles * width + lines,
            [jnp.sum(sums[i], axis=0, keepdims=True) for i in range(2)],
        )
        used = attend_rows(width)[1]
        spare = grads_out.shape[0] - used
        if spare:
            grads_out[used:, :] = jnp.zeros((spare, 128), grads_out.dtype)


def attend_rows(width):
    lines = 2 * (width // 128) * (KWIN * 4 // QBLOCK) * 2
    small = -(-2 * width // 128 // 16) * 16
    return 3 * width // 128 * width, 3 * width // 128 * width + lines + small, lines


def attend_back(
    qkv,
    p,
    go,
    o,
    gmid,
    x,
    x_lead,
    chunks,
    chunks_per_image,
    layer,
    gain1,
    shift1,
    wqkv,
    own,
    part,
    links,
    number,
):
    width = x.shape[1]
    pairs = width // 128
    steps = chunks + 1
    halves = CHUNK // HALO

    def now(g):
        return jnp.minimum(g, chunks - 1)

    def late(g):
        return jnp.maximum(g - 1, 0)

    def rows(cols, lead, index):
        return pl.BlockSpec((CHUNK, cols), lambda g: (index(g) + lead, 0))

    images = chunks // chunks_per_image
    grad_rows = padded_rows(attend_rows(width)[1])
    in_specs = [
        pl.BlockSpec((HALO, 3 * width), lambda g: (jnp.maximum(halves * now(g) - 1, 0), 0)),
        rows(3 * width, 0, now),
        pl.BlockSpec(
            (HALO, 3 * width),
            lambda g: (jnp.minimum(halves * (now(g) + 1), halves * chunks - 1), 0),
        ),
        pl.BlockSpec((CHUNK // QBLOCK, pairs, KWIN, 2 * QBLOCK), lambda g: (now(g) + 1, 0, 0, 0)),
        pl.BlockSpec((CHUNK // QBLOCK, 8, 2 * QBLOCK), lambda g: (now(g) + 1, 0, 0)),
        pl.BlockSpec((None, width, CHUNK), lambda g: (now(g), 0, 0)),
        pl.BlockSpec((None, width, CHUNK), lambda g: (now(g) + 2, 0, 0)),
        rows(width, 0, late),
        rows(width, x_lead, late),
    ]
    in_specs += [layer_spec(w.shape, layer) for w in (gain1, shift1, wqkv)]
    out_specs = [
        rows(width, 1, lambda g: g),
        pl.BlockSpec((1, 8, 2 * width), lambda g: (late(g) // chunks_per_image, 0, 0)),
        const_spec((grad_rows, 128)),
    ]
    out_shape = [
        jax.ShapeDtypeStruct(((steps + 1) * CHUNK, width), F32),
        jax.ShapeDtypeStruct((images, 8, 2 * width), F32),
        jax.ShapeDtypeStruct((grad_rows, 128), BF16),
    ]
    scratch = [
        pltpu.VMEM((width, 3 * width), F32),
        pltpu.VMEM((pairs, KWIN, 2 * QBLOCK), F32),
        pltpu.VMEM((2, 8, width), F32),
        pltpu.VMEM((CHUNK, width), BF16),
        pltpu.VMEM((HALO, 2 * width), BF16),
        pltpu.VMEM((HALO, 2 * width), F32),
        pltpu.VMEM((HALO, 2 * width), F32),
        pltpu.VMEM((CHUNK, 2 * width), BF16),
        pltpu.VMEM((CHUNK // QBLOCK, pairs, KWIN, 2 * QBLOCK), BF16),
    ]
    kernel = functools.partial(attend_back_kernel, pairs, layer, chunks, chunks_per_image)
    if layer == 0:
        plan = link_plan()
        bs = plan[1]
        piece = min(part, CHUNK)
        pieces = CHUNK // piece
        kernel = functools.partial(
            last_attend_back_kernel, pairs, chunks, chunks_per_image, plan, own, part
        )
        out_specs[0] = pl.BlockSpec(memory_space=pl.ANY)
        out_shape[0] = jax.ShapeDtypeStruct((bs, own, part, width), BF16)
        scratch += [
            pltpu.VMEM((Pusher.SLOTS, CHUNK, width), BF16),
            pltpu.SemaphoreType.DMA((Pusher.SLOTS * pieces,)),
            pltpu.SemaphoreType.DMA((max((bs - 1) * own * (part // piece), 1),)),
            pltpu.SemaphoreType.DMA((Pusher.SLOTS * pieces,)),
        ]
    return pl.pallas_call(
        links.host(kernel, len(in_specs), len(out_specs), len(scratch)),
        grid=(steps,),
        in_specs=in_specs + links.specs,
        out_specs=out_specs + links.specs,
        out_shape=out_shape + links.shapes,
        scratch_shapes=scratch + links.scratch,
        compiler_params=links.params(number),
        name="attend_back",
    )(qkv, qkv, qkv, *p, go, o, gmid, x, gain1, shift1, wqkv, *links.arrays)


def final_kernel(plan, lanes_of_chunk, *refs):
    chunk, grad, extra = refs[:3]
    feed_out, attend_out, extra_out = refs[3:6]
    scratch = refs[6:]
    sems = Sems(*scratch[-3:])
    Places(plan).greet()
    parts = {}

    def planned(lane, whens):
        assert len(whens) == len(lane.steps) + 1
        for part, when in enumerate(whens):
            parts.setdefault(when, []).append((lane, part))

    lane = Lane(plan, sems)
    collect_lane(lane, scatter_lane(lane, grad, scratch[:-3]), attend_out)
    planned(lane, range(9))
    devices = 2 * plan[0] * plan[1] * plan[2]
    for low, rows in runs_of(feed_out.shape[0], lanes_of_chunk):
        lane = Lane(plan, sems)
        collect_lane(lane, chunk_ends(chunk, low, rows, devices), feed_out.at[pl.ds(low, rows), :])
        planned(lane, [0, 2, 4, 6, 8])
    lane = Lane(plan, sems)
    extra_lane(lane, extra, extra_out)
    planned(lane, [0, 1, 3, 5, 7])
    for when in sorted(parts):
        for lane, part in parts[when]:
            lane.part(part)


def final_exchange(chunk, lanes_of_chunk, grad, extra):
    plan = link_plan()
    xs, bs, zs = plan
    devices = 2 * xs * bs * zs
    anywhere = pl.BlockSpec(memory_space=pl.ANY)
    here = pl.BlockSpec(memory_space=pltpu.VMEM)
    return pl.pallas_call(
        functools.partial(final_kernel, plan, lanes_of_chunk),
        in_specs=[here, anywhere, here],
        out_specs=[anywhere] * 3,
        out_shape=[
            jax.ShapeDtypeStruct((chunk.shape[0] * devices, 128), BF16),
            jax.ShapeDtypeStruct(grad.shape, BF16),
            jax.ShapeDtypeStruct((devices * extra.shape[0], 128), BF16),
        ],
        scratch_shapes=held_shapes(plan, grad.shape[0]) + sems_shapes(plan, 3 + lanes_of_chunk),
        compiler_params=pltpu.CompilerParams(
            vmem_limit_bytes=VMEM_BYTES, collective_id=0, has_side_effects=True
        ),
        name="final_exchange",
    )(chunk, grad, extra)


def unpack_kernel(layers, lines, *refs):
    ins = [refs[6 * i : 6 * i + 6] for i in range(layers)]
    w2_out, w1_out, attend_out, wo_out = refs[6 * layers : 6 * layers + 4]
    small_outs = refs[6 * layers + 4 : 6 * layers + 11]
    rows_out = refs[6 * layers + 11]
    width = w1_out.shape[1]
    for layer, (w2t, w1, attend, wo, feed_small, attend_small) in enumerate(ins):
        for j in range(w1.shape[0] // width):
            rows = slice(j * width, (j + 1) * width)
            cols = slice(j * 128, (j + 1) * 128)
            w2_out[layer, cols, :] = w2t[rows, :].astype(F32).T
            w1_out[layer, :, cols] = w1[rows, :].astype(F32)
            attend_out[layer, :, cols] = attend[rows, :].astype(F32)
            wo_out[layer, :, cols] = wo[rows, :].astype(F32)
        feed = feed_small[...].astype(F32)
        tail = attend_small[...].astype(F32)
        rows_out[layer] = tail[:lines]
        at = 0
        for out in small_outs[:5]:
            for j in range(out.shape[1] // 128):
                out[layer : layer + 1, j * 128 : (j + 1) * 128] = feed[at : at + 1]
                at += 1
        at = lines
        for out in small_outs[5:]:
            for j in range(out.shape[1] // 128):
                out[layer : layer + 1, j * 128 : (j + 1) * 128] = tail[at : at + 1]
                at += 1


def unpack(fulls, width, hidden):
    layers = len(fulls)
    wide = width // 128
    steps = hidden // width
    rows = wide * width
    last = 3 * width // width - 1
    block = (rows, 128)
    feed_big, feed_small = feed_rows(width, hidden)
    attend_big, attend_all, lines = attend_rows(width)
    attend_small = attend_all - attend_big
    while attend_big % attend_small:
        attend_small += 16
    assert feed_big % feed_small == 0

    def spec(first, top):
        return pl.BlockSpec(block, lambda g: (first + jnp.minimum(g, top), 0))

    ins = [
        spec(0, steps),
        spec(steps, steps),
        spec(0, last),
        spec(2 * steps, 0),
        pl.BlockSpec((feed_small, 128), lambda g: (feed_big // feed_small, 0)),
        pl.BlockSpec((attend_small, 128), lambda g: (attend_big // attend_small, 0)),
    ]
    vectors = [width] * 4 + [hidden] + [width] * 2
    return pl.pallas_call(
        functools.partial(unpack_kernel, layers, lines),
        grid=(steps,),
        in_specs=ins * layers,
        out_specs=[
            pl.BlockSpec((layers, width, width), lambda g: (0, g, 0)),
            pl.BlockSpec((layers, width, width), lambda g: (0, 0, g)),
            pl.BlockSpec((layers, width, width), lambda g: (0, 0, jnp.minimum(g, last))),
            pl.BlockSpec((layers, width, width), lambda g: (0, 0, 0)),
        ]
        + [pl.BlockSpec((layers, n), lambda g: (0, 0)) for n in vectors]
        + [pl.BlockSpec((layers, lines, 128), lambda g: (0, 0, 0))],
        out_shape=[
            jax.ShapeDtypeStruct((layers, hidden, width), F32),
            jax.ShapeDtypeStruct((layers, width, hidden), F32),
            jax.ShapeDtypeStruct((layers, width, 3 * width), F32),
            jax.ShapeDtypeStruct((layers, width, width), F32),
        ]
        + [jax.ShapeDtypeStruct((layers, n), F32) for n in vectors]
        + [jax.ShapeDtypeStruct((layers, lines, 128), F32)],
        compiler_params=pltpu.CompilerParams(vmem_limit_bytes=VMEM_BYTES),
        name="unpack",
    )(
        *[
            ref
            for feed, attend in fulls
            for ref in (
                feed,
                feed,
                attend,
                feed,
                feed,
                attend,
            )
        ]
    )


def time_embedding(timesteps, width):
    half_width = width // 2
    frequency = jnp.exp(
        jnp.arange(half_width, dtype=jnp.int32).astype(F32) * (-math.log(10000.0) / half_width)
    )
    angles = timesteps.astype(F32)[:, None] * frequency[None, :]
    return jnp.concatenate([jnp.sin(angles), jnp.cos(angles)], axis=-1)


def bias_rows(table, index_table, grid_cols):
    heads, entries = table.shape
    span = 2 * WIN + 1
    offsets = 2 * grid_cols - 1
    turned = index_table.reshape(span, offsets)[:, ::-1].reshape(entries)
    select = (turned[None, :] == jnp.arange(entries, dtype=jnp.int32)[:, None]).astype(F32)
    rows = jnp.dot(table, select, precision=EXACT).reshape(heads, span, offsets)
    key_rows = KWIN // grid_cols
    a0, a1, a2, a3 = [
        jnp.pad(
            rows, ((0, 0), (q, key_rows - span - q), (0, 0)), constant_values=NEG_FILL
        )
        for q in range(QBLOCK // grid_cols)
    ]
    gap = jnp.full((heads, key_rows, 1), NEG_FILL, F32)
    even = jnp.concatenate(
        [a0[..., grid_cols - 1 :], gap, a2, gap, a0[..., : grid_cols - 1]], axis=-1
    )
    odd = jnp.concatenate([gap, a1, gap, a3], axis=-1)
    return jnp.stack([even, odd], axis=1)


def spaced(parts, steps):
    return [i * (steps - 1) // (parts - 1) for i in range(parts)]


def body(
    tokens,
    cotangent,
    valid_mask,
    timesteps,
    index_table,
    first_gain,
    first_shift,
    attend_weight,
    time_weight,
    offset_bias,
    output_weight,
    output_bias,
    second_gain,
    second_shift,
    expand_weight,
    expand_bias,
    reduce_weight,
    reduce_bias,
):
    images, band_rows, grid_cols, width = tokens.shape
    layers = attend_weight.shape[0]
    bands = lax.axis_size("band")
    me = lax.axis_index("band")
    own = images // bands
    part = band_rows * grid_cols
    patches = bands * part
    per_image = patches // CHUNK
    chunks = own * per_image

    mine = lax.dynamic_slice_in_dim(valid_mask, me * own, own, 0).reshape(own, patches)
    fill = jnp.where(mine == 1, 0.0, NEG_FILL).astype(F32)
    fill = jnp.pad(fill, ((0, 0), (HALO, HALO)), constant_values=NEG_FILL)
    mask = jnp.stack(
        [fill[:, c * CHUNK : (c + 1) * CHUNK + 2 * HALO] for c in range(per_image)], axis=1
    ).reshape(chunks, 1, CHUNK + 2 * HALO)

    time_low = time_embedding(
        lax.dynamic_slice_in_dim(timesteps, me * own, own, 0), width
    ).astype(BF16)
    heads, entries = offset_bias.shape[1:]

    def make_rows(table):
        return bias_rows(table, index_table, grid_cols)

    biases, bias_pull = jax.vjp(make_rows, offset_bias.reshape(layers * heads, entries))
    biases = biases.reshape(layers, -1, QBLOCK) * LOG2E

    tp = jnp.einsum("it,ltc->lic", time_low, time_weight, preferred_element_type=F32)
    tproj = jnp.concatenate([tp[..., :width], jnp.zeros_like(tp[..., :width]), tp[..., width:]], -1)
    weights = (
        first_gain,
        first_shift,
        attend_weight,
        output_weight,
        output_bias,
        second_gain,
        second_shift,
        expand_weight,
        expand_bias,
        reduce_weight,
        reduce_bias,
    )
    x, x_lead = tokens.reshape(images * part, width), 0
    kept = []
    for layer in range(layers):
        last = layer == layers - 1
        jobs = []
        if last:
            shard = cotangent.reshape(images * part, width)
            jobs = [("images", shard, (own, part), [0, chunks // 2, chunks + 2])]
        qkv, p, inverse, o, mid, acts, nxt, *more = forward_layer(
            x,
            x_lead,
            chunks,
            per_image,
            tproj[layer][:, None, :],
            mask,
            biases,
            layer,
            weights,
            BF16 if last else F32,
            Links(jobs),
            own,
            part,
            1 + layer,
        )
        if layer == 0:
            x = more[0]
        if last:
            gx = more[-1]
        kept.append((x, x_lead, qkv, (p, inverse), o, mid, acts))
        x, x_lead = nxt, 2

    gx_lead = 0
    devices = bands * lax.axis_size("img")
    hidden = expand_weight.shape[2]
    fulls = [[None, None] for _ in range(layers)]
    extra = [time_low]
    attend_grads = feed_part = None
    result = x
    for layer in reversed(range(layers)):
        x, x_lead, qkv, p, o, mid, acts = kept[layer]
        steps = own * patches // FEED
        if layer == layers - 1:
            jobs = [("bands", result, (2 * CHUNK, own, part), [0, steps // 2, steps])]
        else:
            jobs = [("sum", attend_grads, [spaced(9, steps)])]
        gmid, go, feed_grads, *sent = feed_back(
            gx,
            gx_lead,
            own * patches,
            mid,
            acts,
            o,
            layer,
            second_gain,
            second_shift,
            expand_weight,
            reduce_weight,
            output_weight,
            Links(jobs),
            1 + layers + 2 * layer,
        )
        if layer == layers - 1:
            output = sent[0].reshape(tokens.shape)
        else:
            fulls[layer + 1] = [feed_part, sent[0]]
        gx, gtime, attend_grads, feed_part = attend_back(
            qkv,
            p,
            go,
            o,
            gmid,
            x,
            x_lead,
            chunks,
            per_image,
            layer,
            first_gain,
            first_shift,
            attend_weight,
            own,
            part,
            Links(
                [
                    ("sum", feed_grads, [spaced(9, chunks - 1), spaced(9, chunks), [i + 1 for i in spaced(9, chunks)]])
                    if layer
                    else ("scatter", feed_grads, [spaced(6, chunks), [i + 1 for i in spaced(6, chunks)]])
                ]
            ),
            2 + layers + 2 * layer,
        )
        gx_lead = 1
        extra.append(jnp.sum(gtime, axis=1).astype(BF16))
    input_grad = gx.reshape(tokens.shape)

    extra = jnp.concatenate(extra, axis=1).reshape(-1, 128)
    lead = extra.shape[0]
    extra = jnp.pad(extra, ((0, -lead % 16), (0, 0)))
    *fulls[0], gathered = final_exchange(feed_part, 2, attend_grads, extra)
    gathered = gathered.reshape(devices, -1, 128)[:, :lead].reshape(devices * own, -1)
    grad_time = jnp.stack(
        [
            lax.dot_general(
                gathered[:, :width],
                gathered[:, width * (1 + 2 * turn) : width * (3 + 2 * turn)],
                (((0,), (0,)), ((), ())),
                preferred_element_type=F32,
            )
            for turn in reversed(range(layers))
        ]
    )
    (
        grad_reduce,
        grad_expand,
        grad_attend,
        grad_output,
        reduce_bias_grad,
        output_bias_grad,
        second_gain_grad,
        second_shift_grad,
        expand_bias_grad,
        first_gain_grad,
        first_shift_grad,
        grad_rows,
    ) = unpack(fulls, width, hidden)
    (grad_offset,) = bias_pull(grad_rows.reshape(layers * heads, 2, -1, QBLOCK))
    return (
        output,
        input_grad,
        first_gain_grad,
        first_shift_grad,
        grad_attend,
        grad_time,
        grad_offset.reshape(layers, heads, entries),
        grad_output,
        output_bias_grad,
        second_gain_grad,
        second_shift_grad,
        grad_expand,
        expand_bias_grad,
        grad_reduce,
        reduce_bias_grad,
    )


def solution(mesh):
    split = P("img", "band", None, None)
    placed = (split, split, P("img", None, None), P("img")) + (P(),) * 14
    return jax.shard_map(
        body,
        mesh=mesh,
        in_specs=placed,
        out_specs=(split, split) + (P(),) * 13,
        check_vma=False,
    )
```
